32 devices in a mesh: dp: 8 (over z, y), fsdp: 4 (over x, core).
Axes of the slice: x: 2, y: 2, z: 4, core: 2. Of those that a mesh axis runs over, the one named last changes fastest.
Arguments:
- tokens: bfloat16 [32768, 512], P(('dp', 'fsdp')), may hold values from -6 to 6
- cotangent: bfloat16 [32768, 512], P(('dp', 'fsdp')), may hold values from -6 to 6
- halves: int32 [32], P(('dp', 'fsdp')), may hold values 0 or 1
- qkv_weight: float32 [512, 1536], P(('dp', 'fsdp')), may hold values from -0.25 to 0.25
- qkv_mean: float32 [512, 1536], P(('dp', 'fsdp')), may hold values from -0.0029296875 to 0.0029296875
- qkv_square: float32 [512, 1536], P(('dp', 'fsdp')), may hold values from 2.7225047e-07 to 1.0890019e-06
- attnout_weight: float32 [512, 512], P(('dp', 'fsdp')), may hold values from -1 to 1
- attnout_mean: float32 [512, 512], P(('dp', 'fsdp')), may hold values from -0.0029296875 to 0.0029296875
- attnout_square: float32 [512, 512], P(('dp', 'fsdp')), may hold values from 2.7225047e-07 to 1.0890019e-06
- attngate_weight: float32 [512, 512], P(('dp', 'fsdp')), may hold values from -0.25 to 0.25
- attngate_mean: float32 [512, 512], P(('dp', 'fsdp')), may hold values from -0.0029296875 to 0.0029296875
- attngate_square: float32 [512, 512], P(('dp', 'fsdp')), may hold values from 2.7225047e-07 to 1.0890019e-06
- upward_weight: float32 [512, 2048], P(('dp', 'fsdp')), may hold values from -0.25 to 0.25
- upward_mean: float32 [512, 2048], P(('dp', 'fsdp')), may hold values from -0.0029296875 to 0.0029296875
- upward_square: float32 [512, 2048], P(('dp', 'fsdp')), may hold values from 2.7225047e-07 to 1.0890019e-06
- downward_weight: float32 [2048, 512], P(('dp', 'fsdp')), may hold values from -0.125 to 0.125
- downward_mean: float32 [2048, 512], P(('dp', 'fsdp')), may hold values from -0.0029296875 to 0.0029296875
- downward_square: float32 [2048, 512], P(('dp', 'fsdp')), may hold values from 2.7225047e-07 to 1.0890019e-06
- ffngate_weight: float32 [512, 512], P(('dp', 'fsdp')), may hold values from -0.25 to 0.25
- ffngate_mean: float32 [512, 512], P(('dp', 'fsdp')), may hold values from -0.0029296875 to 0.0029296875
- ffngate_square: float32 [512, 512], P(('dp', 'fsdp')), may hold values from 2.7225047e-07 to 1.0890019e-06
- norms_weight: float32 [512, 6], P(('dp', 'fsdp')), may hold values from -2.5 to 3
- norms_mean: float32 [512, 6], P(('dp', 'fsdp')), may hold values from -0.0029296875 to 0.0029296875
- norms_square: float32 [512, 6], P(('dp', 'fsdp')), may hold values from 2.7225047e-07 to 1.0890019e-06
Outputs:
- output: bfloat16 [32768, 512], P(('dp', 'fsdp'))
- input_grad: float32 [32768, 512], P(('dp', 'fsdp'))
- grad_norm: float32 [], replicated
- qkv_newweight: float32 [512, 1536], P(('dp', 'fsdp'))
- qkv_newmean: float32 [512, 1536], P(('dp', 'fsdp'))
- qkv_newsquare: float32 [512, 1536], P(('dp', 'fsdp'))
- attnout_newweight: float32 [512, 512], P(('dp', 'fsdp'))
- attnout_newmean: float32 [512, 512], P(('dp', 'fsdp'))
- attnout_newsquare: float32 [512, 512], P(('dp', 'fsdp'))
- attngate_newweight: float32 [512, 512], P(('dp', 'fsdp'))
- attngate_newmean: float32 [512, 512], P(('dp', 'fsdp'))
- attngate_newsquare: float32 [512, 512], P(('dp', 'fsdp'))
- upward_newweight: float32 [512, 2048], P(('dp', 'fsdp'))
- upward_newmean: float32 [512, 2048], P(('dp', 'fsdp'))
- upward_newsquare: float32 [512, 2048], P(('dp', 'fsdp'))
- downward_newweight: float32 [2048, 512], P(('dp', 'fsdp'))
- downward_newmean: float32 [2048, 512], P(('dp', 'fsdp'))
- downward_newsquare: float32 [2048, 512], P(('dp', 'fsdp'))
- ffngate_newweight: float32 [512, 512], P(('dp', 'fsdp'))
- ffngate_newmean: float32 [512, 512], P(('dp', 'fsdp'))
- ffngate_newsquare: float32 [512, 512], P(('dp', 'fsdp'))
- norms_newweight: float32 [512, 6], P(('dp', 'fsdp'))
- norms_newmean: float32 [512, 6], P(('dp', 'fsdp'))
- norms_newsquare: float32 [512, 6], P(('dp', 'fsdp'))
The draws below stay inside these ranges and needn't reach their ends.
Inputs may be any that keep to these rules, and one draw needn't show every extreme that they name: `halves`: 1 where a device's 1024 tokens are two sequences of 512 tokens, 0 where they are one sequence.
All inputs are finite; a program needn't handle non-finite values.
Results may differ from the reference program's by a relative error of at most 0.017.
The reference program's roundings to bfloat16 on the way count: a program that leaves them out, or rounds other values in their place, can miss the bound.
Values may be sent and summed in bfloat16 or wider, within the bound.
No kernel may reach another device: no remote copies, remote signals or barrier semaphores. Data moves between devices by JAX's collectives and lax.ppermute only.
A program may use at most 256 MiB of HBM per device.

```python
import math
import jax
import jax.numpy as jnp
from jax import lax

D = 512
H = 8
HD = 64
FF = 2048
TOK_DEV = 1024
STEP = 5
TOKENS = 32768
N_DP = 8
N_FSDP = 4


def draw_norms_weight(key, part):
    key = jax.random.fold_in(key, 7)
    keys = jax.random.split(key, 3)
    place = jnp.arange(D, dtype=jnp.float32) / (D - 1)
    rise = 0.6 + 1.2 * place
    jitter = jnp.exp(jax.random.uniform(keys[0], (D, 2), jnp.float32, -0.22, 0.22))
    shifts = jnp.clip(0.3 * jax.random.normal(keys[1], (D, 2), jnp.float32), -1.0, 1.0)
    biases = jnp.clip(0.7 * jax.random.normal(keys[2], (D, 2), jnp.float32), -2.5, 2.5)
    gains = rise[:, None] * jitter
    return jnp.stack([gains[:, 0], shifts[:, 0], biases[:, 0], gains[:, 1], shifts[:, 1], biases[:, 1]], axis=1)


def touch_ends(entries, own_key, least, high):
    index_at = [jax.random.randint(jax.random.fold_in(own_key, axis), (), 0, length) for axis, length in enumerate(entries.shape)]
    widest = entries.shape.index(max(entries.shape))
    neighbour = index_at[:widest] + [(index_at[widest] + 1) % entries.shape[widest]] + index_at[widest + 1:]
    return entries.at[tuple(index_at)].set(least).at[tuple(neighbour)].set(high)


def levels(own_key, extent, cuts, smallest, largest):
    def one(dim, parts):
        draws = jax.random.uniform(jax.random.fold_in(jax.random.fold_in(own_key, 6), dim), (parts,), jnp.float32, smallest / len(cuts), largest / len(cuts))
        return jnp.repeat(jnp.exp(draws), extent[dim] // parts).reshape((-1,) + (1,) * (len(extent) - dim - 1))

    loudness = one(*cuts[0])
    for cut in cuts[1:]:
        loudness = loudness * one(*cut)
    return loudness


def scatter_about(own_key, extent, width, reach, pieces=(), held_as=jnp.bfloat16):
    level = levels(own_key, extent, pieces, -0.22, 0.18) if pieces else 1.0
    result = jax.random.normal(own_key, extent, jnp.float32) * width * level
    return jnp.minimum(jnp.maximum(result, -reach), reach).astype(held_as)


def setup_inputs(seed: int = 0) -> dict:
    streams_of = jax.random.split(jax.random.key(seed), 25)
    tokens = scatter_about(streams_of[0], (TOKENS, D), 1.0, 6.0, ((0, 32),))
    cotangent = scatter_about(streams_of[1], (TOKENS, D), 1.0, 6.0, ((0, 32),))
    halves = touch_ends((jax.random.randint(streams_of[2], (N_DP * N_FSDP,), 0, 2) < 1).astype(jnp.int32), jax.random.fold_in(streams_of[2], 1), 0, 1)
    qkv_weight = scatter_about(streams_of[3], (D, 3 * D), D ** -0.5, 0.25, ((0, 32),), jnp.float32)
    qkv_mean = scatter_about(streams_of[4], (D, 3 * D), (1.0 / (6 * D * D + 2 * D * FF + 6 * D) ** 0.5), 0.0029296875, ((0, 32),), jnp.float32)
    qkv_square = jnp.clip(jnp.exp(math.log(1.0890018984355265e-06) - 1.3862944 * jax.random.uniform(streams_of[5], (D, 3 * D), jnp.float32) ** levels(streams_of[5], (D, 3 * D), ((0, 32),), -0.2, 0.2)), 2.7225047460888163e-07, 1.0890018984355265e-06)
    attnout_weight = scatter_about(streams_of[6], (D, D), (D // 16) ** -0.5, 1.0, ((0, 32),), jnp.float32)
    attnout_mean = scatter_about(streams_of[7], (D, D), (1.0 / (6 * D * D + 2 * D * FF + 6 * D) ** 0.5), 0.0029296875, ((0, 32),), jnp.float32)
    attnout_square = jnp.clip(jnp.exp(math.log(1.0890018984355265e-06) - 1.3862944 * jax.random.uniform(streams_of[8], (D, D), jnp.float32) ** levels(streams_of[8], (D, D), ((0, 32),), -0.2, 0.2)), 2.7225047460888163e-07, 1.0890018984355265e-06)
    attngate_weight = scatter_about(streams_of[9], (D, D), D ** -0.5, 0.25, ((0, 32),), jnp.float32)
    attngate_mean = scatter_about(streams_of[10], (D, D), (1.0 / (6 * D * D + 2 * D * FF + 6 * D) ** 0.5), 0.0029296875, ((0, 32),), jnp.float32)
    attngate_square = jnp.clip(jnp.exp(math.log(1.0890018984355265e-06) - 1.3862944 * jax.random.uniform(streams_of[11], (D, D), jnp.float32) ** levels(streams_of[11], (D, D), ((0, 32),), -0.2, 0.2)), 2.7225047460888163e-07, 1.0890018984355265e-06)
    upward_weight = scatter_about(streams_of[12], (D, FF), D ** -0.5, 0.25, ((0, 32),), jnp.float32)
    upward_mean = scatter_about(streams_of[13], (D, FF), (1.0 / (6 * D * D + 2 * D * FF + 6 * D) ** 0.5), 0.0029296875, ((0, 32),), jnp.float32)
    upward_square = jnp.clip(jnp.exp(math.log(1.0890018984355265e-06) - 1.3862944 * jax.random.uniform(streams_of[14], (D, FF), jnp.float32) ** levels(streams_of[14], (D, FF), ((0, 32),), -0.2, 0.2)), 2.7225047460888163e-07, 1.0890018984355265e-06)
    downward_weight = scatter_about(streams_of[15], (FF, D), FF ** -0.5, 0.125, ((0, 32),), jnp.float32)
    downward_mean = scatter_about(streams_of[16], (FF, D), (1.0 / (6 * D * D + 2 * D * FF + 6 * D) ** 0.5), 0.0029296875, ((0, 32),), jnp.float32)
    downward_square = jnp.clip(jnp.exp(math.log(1.0890018984355265e-06) - 1.3862944 * jax.random.uniform(streams_of[17], (FF, D), jnp.float32) ** levels(streams_of[17], (FF, D), ((0, 32),), -0.2, 0.2)), 2.7225047460888163e-07, 1.0890018984355265e-06)
    ffngate_weight = scatter_about(streams_of[18], (D, D), D ** -0.5, 0.25, ((0, 32),), jnp.float32)
    ffngate_mean = scatter_about(streams_of[19], (D, D), (1.0 / (6 * D * D + 2 * D * FF + 6 * D) ** 0.5), 0.0029296875, ((0, 32),), jnp.float32)
    ffngate_square = jnp.clip(jnp.exp(math.log(1.0890018984355265e-06) - 1.3862944 * jax.random.uniform(streams_of[20], (D, D), jnp.float32) ** levels(streams_of[20], (D, D), ((0, 32),), -0.2, 0.2)), 2.7225047460888163e-07, 1.0890018984355265e-06)
    norms_weight = draw_norms_weight(jax.random.fold_in(streams_of[24], 71), 0)
    norms_mean = scatter_about(streams_of[22], (D, 6), (1.0 / (6 * D * D + 2 * D * FF + 6 * D) ** 0.5), 0.0029296875, ((0, 32),), jnp.float32)
    norms_square = jnp.clip(jnp.exp(math.log(1.0890018984355265e-06) - 1.3862944 * jax.random.uniform(streams_of[23], (D, 6), jnp.float32) ** levels(streams_of[23], (D, 6), ((0, 32),), -0.2, 0.2)), 2.7225047460888163e-07, 1.0890018984355265e-06)
    return {"tokens": tokens, "cotangent": cotangent, "halves": halves, "qkv_weight": qkv_weight, "qkv_mean": qkv_mean, "qkv_square": qkv_square, "attnout_weight": attnout_weight, "attnout_mean": attnout_mean, "attnout_square": attnout_square, "attngate_weight": attngate_weight, "attngate_mean": attngate_mean, "attngate_square": attngate_square, "upward_weight": upward_weight, "upward_mean": upward_mean, "upward_square": upward_square, "downward_weight": downward_weight, "downward_mean": downward_mean, "downward_square": downward_square, "ffngate_weight": ffngate_weight, "ffngate_mean": ffngate_mean, "ffngate_square": ffngate_square, "norms_weight": norms_weight, "norms_mean": norms_mean, "norms_square": norms_square}


@jax.custom_vjp
def low(v):
    return lax.optimization_barrier(v.astype(jnp.bfloat16)).astype(jnp.float32)

@jax.custom_vjp
def low_back(v):
    return v

def low_keep(v):
    return (low(v), None)

def low_pass(kept, grad):
    return (grad,)

def back_keep(v):
    return (v, None)

def back_low(kept, grad):
    return (low(grad),)
low.defvjp(low_keep, low_pass)
low_back.defvjp(back_keep, back_low)
BEST = lax.Precision.HIGHEST

def layer_norm(values, gain, shift):
    center = values - lax.optimization_barrier(jnp.mean(values, axis=-1, keepdims=True))
    scale = lax.rsqrt(lax.optimization_barrier(jnp.mean(center * center, axis=-1, keepdims=True)) + 1e-05)
    return center * scale * gain + shift

def block(weights, item):
    w_joint, w_attn, w_agate, w_upper, w_lower, w_fgate, vectors = weights
    xfull, segment = item
    length = xfull.shape[0]
    first = low(layer_norm(xfull, vectors[:, 0], vectors[:, 1]))
    joint = low_back(low(jnp.dot(first, w_joint, precision=BEST)))
    heads = joint.reshape(length, 3, H, HD).transpose(1, 2, 0, 3)
    raw = low_back(jnp.einsum('hqd,hkd->hqk', heads[0], heads[1], precision=BEST) * 0.125)
    places = jnp.arange(length)
    allowed = (places[None, :] <= places[:, None]) & (segment[:, None] == segment[None, :])
    probs = low(jax.nn.softmax(jnp.where(allowed[None], raw, -1e+30), axis=-1))
    mixed = low_back(low(jnp.einsum('hqk,hkd->hqd', probs, heads[2], precision=BEST)))
    merged = mixed.transpose(1, 0, 2).reshape(length, D)
    attend = low_back(jnp.dot(merged, w_attn, precision=BEST))
    gate_one = jax.nn.sigmoid(low_back(jnp.dot(first, w_agate, precision=BEST) + vectors[:, 2]))
    middle = gate_one * attend + (1.0 - gate_one) * xfull
    second = low(layer_norm(middle, vectors[:, 3], vectors[:, 4]))
    upper = low_back(jnp.dot(second, w_upper, precision=BEST))
    hidden = low(jax.nn.gelu(upper))
    branch = low_back(jnp.dot(hidden, w_lower, precision=BEST))
    gate_two = jax.nn.sigmoid(low_back(jnp.dot(second, w_fgate, precision=BEST) + vectors[:, 5]))
    return gate_two * branch + (1.0 - gate_two) * middle

def adamw(master, moment, square, grad, clip, rate):
    clipped = grad * clip
    new_moment = 0.5 * moment + 0.5 * clipped
    new_square = 0.5 * square + 0.5 * clipped * clipped
    fix = 1.0 - 0.5 ** STEP
    stepped = new_moment / fix / (jnp.sqrt(new_square / fix) + 1e-08)
    return (master - rate * (stepped + 0.01 * master), new_moment, new_square)

def reference(tokens, cotangent, halves, qkv_weight, qkv_mean, qkv_square, attnout_weight, attnout_mean, attnout_square, attngate_weight, attngate_mean, attngate_square, upward_weight, upward_mean, upward_square, downward_weight, downward_mean, downward_square, ffngate_weight, ffngate_mean, ffngate_square, norms_weight, norms_mean, norms_square):
    count = N_DP * N_FSDP
    masters = (qkv_weight, attnout_weight, attngate_weight, upward_weight, downward_weight, ffngate_weight, norms_weight)
    moments = (qkv_mean, attnout_mean, attngate_mean, upward_mean, downward_mean, ffngate_mean, norms_mean)
    squares = (qkv_square, attnout_square, attngate_square, upward_square, downward_square, ffngate_square, norms_square)
    inputs = tokens.astype(jnp.float32).reshape(count, TOK_DEV, D)
    places = jnp.arange(TOK_DEV)
    segments = (places[None, :] >= TOK_DEV // 2).astype(jnp.int32) * halves[:, None]

    def whole(params, values):
        weights = tuple((low(item) for item in params))
        step_fn = jax.checkpoint(lambda item: block(weights, item))
        return lax.map(step_fn, (values, segments))
    outputs, pull = jax.vjp(whole, masters, inputs)
    grads, dinput = pull(cotangent.astype(jnp.float32).reshape(count, TOK_DEV, D))
    total = jnp.float32(0.0)
    for grad in grads:
        total = total + jnp.sum(grad * grad)
    norm = jnp.sqrt(total)
    clip = jnp.minimum(1.0, 1.0 / (norm + 1e-06))
    rates = (D ** (-0.5), (D // 16) ** (-0.5), D ** (-0.5), D ** (-0.5), FF ** (-0.5), D ** (-0.5), 0.5)
    results = [outputs.reshape(TOKENS, D).astype(jnp.bfloat16), dinput.reshape(TOKENS, D), norm]
    for index in range(7):
        results.extend(adamw(masters[index], moments[index], squares[index], grads[index], clip, rates[index]))
    return tuple(results)
```

```python
import functools
import jax
import jax.numpy as jnp
from jax import lax
from jax.experimental import pallas as pl
from jax.experimental.pallas import tpu as pltpu
from jax.sharding import PartitionSpec as P

D = 512
H = 8
HD = 64
FF = 2048
STEP = 5
PAIRS = H // 2
SUB = 16
OWNERS = D // SUB
F32 = jnp.float32
BF16 = jnp.bfloat16
MIB = 1024 * 1024


def params(mib):
    return pltpu.CompilerParams(vmem_limit_bytes=mib * MIB)


def dot(a, b):
    return lax.dot_general(a, b, (((1,), (0,)), ((), ())), preferred_element_type=F32)


def dot_nt(a, b):
    return lax.dot_general(a, b, (((1,), (1,)), ((), ())), preferred_element_type=F32)


def dot_tn(a, b):
    return lax.dot_general(a, b, (((0,), (0,)), ((), ())), preferred_element_type=F32)


def weight(ref, j):
    part = ref[:, :, SUB * j : SUB * (j + 1), :]
    return part.swapaxes(0, 1).reshape(D, D)


def put(ref, j, value):
    nf, nd = ref.shape[0], ref.shape[1]
    ref[:, :, SUB * j : SUB * (j + 1), :] = (
        value.astype(ref.dtype).reshape(nd, nf, SUB, D).swapaxes(0, 1)
    )


def normed(values):
    center = values - jnp.mean(values, axis=-1, keepdims=True)
    scale = lax.rsqrt(jnp.mean(center * center, axis=-1, keepdims=True) + 1e-05)
    return center * scale, scale


def norm_back(grad, unit, scale, gain):
    inner = grad * gain
    first = jnp.mean(inner, axis=-1, keepdims=True)
    second = jnp.mean(inner * unit, axis=-1, keepdims=True)
    return scale * (inner - first - unit * second)


def project_kernel(x_ref, g_ref, a_ref, qkv_ref, vec_ref):
    @pl.when(pl.program_id(0) == 0)
    def _():
        nf, nd = g_ref.shape[0], g_ref.shape[1]
        cols = g_ref[:, :, 3 * SUB : 4 * SUB, 0:128].swapaxes(0, 1).reshape(D, 128)
        vec_ref[...] = cols.astype(F32).T[0:8, :]

    unit, _ = normed(x_ref[...].astype(F32))
    a1 = (unit * vec_ref[0:1, :] + vec_ref[1:2, :]).astype(BF16)
    a_ref[...] = a1
    for j in range(3):
        qkv_ref[:, j * D : (j + 1) * D] = dot(a1, weight(g_ref, j)).astype(BF16)


def project(x, g1, rows=256):
    t = x.shape[0]
    return pl.pallas_call(
        project_kernel,
        grid=(t // rows,),
        in_specs=[
            pl.BlockSpec((rows, D), lambda i: (i, 0)),
            pl.BlockSpec(g1.shape, lambda i: (0, 0, 0, 0)),
        ],
        out_specs=[
            pl.BlockSpec((rows, D), lambda i: (i, 0)),
            pl.BlockSpec((rows, 3 * D), lambda i: (i, 0)),
            pl.BlockSpec((8, D), lambda i: (0, 0)),
        ],
        out_shape=[
            jax.ShapeDtypeStruct((t, D), BF16),
            jax.ShapeDtypeStruct((t, 3 * D), BF16),
            jax.ShapeDtypeStruct((8, D), F32),
        ],
        compiler_params=params(32),
        cost_estimate=pl.CostEstimate(flops=2 * t * D * 3 * D, bytes_accessed=8 * MIB, transcendentals=0),
        name="project",
    )(x, g1)


BLK = 256


def lane_half(shape, head):
    lane = lax.broadcasted_iota(jnp.int32, shape, 1)
    return (lane >= HD) if head else (lane < HD)


def key_range(i, two, length):
    per = length // BLK
    if two and i >= per // 2:
        return per // 2
    return 0


def diagonal():
    row = lax.broadcasted_iota(jnp.int32, (BLK, BLK), 0)
    col = lax.broadcasted_iota(jnp.int32, (BLK, BLK), 1)
    return row <= col


def attend_kernel(halves_ref, q_ref, k_ref, v_ref, o_ref, lse_ref, vt_ref):
    length = q_ref.shape[0]
    vt_ref[...] = v_ref[...].T
    allowed = diagonal()

    def block(i, first):
        rows = slice(i * BLK, (i + 1) * BLK)
        qs = q_ref[rows, :] * jnp.bfloat16(0.125)
        outs = []
        for head in range(2):
            qh = jnp.where(lane_half(qs.shape, head), qs, jnp.bfloat16(0))
            st = dot_nt(k_ref[first * BLK : (i + 1) * BLK, :], qh)
            n = i - first
            last = jnp.where(allowed, st[n * BLK :, :], -1e30)
            top = jnp.max(last, axis=0, keepdims=True)
            if n:
                top = jnp.maximum(top, jnp.max(st[: n * BLK, :], axis=0, keepdims=True))
            elast = jnp.exp(last - top)
            total = jnp.sum(elast, axis=0, keepdims=True)
            if n:
                erest = jnp.exp(st[: n * BLK, :] - top)
                total = total + jnp.sum(erest, axis=0, keepdims=True)
                expo = jnp.concatenate([erest, elast], axis=0)
            else:
                expo = elast
            vt = vt_ref[head * HD : (head + 1) * HD, first * BLK : (i + 1) * BLK]
            ot = dot(vt, expo.astype(BF16))
            outs.append(ot * (1.0 / total))
            lse_ref[0, head : head + 1, rows] = top + jnp.log(total)
        o_ref[rows, :] = jnp.concatenate(outs, axis=0).T.astype(BF16)

    per = length // BLK
    for i in range(per // 2):
        block(i, 0)

    @pl.when(halves_ref[0] == 0)
    def _():
        for i in range(per // 2, per):
            block(i, 0)

    @pl.when(halves_ref[0] != 0)
    def _():
        for i in range(per // 2, per):
            block(i, per // 2)


def attend(halves, qkv):
    t = qkv.shape[0]
    return pl.pallas_call(
        attend_kernel,
        grid=(PAIRS,),
        in_specs=[
            pl.BlockSpec(memory_space=pltpu.SMEM),
            pl.BlockSpec((t, 128), lambda p: (0, p)),
            pl.BlockSpec((t, 128), lambda p: (0, PAIRS + p)),
            pl.BlockSpec((t, 128), lambda p: (0, 2 * PAIRS + p)),
        ],
        out_specs=[
            pl.BlockSpec((t, 128), lambda p: (0, p)),
            pl.BlockSpec((1, 2, t), lambda p: (p, 0, 0)),
        ],
        out_shape=[
            jax.ShapeDtypeStruct((t, D), BF16),
            jax.ShapeDtypeStruct((PAIRS, 2, t), F32),
        ],
        scratch_shapes=[pltpu.VMEM((128, t), BF16)],
        compiler_params=params(32),
        cost_estimate=pl.CostEstimate(flops=4 * t * t * D, bytes_accessed=8 * MIB, transcendentals=t * t * H),
        name="attend",
    )(halves, qkv, qkv, qkv)


def attend_back_kernel(halves_ref, q_ref, k_ref, v_ref, o_ref, do_ref, lse_ref, dq_ref, dk_ref, dv_ref, kt_ref, qt_ref, dot_ref, dkt_ref, dvt_ref):
    length = q_ref.shape[0]
    kt_ref[...] = k_ref[...].T
    qt_ref[...] = q_ref[...].T
    dot_ref[...] = do_ref[...].T
    prod = (do_ref[...].astype(F32) * o_ref[...].astype(F32)).T
    delta = [jnp.sum(prod[head * HD : (head + 1) * HD, :], axis=0, keepdims=True) for head in range(2)]
    dkt_ref[...] = jnp.zeros_like(dkt_ref)
    dvt_ref[...] = jnp.zeros_like(dvt_ref)
    allowed = diagonal()

    def block(i, first):
        rows = slice(i * BLK, (i + 1) * BLK)
        keys = slice(first * BLK, (i + 1) * BLK)
        qs = q_ref[rows, :] * jnp.bfloat16(0.125)
        dob = do_ref[rows, :]
        outs = []
        n = i - first
        for head in range(2):
            half = lane_half(qs.shape, head)
            own = slice(head * HD, (head + 1) * HD)
            qh = jnp.where(half, qs, jnp.bfloat16(0))
            dh = jnp.where(half, dob, jnp.bfloat16(0))
            lse = lse_ref[0, head : head + 1, rows]
            st = dot_nt(k_ref[keys, :], qh)
            dpt = dot_nt(v_ref[keys, :], dh)
            last = jnp.where(allowed, jnp.exp(st[n * BLK :, :] - lse), 0.0)
            if n:
                pt = jnp.concatenate([jnp.exp(st[: n * BLK, :] - lse), last], axis=0)
            else:
                pt = last
            dst = (pt * (dpt - delta[head][:, rows])).astype(BF16)
            pb = pt.astype(BF16)
            dvt_ref[own, keys] += dot_nt(dot_ref[own, rows], pb)
            dkt_ref[own, keys] += dot_nt(qt_ref[own, rows], dst)
            outs.append(dot(kt_ref[own, keys], dst) * 0.125)
        dq_ref[rows, :] = jnp.concatenate(outs, axis=0).T.astype(BF16)

    per = length // BLK
    for i in range(per // 2):
        block(i, 0)

    @pl.when(halves_ref[0] == 0)
    def _():
        for i in range(per // 2, per):
            block(i, 0)

    @pl.when(halves_ref[0] != 0)
    def _():
        for i in range(per // 2, per):
            block(i, per // 2)

    dk_ref[...] = (dkt_ref[...] * 0.125).T.astype(BF16)
    dv_ref[...] = dvt_ref[...].T.astype(BF16)


def attend_back(halves, qkv, o, do, lse, first=0, count=PAIRS):
    t = qkv.shape[0]
    col = pl.BlockSpec((t, 128), lambda p: (0, first + p))
    out = pl.BlockSpec((t, 128), lambda p: (0, p))
    return pl.pallas_call(
        attend_back_kernel,
        grid=(count,),
        in_specs=[
            pl.BlockSpec(memory_space=pltpu.SMEM),
            col,
            pl.BlockSpec((t, 128), lambda p: (0, PAIRS + first + p)),
            pl.BlockSpec((t, 128), lambda p: (0, 2 * PAIRS + first + p)),
            col,
            col,
            pl.BlockSpec((1, 2, t), lambda p: (first + p, 0, 0)),
        ],
        out_specs=[out, out, out],
        out_shape=[jax.ShapeDtypeStruct((t, 128 * count), BF16)] * 3,
        scratch_shapes=[pltpu.VMEM((128, t), BF16)] * 3 + [pltpu.VMEM((128, t), F32)] * 2,
        compiler_params=params(48),
        cost_estimate=pl.CostEstimate(flops=10 * t * t * 128 * count, bytes_accessed=8 * MIB, transcendentals=t * t * 2 * count),
        name="attend_back",
    )(halves, qkv, qkv, qkv, o, do, lse)


def middle_kernel(
    x_ref, a1_ref, o_ref, dy_ref, vec_ref, g_ref,
    y_ref, dh1_ref, a2_ref, e_ref, df_ref, du_ref, dz2_ref, dz1_ref, datt_ref, do_ref, dvec_ref,
):
    @pl.when(pl.program_id(0) == 0)
    def _():
        dvec_ref[...] = jnp.zeros_like(dvec_ref)

    c1, g2, b2, c2 = (vec_ref[k : k + 1, :] for k in (2, 3, 4, 5))
    x = x_ref[...].astype(F32)
    w_attn, w_gate1, w_gate2 = weight(g_ref, 0), weight(g_ref, 1), weight(g_ref, 2)
    att = dot(o_ref[...], w_attn)
    t1 = jax.nn.sigmoid(dot(a1_ref[...], w_gate1) + c1)
    h1 = t1 * att + (1.0 - t1) * x
    unit, scale = normed(h1)
    a2 = (unit * g2 + b2).astype(BF16)
    a2_ref[...] = a2
    t2 = jax.nn.sigmoid(dot(a2, w_gate2) + c2)
    nf, nd = g_ref.shape[0], g_ref.shape[1]
    f = None
    slopes = []
    kc = 0.7978845608028654
    for j in range(FF // D):
        u = dot(a2, weight(g_ref, 3 + j))
        sq = u * u
        half = 0.5 * jnp.tanh(u * (kc + (kc * 0.044715) * sq)) + 0.5
        gel = u * half
        e = gel.astype(BF16)
        slopes.append(half + gel * (1.0 - half) * (2.0 * kc + (6.0 * kc * 0.044715) * sq))
        e_ref[:, j * D : (j + 1) * D] = e
        part = dot(e, lower(g_ref, j))
        f = part if f is None else f + part
    y = t2 * f + (1.0 - t2) * h1
    y_ref[...] = y.astype(BF16)
    dy = dy_ref[...].astype(F32)
    dz2 = (dy * (f - h1) * t2 * (1.0 - t2)).astype(BF16)
    df = (dy * t2).astype(BF16)
    dz2_ref[...] = dz2
    df_ref[...] = df
    da2 = dot_nt(dz2, w_gate2)
    for j in range(FF // D):
        du = (dot_nt(df, lower(g_ref, j)) * slopes[j]).astype(BF16)
        du_ref[:, j * D : (j + 1) * D] = du
        da2 = da2 + dot_nt(du, weight(g_ref, 3 + j))
    dh1 = dy * (1.0 - t2) + norm_back(da2, unit, scale, g2)
    dz1 = (dh1 * (att - x) * t1 * (1.0 - t1)).astype(BF16)
    datt = (dh1 * t1).astype(BF16)
    dz1_ref[...] = dz1
    datt_ref[...] = datt
    dh1_ref[...] = dh1 * (1.0 - t1)
    do_ref[...] = dot_nt(datt, w_attn).astype(BF16)

    def total(v):
        return jnp.sum(v, axis=0, keepdims=True)

    dvec_ref[2:3, :] += total(dz1.astype(F32))
    dvec_ref[3:4, :] += total(da2 * unit)
    dvec_ref[4:5, :] += total(da2)
    dvec_ref[5:6, :] += total(dz2.astype(F32))


def lower(ref, j):
    nf, base, wide = ref.shape[0], 7 * SUB, (FF // D) * SUB
    per = D // wide // nf
    part = ref[:, per * j : per * (j + 1), base : base + wide, :]
    return part.swapaxes(0, 1).reshape(D, D)


def middle(x, a1, o, dy, vec, g2, rows=256):
    t = x.shape[0]

    def row(width):
        return pl.BlockSpec((rows, width), lambda i: (i, 0))

    shapes = [(D, BF16), (D, F32), (D, BF16), (FF, BF16), (D, BF16), (FF, BF16), (D, BF16), (D, BF16), (D, BF16), (D, BF16)]
    return pl.pallas_call(
        middle_kernel,
        grid=(t // rows,),
        in_specs=[row(D)] * 4
        + [pl.BlockSpec((8, D), lambda i: (0, 0)), pl.BlockSpec(g2.shape, lambda i: (0, 0, 0, 0), pipeline_mode=pl.Buffered(1))],
        out_specs=[row(w) for w, _ in shapes] + [pl.BlockSpec((8, D), lambda i: (0, 0))],
        out_shape=[jax.ShapeDtypeStruct((t, w), ty) for w, ty in shapes] + [jax.ShapeDtypeStruct((8, D), F32)],
        compiler_params=params(56),
        cost_estimate=pl.CostEstimate(flops=2 * t * D * (4 * FF + 6 * D), bytes_accessed=24 * MIB, transcendentals=t * FF),
        name="middle",
    )(x, a1, o, dy, vec, g2)


def grads_kernel(a1_ref, o_ref, a2_ref, e_ref, df_ref, du_ref, dz2_ref, dz1_ref, datt_ref, out_ref):
    step = pl.program_id(0)
    for j in range(FF // D):
        @pl.when(step == j)
        def _(j=j):
            put(out_ref, 3 + j, dot_tn(a2_ref[...], du_ref[...]))
            nf, base, wide = out_ref.shape[0], 7 * SUB, (FF // D) * SUB
            per = D // wide // nf
            low = dot_tn(e_ref[...], df_ref[...]).astype(out_ref.dtype)
            out_ref[:, per * j : per * (j + 1), base : base + wide, :] = low.reshape(
                per, nf, wide, D
            ).swapaxes(0, 1)

    @pl.when(step == FF // D)
    def _():
        put(out_ref, 0, dot_tn(o_ref[...], datt_ref[...]))
        put(out_ref, 1, dot_tn(a1_ref[...], dz1_ref[...]))
        put(out_ref, 2, dot_tn(a2_ref[...], dz2_ref[...]))


def grads(a1, o, a2, e, df, du, dz2, dz1, datt, nf, nd):
    t = a1.shape[0]
    last = FF // D - 1

    def whole():
        return pl.BlockSpec((t, D), lambda i: (0, 0))

    col = pl.BlockSpec((t, D), lambda i: (0, jnp.minimum(i, last)))
    shape = (nf, nd, 11 * SUB, D)
    return pl.pallas_call(
        grads_kernel,
        grid=(FF // D + 1,),
        in_specs=[whole(), whole(), whole(), col, whole(), col, whole(), whole(), whole()],
        out_specs=pl.BlockSpec(shape, lambda i: (0, 0, 0, 0)),
        out_shape=jax.ShapeDtypeStruct(shape, BF16),
        compiler_params=params(56),
        cost_estimate=pl.CostEstimate(flops=2 * t * D * (2 * FF + 3 * D), bytes_accessed=24 * MIB, transcendentals=0),
        name="grads",
    )(a1, o, a2, e, df, du, dz2, dz1, datt)


def final_kernel(
    x_ref, a1_ref, dq_ref, dk_ref, dv_ref, dz1_ref, part_ref, vec_ref, dvec_ref, g1_ref, g2_ref,
    dx_ref, out_ref, acc_ref,
):
    step = pl.program_id(0)
    rows = x_ref.shape[0]

    @pl.when(step == 0)
    def _():
        acc_ref[...] = dvec_ref[...]

    unit, scale = normed(x_ref[...].astype(F32))
    da1 = dot_nt(dz1_ref[...], weight(g2_ref, 1))
    here = pl.ds(pl.multiple_of(step * rows, rows), rows)
    for j, ref in enumerate((dq_ref, dk_ref, dv_ref)):
        da1 = da1 + dot_nt(ref[here, :], weight(g1_ref, j))
    dx_ref[...] = part_ref[...] + norm_back(da1, unit, scale, vec_ref[0:1, :])
    acc_ref[0:1, :] += jnp.sum(da1 * unit, axis=0, keepdims=True)
    acc_ref[1:2, :] += jnp.sum(da1, axis=0, keepdims=True)

    @pl.when(step == pl.num_programs(0) - 1)
    def _():
        for j, ref in enumerate((dq_ref, dk_ref, dv_ref)):
            put(out_ref, j, dot_tn(a1_ref[...], ref[...]))
        wide = jnp.concatenate([acc_ref[...], jnp.zeros((120, D), F32)], axis=0).T
        put(out_ref, 3, jnp.concatenate([wide, jnp.zeros((D, D - 128), F32)], axis=1))


def final(x, a1, dq, dk, dv, dz1, part, vec, dvec, g1, g2, nf, nd, rows=256):
    t = x.shape[0]

    def row(width=D):
        return pl.BlockSpec((rows, width), lambda i: (i, 0))

    def whole(shape):
        return pl.BlockSpec(shape, lambda i: (0,) * len(shape), pipeline_mode=pl.Buffered(1))

    shape = (nf, nd, 4 * SUB, D)
    return pl.pallas_call(
        final_kernel,
        grid=(t // rows,),
        in_specs=[row(), whole((t, D)), whole((t, D)), whole((t, D)), whole((t, D)), row(), row(), whole((8, D)), whole((8, D)), whole(g1.shape), whole(g2.shape[:2] + (2 * SUB, D))],
        out_specs=[row(), pl.BlockSpec(shape, lambda i: (0, 0, 0, 0))],
        out_shape=[jax.ShapeDtypeStruct((t, D), F32), jax.ShapeDtypeStruct(shape, BF16)],
        scratch_shapes=[pltpu.VMEM((8, D), F32)],
        compiler_params=params(56),
        cost_estimate=pl.CostEstimate(flops=2 * t * D * 7 * D, bytes_accessed=24 * MIB, transcendentals=0),
        name="final",
    )(x, a1, dq, dk, dv, dz1, part, vec, dvec, g1, g2)


def collect_kernel(first_ref, second_ref, r1_ref, r2_ref, sq_ref):
    r1 = jnp.sum(first_ref[...].astype(F32), axis=0)
    r2 = jnp.sum(second_ref[...].astype(F32), axis=0)
    r1_ref[...] = r1
    r2_ref[...] = r2
    sq_ref[...] = jnp.broadcast_to(jnp.sum(r1 * r1) + jnp.sum(r2 * r2), sq_ref.shape)


def collect(first, second, n):
    return pl.pallas_call(
        collect_kernel,
        out_shape=[
            jax.ShapeDtypeStruct(first.shape[1:], F32),
            jax.ShapeDtypeStruct(second.shape[1:], F32),
            jax.ShapeDtypeStruct((n, 8, 128), F32),
        ],
        compiler_params=params(48),
        cost_estimate=pl.CostEstimate(flops=MIB, bytes_accessed=8 * MIB, transcendentals=0),
        name="collect",
    )(first, second)


RATES = (D ** (-0.5), (D // 16) ** (-0.5), D ** (-0.5), D ** (-0.5), FF ** (-0.5), D ** (-0.5), 0.5)


def update(grad, master, moment, square, clip, rate):
    clipped = grad * clip
    new_moment = 0.5 * moment + 0.5 * clipped
    new_square = 0.5 * square + 0.5 * clipped * clipped
    fix = 1.0 - 0.5**STEP
    stepped = new_moment / fix / (jnp.sqrt(new_square / fix) + 1e-08)
    return (master - rate * (stepped + 0.01 * master), new_moment, new_square)


def adam_kernel(*refs):
    r1_ref, r2_ref, sq_ref = refs[:3]
    state = refs[3:24]
    sub = r1_ref.shape[0] // 4
    norm_ref = refs[24]
    outs = refs[25:]
    total = jnp.sum(sq_ref[...], axis=0)[0:1, 0:1]
    norm = jnp.sqrt(total)
    norm_ref[...] = jnp.broadcast_to(norm, norm_ref.shape)
    clip = jnp.minimum(1.0, 1.0 / (norm + 1e-06))

    def piece(index, grad, at):
        got = update(grad, state[3 * index][at], state[3 * index + 1][at], state[3 * index + 2][at], clip, RATES[index])
        for k in range(3):
            outs[3 * index + k][at] = got[k]

    every = slice(None)
    for j in range(3):
        piece(0, r1_ref[sub * j : sub * (j + 1), :], (every, slice(D * j, D * (j + 1))))
    piece(6, r1_ref[3 * sub : 4 * sub, 0:6], (every, every))
    piece(1, r2_ref[0:sub, :], (every, every))
    piece(2, r2_ref[sub : 2 * sub, :], (every, every))
    piece(5, r2_ref[2 * sub : 3 * sub, :], (every, every))
    for j in range(FF // D):
        piece(3, r2_ref[sub * (3 + j) : sub * (4 + j), :], (every, slice(D * j, D * (j + 1))))
    piece(4, r2_ref[7 * sub : 11 * sub, :], (every, every))


def adam(r1, r2, squares, state):
    return pl.pallas_call(
        adam_kernel,
        out_shape=[jax.ShapeDtypeStruct((1, 128), F32)] + [jax.ShapeDtypeStruct(s.shape, F32) for s in state],
        compiler_params=params(48),
        cost_estimate=pl.CostEstimate(flops=4 * MIB, bytes_accessed=4 * MIB, transcendentals=0),
        name="adam",
    )(r1, r2, squares, *state)


def forward_backward(x, dy, halves, g1, g2, nf, nd):
    a1, qkv, vec = project(x, g1)
    o, lse = attend(halves, qkv)
    y, part, a2, e, df, du, dz2, dz1, datt, do, dvec = middle(x, a1, o, dy, vec, g2)
    terms2 = grads(a1, o, a2, e, df, du, dz2, dz1, datt, nf, nd)
    dq, dk, dv = attend_back(halves, qkv, o, do, lse)
    dx, terms1 = final(x, a1, dq, dk, dv, dz1, part, vec, dvec, g1, g2, nf, nd)
    return y, dx, terms1, terms2


def column_blocks(w):
    return [w[..., D * j : D * (j + 1)] for j in range(w.shape[-1] // D)]


def widen(norms):
    return jnp.pad(norms, ((0, 0), (0, D - norms.shape[1])))


def pack(weights):
    qkv, attn, gate, up, down, fgate, norms = weights
    one = jnp.concatenate(column_blocks(qkv) + [widen(norms)], axis=-2)
    two = jnp.concatenate([attn, gate, fgate] + column_blocks(up) + [down], axis=-2)
    return one, two


def pack_whole(weights):
    split = [w.reshape(OWNERS, w.shape[0] // OWNERS, w.shape[1]) for w in weights]
    split[6] = jnp.pad(split[6], ((0, 0), (0, 0), (0, D - split[6].shape[2])))
    one = jnp.concatenate(column_blocks(split[0]) + [split[6]], axis=1)
    two = jnp.concatenate(split[1:3] + split[5:6] + column_blocks(split[3]) + split[4:5], axis=1)
    return one, two


def unpack_whole(one, two):
    def blocks(g, start, count):
        parts = [g[:, SUB * j : SUB * (j + 1), :] for j in range(start, start + count)]
        return jnp.concatenate(parts, axis=2).reshape(D, count * D)

    return (
        blocks(one, 0, 3),
        blocks(two, 0, 1),
        blocks(two, 1, 1),
        blocks(two, 3, FF // D),
        two[:, 7 * SUB :, :].reshape(FF, D),
        blocks(two, 2, 1),
        blocks(one, 3, 1)[:, :6],
    )


def body(nd, nf, tokens, cotangent, halves, *state):
    n = nd * nf
    both = ("dp", "fsdp")
    rounded = [m.astype(BF16) for m in state[0::3]]
    if n == OWNERS:
        one, two = pack(rounded)
        spread = jnp.broadcast_to(one[None], (nd,) + one.shape)
        g1 = lax.all_to_all(spread, "dp", 0, 0, tiled=True)
        g1 = lax.all_gather(g1, "fsdp", axis=0)
        g2 = lax.all_gather(two, both, axis=0)[None]
        y, dx, terms1, terms2 = forward_backward(tokens, cotangent, halves, g1, g2, nf, nd)
        got2 = lax.psum_scatter(terms2, "fsdp", scatter_dimension=0)
        got2 = lax.all_to_all(got2, "dp", 0, 0, tiled=True)
        terms1 = terms1.reshape((n,) + terms1.shape[2:])
        got1 = lax.all_to_all(terms1, ("fsdp", "dp"), 0, 0, tiled=True)
    else:
        whole = [lax.all_gather(w, both, axis=0, tiled=True) for w in rounded]
        one, two = pack_whole(whole)
        y, dx, terms1, terms2 = forward_backward(
            tokens, cotangent, halves, one[None], two[None], 1, OWNERS
        )
        terms = unpack_whole(terms1[0].astype(F32), terms2[0].astype(F32))
        got = [lax.psum_scatter(t, both, scatter_dimension=0, tiled=True) for t in terms]
        one, two = pack(got)
        got1, got2 = one[None], two[None]
    r1, r2, squares = collect(got1, got2, n)
    squares = lax.all_to_all(squares, both, 0, 0, tiled=True)
    norm, *new = adam(r1, r2, squares, state)
    return (y, dx, norm[0, 0], *new)


def solution(mesh):
    rows = P(("dp", "fsdp"), None)
    nd, nf = mesh.shape["dp"], mesh.shape["fsdp"]
    return jax.shard_map(
        functools.partial(body, nd, nf),
        mesh=mesh,
        in_specs=(rows, rows, P(("dp", "fsdp"))) + (rows,) * 21,
        out_specs=(rows, rows, P()) + (rows,) * 21,
        check_vma=False,
    )
```

```python
import functools
import jax
import jax.numpy as jnp
from jax import lax
from jax.experimental import pallas as pl
from jax.experimental.pallas import tpu as pltpu
from jax.sharding import PartitionSpec as P

D = 512
H = 8
HD = 64
FF = 2048
STEP = 5
PAIRS = H // 2
SUB = 16
OWNERS = D // SUB
COLS = FF // D
F32 = jnp.float32
BF16 = jnp.bfloat16
MIB = 1024 * 1024
CORES = 2


def params():
    return pltpu.CompilerParams(vmem_limit_bytes=60 * MIB)


def cost(flops, mib, trans=0):
    return pl.CostEstimate(flops=flops, bytes_accessed=int(mib * MIB), transcendentals=trans)


def dot(a, b):
    return lax.dot_general(a, b, (((1,), (0,)), ((), ())), preferred_element_type=F32)


def dot_nt(a, b):
    return lax.dot_general(a, b, (((1,), (1,)), ((), ())), preferred_element_type=F32)


def normed(values):
    center = values - jnp.mean(values, axis=-1, keepdims=True)
    scale = lax.rsqrt(jnp.mean(center * center, axis=-1, keepdims=True) + 1e-05)
    return center * scale, scale


def norm_back(grad, unit, scale, gain):
    inner = grad * gain
    first = jnp.mean(inner, axis=-1, keepdims=True)
    second = jnp.mean(inner * unit, axis=-1, keepdims=True)
    return scale * (inner - first - unit * second)


def full(shape, once=True):
    zeros = (0,) * len(shape)
    if once:
        return pl.BlockSpec(shape, lambda *_: zeros, pipeline_mode=pl.Buffered(1))
    return pl.BlockSpec(shape, lambda *_: zeros)


def turned(values):
    return values.T.reshape(OWNERS // CORES, CORES, SUB, values.shape[0])


def sds(shape, dtype):
    return jax.ShapeDtypeStruct(shape, dtype)


def hbm(value):
    return pltpu.with_memory_space_constraint(value, pltpu.HBM)


def launch(kernel, name, ins, outs, grid=(), scratch=(), price=None, deps=(), scalars=0, aliases=None):
    count = len(ins)

    def wrapped(*refs):
        kernel(*refs[:count], *refs[count + len(deps) :])

    in_specs = [s for _, s in ins[scalars:]] + [pl.BlockSpec(memory_space=pl.ANY)] * len(deps)
    return pl.pallas_call(
        wrapped if deps else kernel,
        grid_spec=pltpu.PrefetchScalarGridSpec(
            num_scalar_prefetch=scalars,
            grid=grid,
            in_specs=in_specs,
            out_specs=[s for _, s in outs],
            scratch_shapes=list(scratch),
        ),
        out_shape=[o for o, _ in outs],
        input_output_aliases=aliases or {},
        compiler_params=params(),
        cost_estimate=price,
        name=name,
    )(*[a for a, _ in ins], *deps)


def project_kernel(me_ref, x_ref, *refs):
    parts = refs[:-5]
    a1t_ref, a_ref, qkv_ref, vec_ref, w_ref = refs[-5:]
    count = len(parts)

    @pl.when(pl.program_id(0) == 0)
    def _():
        per = OWNERS // count
        for k, part in enumerate(parts):
            here = jnp.bitwise_xor(me_ref[0], k)
            for d in range(per):
                at = pl.ds(pl.multiple_of((d * count + here) * SUB, SUB), SUB)
                w_ref[at, :] = part[d]
        vec_ref[...] = w_ref[:, 3 * D : 3 * D + 128].astype(F32).T[0:8, :]

    unit, _ = normed(x_ref[...].astype(F32))
    a1 = (unit * vec_ref[0:1, :] + vec_ref[1:2, :]).astype(BF16)
    a_ref[...] = a1
    a1t_ref[...] = turned(a1)
    for j in range(3):
        qkv_ref[j] = dot(a1, w_ref[:, j * D : (j + 1) * D]).astype(BF16)


def project(at, x, parts, rows=512):
    t = x.shape[0]
    width = parts[0].shape[-1]
    row = pl.BlockSpec((rows, D), lambda i, *_: (i, 0))
    pairs = OWNERS // CORES
    return launch(
        project_kernel,
        "project",
        [(at, None), (x, row)] + [(p, full(p.shape)) for p in parts],
        [
            (sds((pairs, CORES, SUB, t), BF16), pl.BlockSpec((pairs, CORES, SUB, rows), lambda i, *_: (0, 0, 0, i))),
            (sds((t, D), BF16), row),
            (sds((3, t, D), BF16), pl.BlockSpec((3, rows, D), lambda i, *_: (0, i, 0))),
            (sds((8, D), F32), full((8, D), False)),
            (sds((D, width), BF16), full((D, width), False)),
        ],
        grid=(t // rows,),
        price=cost(2 * t * D * 3 * D, 9),
        scalars=1,
    )


BLK = 256


def lane_half(shape, head):
    lane = lax.broadcasted_iota(jnp.int32, shape, 1)
    return (lane >= HD) if head else (lane < HD)


def key_range(i, two, length):
    per = length // BLK
    if two and i >= per // 2:
        return per // 2
    return 0


def diagonal():
    row = lax.broadcasted_iota(jnp.int32, (BLK, BLK), 0)
    col = lax.broadcasted_iota(jnp.int32, (BLK, BLK), 1)
    return row <= col


def attend_kernel(halves_ref, qkv_ref, o_ref, ot_ref, lse_ref, vt_ref):
    q_ref, k_ref, v_ref = (qkv_ref.at[j] for j in range(3))
    length = q_ref.shape[0]
    vt_ref[...] = v_ref[...].T
    allowed = diagonal()

    def block(i, first):
        rows = slice(i * BLK, (i + 1) * BLK)
        qs = q_ref[rows, :] * jnp.bfloat16(0.125)
        outs = []
        for head in range(2):
            qh = jnp.where(lane_half(qs.shape, head), qs, jnp.bfloat16(0))
            st = dot_nt(k_ref[first * BLK : (i + 1) * BLK, :], qh)
            n = i - first
            last = jnp.where(allowed, st[n * BLK :, :], -1e30)
            top = jnp.max(last, axis=0, keepdims=True)
            if n:
                top = jnp.maximum(top, jnp.max(st[: n * BLK, :], axis=0, keepdims=True))
            elast = jnp.exp(last - top)
            total = jnp.sum(elast, axis=0, keepdims=True)
            if n:
                erest = jnp.exp(st[: n * BLK, :] - top)
                total = total + jnp.sum(erest, axis=0, keepdims=True)
                expo = jnp.concatenate([erest, elast], axis=0)
            else:
                expo = elast
            vt = vt_ref[head * HD : (head + 1) * HD, first * BLK : (i + 1) * BLK]
            ot = dot(vt, expo.astype(BF16))
            outs.append(ot * (1.0 / total))
            lse_ref[0, head : head + 1, rows] = top + jnp.log(total)
        out = jnp.concatenate(outs, axis=0).astype(BF16)
        ot_ref[:, :, :, rows] = out.reshape(128 // SUB // CORES, CORES, SUB, BLK)
        o_ref[rows, :] = out.T

    per = length // BLK
    for i in range(per // 2):
        block(i, 0)

    @pl.when(halves_ref[0] == 0)
    def _():
        for i in range(per // 2, per):
            block(i, 0)

    @pl.when(halves_ref[0] != 0)
    def _():
        for i in range(per // 2, per):
            block(i, per // 2)


def attend(halves, qkv):
    t = qkv.shape[1]
    pairs = OWNERS // CORES
    part = 128 // SUB // CORES
    return launch(
        attend_kernel,
        "attend",
        [
            (halves, None),
            (qkv, pl.BlockSpec((3, t, 128), lambda p, *_: (0, 0, p))),
        ],
        [
            (sds((t, D), BF16), pl.BlockSpec((t, 128), lambda p, *_: (0, p))),
            (sds((pairs, CORES, SUB, t), BF16), pl.BlockSpec((part, CORES, SUB, t), lambda p, *_: (p, 0, 0, 0))),
            (sds((PAIRS, 2, t), F32), pl.BlockSpec((1, 2, t), lambda p, *_: (p, 0, 0))),
        ],
        grid=(PAIRS,),
        scratch=[pltpu.VMEM((128, t), BF16)],
        price=cost(4 * t * t * D, 8, t * t * H),
        scalars=1,
    )


def attend_back_kernel(halves_ref, qkv_ref, o_ref, do_ref, lse_ref, dqkv_ref, kt_ref, qt_ref, dot_ref, dkt_ref, dvt_ref):
    q_ref, k_ref, v_ref = (qkv_ref.at[j] for j in range(3))
    dq_ref, dk_ref, dv_ref = (dqkv_ref.at[j] for j in range(3))
    length = q_ref.shape[0]
    kt_ref[...] = k_ref[...].T
    qt_ref[...] = q_ref[...].T
    dot_ref[...] = do_ref[...].T
    prod = (do_ref[...].astype(F32) * o_ref[...].astype(F32)).T
    delta = [jnp.sum(prod[head * HD : (head + 1) * HD, :], axis=0, keepdims=True) for head in range(2)]
    dkt_ref[...] = jnp.zeros_like(dkt_ref)
    dvt_ref[...] = jnp.zeros_like(dvt_ref)
    allowed = diagonal()

    def block(i, first):
        rows = slice(i * BLK, (i + 1) * BLK)
        keys = slice(first * BLK, (i + 1) * BLK)
        qs = q_ref[rows, :] * jnp.bfloat16(0.125)
        dob = do_ref[rows, :]
        outs = []
        n = i - first
        for head in range(2):
            half = lane_half(qs.shape, head)
            own = slice(head * HD, (head + 1) * HD)
            qh = jnp.where(half, qs, jnp.bfloat16(0))
            dh = jnp.where(half, dob, jnp.bfloat16(0))
            lse = lse_ref[0, head : head + 1, rows]
            st = dot_nt(k_ref[keys, :], qh)
            dpt = dot_nt(v_ref[keys, :], dh)
            last = jnp.where(allowed, jnp.exp(st[n * BLK :, :] - lse), 0.0)
            if n:
                pt = jnp.concatenate([jnp.exp(st[: n * BLK, :] - lse), last], axis=0)
            else:
                pt = last
            dst = (pt * (dpt - delta[head][:, rows])).astype(BF16)
            pb = pt.astype(BF16)
            dvt_ref[own, keys] += dot_nt(dot_ref[own, rows], pb)
            dkt_ref[own, keys] += dot_nt(qt_ref[own, rows], dst)
            outs.append(dot(kt_ref[own, keys], dst) * 0.125)
        dq_ref[rows, :] = jnp.concatenate(outs, axis=0).T.astype(BF16)

    per = length // BLK
    for i in range(per // 2):
        block(i, 0)

    @pl.when(halves_ref[0] == 0)
    def _():
        for i in range(per // 2, per):
            block(i, 0)

    @pl.when(halves_ref[0] != 0)
    def _():
        for i in range(per // 2, per):
            block(i, per // 2)

    dk_ref[...] = (dkt_ref[...] * 0.125).T.astype(BF16)
    dv_ref[...] = dvt_ref[...].T.astype(BF16)


def attend_back_first(halves, qkv, o, do, lse, count):
    t = qkv.shape[1]
    col = pl.BlockSpec((t, 128), lambda p, *_: (0, p))
    three = pl.BlockSpec((3, t, 128), lambda p, *_: (0, 0, p))
    return launch(
        attend_back_kernel,
        "attend_back_first",
        [(halves, None), (qkv, three), (o, col), (do, col), (lse, pl.BlockSpec((1, 2, t), lambda p, *_: (p, 0, 0)))],
        [(sds((3, t, D), BF16), three)],
        grid=(count,),
        scratch=[pltpu.VMEM((128, t), BF16)] * 3 + [pltpu.VMEM((128, t), F32)] * 2,
        price=cost(10 * t * t * 128 * count, 2.5 * count, t * t * 2 * count),
        scalars=1,
    )[0]


def attend_back_rest(halves, qkv, o, do, lse, into, first, deps=()):
    t = qkv.shape[1]
    col = pl.BlockSpec((t, 128), lambda p, *_: (0, first + p))
    three = pl.BlockSpec((3, t, 128), lambda p, *_: (0, 0, first + p))
    count = PAIRS - first
    return launch(
        attend_back_kernel,
        "attend_back_rest",
        [(halves, None), (qkv, three), (o, col), (do, col), (lse, pl.BlockSpec((1, 2, t), lambda p, *_: (first + p, 0, 0)))],
        [(sds((3, t, D), BF16), three)],
        grid=(count,),
        scratch=[pltpu.VMEM((128, t), BF16)] * 3 + [pltpu.VMEM((128, t), F32)] * 2,
        price=cost(10 * t * t * 128 * count, 2.5 * count, t * t * 2 * count),
        scalars=1,
        deps=(into,) + tuple(deps),
        aliases={5: 0},
    )[0]


def joint_kernel(me_ref, a1t_ref, dqkv_ref, own_ref, other_ref):
    t = dqkv_ref.shape[1]
    split_cores(me_ref, dot(a1t_ref[...].reshape(D, t), dqkv_ref[0]), own_ref, other_ref)


def joint_grads(me, a1t, dqkv, deps=()):
    t = dqkv.shape[1]
    pairs = OWNERS // CORES
    out = (sds((pairs, SUB, 3 * D), BF16), pl.BlockSpec((pairs, SUB, D), lambda i, *_: (0, 0, i)))
    return launch(
        joint_kernel,
        "joint_grads",
        [(me, None), (a1t, full(a1t.shape)), (dqkv, pl.BlockSpec((1, t, D), lambda i, *_: (i, 0, 0)))],
        [out, out],
        grid=(3,),
        price=cost(2 * t * D * 3 * D, 6),
        scalars=1,
        deps=deps,
    )


def block_of(ref, j):
    return ref[:, :, :, SUB * j : SUB * (j + 1), :].reshape(D, D)


def lower(ref, j):
    halfway = COLS // CORES
    core, part = j // halfway, j % halfway
    per = ref.shape[0] // halfway
    base, wide = (3 + COLS) * SUB, COLS * SUB
    return ref[per * part : per * (part + 1), :, core, base : base + wide, :].reshape(D, D)


FIRST = COLS + 2
SECOND = COLS + 1


def middle_rows(x_ref, a1_ref, o_ref, dy_ref, vec_ref, g_ref, y_ref, part_ref, dz1o_ref, do_ref, dvec_ref,
                a2t_ref, et_ref, df_ref, du_ref, dz2_ref, dz1_ref, datt_ref, step):
    rows = x_ref.shape[0]
    here = pl.ds(pl.multiple_of(step * rows, rows), rows)
    c1, g2, b2, c2 = (vec_ref[k : k + 1, :] for k in (2, 3, 4, 5))
    x = x_ref[...].astype(F32)
    att = dot(o_ref[...], block_of(g_ref, 0))
    t1 = jax.nn.sigmoid(dot(a1_ref[...], block_of(g_ref, 1)) + c1)
    h1 = t1 * att + (1.0 - t1) * x
    unit, scale = normed(h1)
    a2 = (unit * g2 + b2).astype(BF16)
    a2t_ref[:, :, :, here] = turned(a2)
    t2 = jax.nn.sigmoid(dot(a2, block_of(g_ref, 2)) + c2)
    f = None
    slopes = []
    kc = 0.7978845608028654
    for j in range(COLS):
        u = dot(a2, block_of(g_ref, 3 + j))
        sq = u * u
        half = 0.5 * jnp.tanh(u * (kc + (kc * 0.044715) * sq)) + 0.5
        gel = u * half
        e = gel.astype(BF16)
        slopes.append(half + gel * (1.0 - half) * (2.0 * kc + (6.0 * kc * 0.044715) * sq))
        et_ref[j, :, :, here] = e.T.reshape(et_ref.shape[1:3] + (rows,))
        part = dot(e, lower(g_ref, j))
        f = part if f is None else f + part
    y_ref[...] = (t2 * f + (1.0 - t2) * h1).astype(BF16)
    dy = dy_ref[...].astype(F32)
    dz2 = (dy * (f - h1) * t2 * (1.0 - t2)).astype(BF16)
    df = (dy * t2).astype(BF16)
    dz2_ref[here, :] = dz2
    df_ref[here, :] = df
    da2 = dot_nt(dz2, block_of(g_ref, 2))
    for j in range(COLS):
        du = (dot_nt(df, lower(g_ref, j)) * slopes[j]).astype(BF16)
        du_ref[j, here, :] = du
        da2 = da2 + dot_nt(du, block_of(g_ref, 3 + j))
    dh1 = dy * (1.0 - t2) + norm_back(da2, unit, scale, g2)
    dz1 = (dh1 * (att - x) * t1 * (1.0 - t1)).astype(BF16)
    datt = (dh1 * t1).astype(BF16)
    dz1_ref[here, :] = dz1
    dz1o_ref[...] = dz1
    datt_ref[here, :] = datt
    part_ref[...] = dh1 * (1.0 - t1)
    do_ref[...] = dot_nt(datt, block_of(g_ref, 0)).astype(BF16)

    def total(v):
        return jnp.sum(v, axis=0, keepdims=True)

    dvec_ref[2:3, :] += total(dz1.astype(F32))
    dvec_ref[3:4, :] += total(da2 * unit)
    dvec_ref[4:5, :] += total(da2)
    dvec_ref[5:6, :] += total(dz2.astype(F32))


def split_cores(me_ref, value, own_ref, other_ref):
    value = value.reshape(OWNERS // CORES, CORES, SUB, D)
    low = me_ref[0] == 0
    own_ref[...] = jnp.where(low, value[:, 0], value[:, 1]).astype(BF16)
    other_ref[...] = jnp.where(low, value[:, 1], value[:, 0]).astype(BF16)


def middle_kernel(
    me_ref, x_ref, a1_ref, o_ref, dy_ref, vec_ref, g_ref, a1t_ref, ot_ref,
    y_ref, part_ref, dz1o_ref, do_ref, dvec_ref, own1_ref, other1_ref, own2_ref, other2_ref,
    a2t_ref, et_ref, df_ref, du_ref, dz2_ref, dz1_ref, datt_ref,
):
    step = pl.program_id(0)
    t = df_ref.shape[0]
    blocks = t // x_ref.shape[0]

    @pl.when(step == 0)
    def _():
        dvec_ref[...] = jnp.zeros_like(dvec_ref)

    @pl.when(step < blocks)
    def _():
        middle_rows(x_ref, a1_ref, o_ref, dy_ref, vec_ref, g_ref, y_ref, part_ref, dz1o_ref, do_ref, dvec_ref,
                    a2t_ref, et_ref, df_ref, du_ref, dz2_ref, dz1_ref, datt_ref, step)

    def product(left, right, own_ref, other_ref):
        split_cores(me_ref, dot(left.reshape(D, t), right), own_ref, other_ref)

    @pl.when((step >= blocks) & (step < blocks + COLS))
    def _():
        product(a2t_ref[...], du_ref[step - blocks], own1_ref, other1_ref)

    @pl.when(step == blocks + COLS)
    def _():
        product(a2t_ref[...], dz2_ref[...], own1_ref, other1_ref)

    @pl.when(step == blocks + COLS + 1)
    def _():
        product(ot_ref[...], datt_ref[...], own1_ref, other1_ref)

    begin = blocks + FIRST
    for j in range(COLS):
        @pl.when(step == begin + j)
        def _(j=j):
            left = et_ref[:, :, SUB * j : SUB * (j + 1), :]
            left = left.reshape(CORES, OWNERS // CORES, SUB, t).swapaxes(0, 1)
            product(left, df_ref[...], own2_ref, other2_ref)

    @pl.when(step == begin + COLS)
    def _():
        product(a1t_ref[...], dz1_ref[...], own2_ref, other2_ref)


def middle(me, x, a1, o, dy, vec, g, a1t, ot, rows=512):
    t = x.shape[0]
    blocks = t // rows
    pairs = OWNERS // CORES
    row = pl.BlockSpec((rows, D), lambda i, *_: (jnp.minimum(i, blocks - 1), 0))

    def terms(begin, count):
        return pl.BlockSpec((pairs, SUB, D), lambda i, *_: (0, jnp.clip(i - begin, 0, count - 1), 0))

    one, two = terms(blocks, FIRST), terms(blocks + FIRST, SECOND)
    wide = FF // OWNERS
    return launch(
        middle_kernel,
        "middle",
        [(me, None)]
        + [(v, row) for v in (x, a1, o, dy)]
        + [(v, full(v.shape)) for v in (vec, g, a1t, ot)],
        [
            (sds((t, D), BF16), row),
            (sds((t, D), F32), row),
            (sds((t, D), BF16), row),
            (sds((t, D), BF16), row),
            (sds((8, D), F32), full((8, D), False)),
            (sds((pairs, FIRST * SUB, D), BF16), one),
            (sds((pairs, FIRST * SUB, D), BF16), one),
            (sds((pairs, SECOND * SUB, D), BF16), two),
            (sds((pairs, SECOND * SUB, D), BF16), two),
        ],
        grid=(blocks + FIRST + SECOND,),
        scratch=[
            pltpu.VMEM((pairs, CORES, SUB, t), BF16),
            pltpu.VMEM((COLS, D // wide, wide, t), BF16),
            pltpu.VMEM((t, D), BF16),
            pltpu.VMEM((COLS, t, D), BF16),
            pltpu.VMEM((t, D), BF16),
            pltpu.VMEM((t, D), BF16),
            pltpu.VMEM((t, D), BF16),
        ],
        price=cost(2 * t * D * (6 * FF + 9 * D), 20, t * FF),
        scalars=1,
    )


def merge_kernel(bits, me_ref, *refs):
    count = len(bits)
    for k, bit in enumerate(bits):
        own_ref, got_ref = refs[2 * k], refs[2 * k + 1]
        keep_ref, send_ref = refs[2 * count + 2 * k], refs[2 * count + 2 * k + 1]
        sums = [own_ref[:, j].astype(F32) + got_ref[:, j].astype(F32) for j in range(2)]
        low = me_ref[bit] == 0
        keep_ref[...] = jnp.where(low, sums[0], sums[1]).astype(BF16)
        send_ref[...] = jnp.where(low, sums[1], sums[0]).astype(BF16)


def merge(me, items, steps=1, deps=()):
    ins, outs, bits = [(me, None)], [], []
    for own, got, bit, inner in items:
        blocks, rows, width = own.shape
        outer = blocks // (2 * inner)
        both = pl.BlockSpec((outer // steps, 2, inner, rows, width), lambda i, *_: (i, 0, 0, 0, 0))
        half = pl.BlockSpec((outer // steps, inner, rows, width), lambda i, *_: (i, 0, 0, 0))
        ins += [(hbm(v.reshape(outer, 2, inner, rows, width)), both) for v in (own, got)]
        outs += [(sds((outer, inner, rows, width), BF16), half)] * 2
        bits.append(bit)
    done = launch(
        functools.partial(merge_kernel, tuple(bits)),
        "merge",
        ins,
        outs,
        grid=(steps,),
        price=cost(MIB, 3 * len(items)),
        scalars=1,
        deps=deps,
    )
    return [v.reshape((v.shape[0] * v.shape[1],) + v.shape[2:]) for v in done]


def sum_kernel(me_ref, *refs):
    begin = 0
    ins = [r for r in refs if len(r.shape) == 3]
    outs = refs[len(ins) :]
    if not outs:
        ins, outs = refs[:-1], refs[-1:]
    for k in range(0, len(ins), 2):
        rows = ins[k].shape[1]
        if len(outs) == 1:
            total = ins[k][...].astype(F32) + ins[k + 1][...].astype(F32)
            outs[0][:, begin : begin + rows, :] = total.astype(BF16)
        else:
            for j, out_ref in enumerate(outs):
                at = jnp.bitwise_xor(me_ref[3], j)
                total = ins[k][at].astype(F32) + ins[k + 1][at].astype(F32)
                out_ref[begin : begin + rows, :] = total.astype(BF16)
        begin += rows


def sum_pairs(me, items, split=False, deps=()):
    ins = [(hbm(v), full(v.shape)) for item in items for v in item]
    blocks, _, width = items[0][0].shape
    rows = sum(one.shape[1] for one, _ in items)
    shapes = [(rows, width)] * blocks if split else [(blocks, rows, width)]
    return launch(
        sum_kernel,
        "sum_pairs",
        [(me, None)] + ins,
        [(sds(s, BF16), full(s, False)) for s in shapes],
        grid=(1,),
        price=cost(MIB, 2),
        scalars=1,
        deps=deps,
    )


def joint_sum_kernel(count, me_ref, keep_ref, far_ref, *refs):
    out_ref = refs[count]
    width = keep_ref.shape[2]
    out_ref[:, :, :width] = (keep_ref[...].astype(F32) + far_ref[...].astype(F32)).astype(BF16)
    vec = refs[0][...]
    for k in range(1, count):
        vec = vec + refs[k][...]
    vec = jnp.concatenate([vec, jnp.zeros((120, D), F32)], axis=0).T
    vec = vec.reshape(out_ref.shape[0], 2, CORES, SUB, 128)
    mine = jnp.where(me_ref[1] == 0, vec[:, 0], vec[:, 1])
    out_ref[:, :, width:] = jnp.where(me_ref[0] == 0, mine[:, 0], mine[:, 1]).astype(BF16)


def joint_sum(me, keep, far, vecs, deps=()):
    shape = keep.shape[:2] + (keep.shape[2] + 128,)
    ins = [hbm(keep), hbm(far)] + list(vecs)
    return launch(
        functools.partial(joint_sum_kernel, len(vecs)),
        "joint_sum",
        [(me, None)] + [(v, full(v.shape)) for v in ins],
        [(sds(shape, BF16), full(shape, False))],
        grid=(1,),
        price=cost(MIB, 2),
        scalars=1,
        deps=deps,
    )[0]


def inputs_kernel(x_ref, dqkv_ref, dz1_ref, part_ref, vec_ref, dvec_ref, w_ref, g_ref, dx_ref, out_ref, acc_ref):
    step = pl.program_id(0)

    @pl.when(step == 0)
    def _():
        acc_ref[...] = dvec_ref[...]

    unit, scale = normed(x_ref[...].astype(F32))
    da1 = dot_nt(dz1_ref[...], block_of(g_ref, 1))
    for j in range(3):
        da1 = da1 + dot_nt(dqkv_ref[j], w_ref[:, D * j : D * (j + 1)])
    dx_ref[...] = part_ref[...] + norm_back(da1, unit, scale, vec_ref[0:1, :])
    acc_ref[0:1, :] += jnp.sum(da1 * unit, axis=0, keepdims=True)
    acc_ref[1:2, :] += jnp.sum(da1, axis=0, keepdims=True)

    @pl.when(step == pl.num_programs(0) - 1)
    def _():
        out_ref[...] = acc_ref[...]


def inputs(x, dqkv, dz1, part, vec, dvec, w, g, rows=512, deps=()):
    t = x.shape[0]
    row = pl.BlockSpec((rows, D), lambda i: (i, 0))
    narrow = g.shape[:3] + (2 * SUB, D)
    shape = (8, D)
    return launch(
        inputs_kernel,
        "inputs",
        [
            (x, row),
            (dqkv, pl.BlockSpec((3, rows, D), lambda i: (0, i, 0))),
            (dz1, row),
            (part, row),
            (vec, full((8, D))),
            (dvec, full((8, D))),
            (w, full(w.shape)),
            (g, full(narrow)),
        ],
        [(sds((t, D), F32), row), (sds(shape, F32), full(shape, False))],
        grid=(t // rows,),
        scratch=[pltpu.VMEM((8, D), F32)],
        price=cost(2 * t * D * 4 * D, 12),
        deps=deps,
    )


def collect_kernel(counts, *refs):
    total = jnp.float32(0.0)
    begin = 0
    outs = refs[sum(counts) :]
    for k, count in enumerate(counts):
        parts = refs[begin : begin + count]
        begin += count
        if count == 1:
            value = jnp.sum(parts[0][...].astype(F32), axis=0)
        else:
            value = sum(p[...].astype(F32) for p in parts)
        outs[k][...] = value
        total = total + jnp.sum(value * value)
    outs[-1][...] = jnp.full(outs[-1].shape, total, F32)


def collect(groups, n):
    shapes = [g[0].shape[1:] if len(g) == 1 else g[0].shape for g in groups]
    return pl.pallas_call(
        functools.partial(collect_kernel, tuple(len(g) for g in groups)),
        out_shape=[sds(s, F32) for s in shapes] + [sds((n, 8, 128), F32)],
        compiler_params=params(),
        cost_estimate=cost(MIB, 3),
        name="collect",
    )(*[v for g in groups for v in g])


RATES = (D ** (-0.5), (D // 16) ** (-0.5), D ** (-0.5), D ** (-0.5), FF ** (-0.5), D ** (-0.5), 0.5)


def update(grad, master, moment, square, clip, rate):
    clipped = grad * clip
    new_moment = 0.5 * moment + 0.5 * clipped
    new_square = 0.5 * square + 0.5 * clipped * clipped
    fix = 1.0 - 0.5**STEP
    stepped = new_moment / fix / (jnp.sqrt(new_square / fix) + 1e-08)
    return (master - rate * (stepped + 0.01 * master), new_moment, new_square)


def adam_kernel(*refs):
    down_ref, joint_ref, sq_ref = refs[:3]
    state = refs[3:24]
    norm_ref = refs[24]
    outs = refs[25:]
    sub = joint_ref.shape[0]
    norm = jnp.sqrt(jnp.sum(sq_ref[...], axis=0)[0:1, 0:1])
    norm_ref[...] = jnp.broadcast_to(norm, norm_ref.shape)
    clip = jnp.minimum(1.0, 1.0 / (norm + 1e-06))

    def piece(index, grad, at):
        old = [state[3 * index + k][at] for k in range(3)]
        new = update(grad, *old, clip, RATES[index])
        for k in range(3):
            outs[3 * index + k][at] = new[k]

    every = slice(None)
    piece(0, joint_ref[:, : 3 * D], (every, every))
    turned_vec = jnp.concatenate([joint_ref[:, 3 * D :], jnp.zeros((128 - sub, 128), F32)], axis=0).T
    piece(6, turned_vec[0:6, 0:sub], (every, every))

    def down(j, count=1):
        return down_ref[sub * j : sub * (j + count), :]

    up = jnp.concatenate([down(j) for j in range(COLS)], axis=1)
    step = FF // OWNERS
    order = [up[:, FF // CORES * c + step * p :][:, :step] for p in range(OWNERS // CORES) for c in range(CORES)]
    piece(3, jnp.concatenate(order, axis=1), (every, every))
    piece(5, down(COLS), (every, every))
    piece(1, down(COLS + 1), (every, every))
    piece(4, down(COLS + 2, COLS), (every, every))
    piece(2, down(2 * COLS + 2), (every, every))


def adam(grads, squares, state):
    return pl.pallas_call(
        adam_kernel,
        out_shape=[sds((1, 128), F32)] + [sds(s.shape, F32) for s in state],
        compiler_params=params(),
        cost_estimate=cost(4 * MIB, 4),
        name="adam",
    )(*grads, squares, *state)


def ordered(up):
    rows = up.shape[0]
    return up.reshape(rows, OWNERS // CORES, CORES, FF // OWNERS).swapaxes(1, 2).reshape(rows, FF)


def turn_norms(state):
    return tuple(state[:18]) + tuple(s.T for s in state[18:])


def column_blocks(w):
    return [w[..., D * j : D * (j + 1)] for j in range(w.shape[-1] // D)]


def pack_kernel(qkv_ref, attn_ref, gate_ref, up_ref, down_ref, fgate_ref, norms_ref, one_ref, two_ref):
    sub = qkv_ref.shape[0]
    norms = jnp.concatenate([norms_ref[...], jnp.zeros((128 - norms_ref.shape[0], sub), F32)], axis=0)
    norms = jnp.concatenate([norms, jnp.zeros((128, 128 - sub), F32)], axis=1).T[0:sub]
    one = jnp.concatenate([qkv_ref[...], norms], axis=1).astype(BF16)
    for k in range(one_ref.shape[0]):
        one_ref[k] = one
    for j, ref in enumerate((attn_ref, gate_ref, fgate_ref)):
        two_ref[sub * j : sub * (j + 1), :] = ref[...].astype(BF16)
    step = FF // OWNERS
    up = up_ref[...]
    order = [up[:, step * (CORES * p + c) :][:, :step] for c in range(CORES) for p in range(OWNERS // CORES)]
    up = jnp.concatenate(order, axis=1).astype(BF16)
    for j in range(COLS):
        two_ref[sub * (3 + j) : sub * (4 + j), :] = up[:, D * j : D * (j + 1)]
    two_ref[sub * (3 + COLS) :, :] = down_ref[...].astype(BF16)


def pack(masters, copies):
    sub = masters[0].shape[0]
    return pl.pallas_call(
        pack_kernel,
        out_shape=[sds((copies, sub, 3 * D + 128), BF16), sds(((3 + 2 * COLS) * sub, D), BF16)],
        compiler_params=params(),
        cost_estimate=cost(MIB, 3),
        name="pack",
    )(*masters[:6], masters[6].T)


def pack_whole(weights):
    qkv, attn, gate, up, down, fgate, norms = weights
    one = jnp.concatenate([qkv, jnp.pad(norms, ((0, 0), (0, 128 - norms.shape[1])))], axis=1)
    parts = [attn, gate, fgate] + column_blocks(ordered(up))
    parts = [p.reshape(OWNERS, SUB, D) for p in parts] + [down.reshape(OWNERS, COLS * SUB, D)]
    return one.reshape(OWNERS, SUB, one.shape[1]), jnp.concatenate(parts, axis=1)


def unpack_whole(one, two, joint, vec):
    def blocks(g, start, count):
        parts = [g[:, SUB * j : SUB * (j + 1), :].reshape(D, D) for j in range(start, start + count)]
        return jnp.concatenate(parts, axis=1)

    up = blocks(one, 0, COLS).reshape(D, CORES, OWNERS // CORES, FF // OWNERS)
    return (
        joint.reshape(D, 3 * D),
        blocks(one, COLS + 1, 1),
        blocks(two, COLS, 1),
        up.swapaxes(1, 2).reshape(D, FF),
        two[:, : COLS * SUB, :].reshape(FF, D),
        blocks(one, COLS, 1),
        vec[:6].T,
    )


def swap(value, axis, size, bit):
    return lax.ppermute(value, axis, [(i, i ^ bit) for i in range(size)])


def body(nd, nf, tokens, cotangent, halves, *state):
    n = nd * nf
    if n == OWNERS and nf == 2 * CORES:
        return direct(nd, nf, tokens, cotangent, halves, *state)
    return general(n, tokens, cotangent, halves, *state)


def direct(nd, nf, tokens, cotangent, halves, *state):
    both = ("dp", "fsdp")
    nx = nf // CORES
    place_f = lax.axis_index("fsdp").astype(jnp.int32)
    place_d = lax.axis_index("dp").astype(jnp.int32)
    me = jnp.stack([place_f % 2, place_f // 2, place_d % 2, place_d // 2])

    def to_core(v):
        return swap(v, "fsdp", nf, 1)

    def to_x(v):
        return swap(v, "fsdp", nf, CORES)

    def to_y(v):
        return swap(v, "dp", nd, 1)

    def to_z(parts):
        return [parts[0]] + [swap(v, "dp", nd, 2 * k) for k, v in enumerate(parts) if k]

    def over_dp(v):
        return lax.all_to_all(v, "dp", 0, 0, tiled=True)

    copies, two = pack(state[0::3], nd)
    g2 = lax.all_gather(two, both, axis=0)
    own = over_dp(copies)
    far = to_x(own)
    parts = [hbm(v) for v in (own, to_core(own), far, to_core(far))]
    g2 = g2.reshape((nd, nx, CORES) + two.shape)

    a1t, a1, qkv, vec, w = project(place_f[None], tokens, parts)
    o, ot, lse = attend(halves, qkv)
    y, part, dz1, do, dvec, own1, other1, own2, other2 = middle(
        me, tokens, a1, o, cotangent, vec, g2, a1t, ot
    )
    got1, got2 = to_core(other1), to_core(other2)
    head = attend_back_first(halves, qkv, o, do, lse, 1)
    keep1, send1, keep2, send2 = merge(me, [(own1, got1, 1, 1), (own2, got2, 2, nx)], 4, deps=(head,))
    far1, far2 = to_x(send1), to_y(send2)
    dqkv = attend_back_rest(halves, qkv, o, do, lse, head, 1, deps=(keep1,))
    keep1, send1, keep2, send2 = merge(
        me, [(keep1, far1, 2, 1), (keep2, far2, 1, 1)], 2, deps=(dqkv,)
    )
    far1, far2 = to_y(send1), to_x(send2)
    own3, other3 = joint_grads(me, a1t, dqkv, deps=(keep1,))
    keep3, send3 = merge(me, [(own3, to_core(other3), 1, 1)])
    far3 = to_x(send3)
    out1 = sum_pairs(me, [(keep1, far1), (keep2, far2)], split=True, deps=(keep3,))
    in1 = to_z(out1)
    dx, dvec = inputs(tokens, dqkv, dz1, part, vec, dvec, w, g2, deps=(out1[0],))
    vecs = [dvec] + [swap(dvec, "fsdp", nf, k) for k in range(1, nf)]
    in3 = over_dp(joint_sum(me, keep3, far3, vecs, deps=tuple(in1[1:])))

    *grads, squares = collect([in1, [in3]], nd * nf)
    squares = lax.all_to_all(squares, both, 0, 0, tiled=True)
    norm, *new = adam(grads, squares, turn_norms(state))
    return (y, dx, norm[0, 0], *turn_norms(new))


def layer_general(me, tokens, cotangent, halves, one, g2):
    a1t, a1, qkv, vec, w = project(me[:1], tokens, [one])
    o, ot, lse = attend(halves, qkv)
    y, part, dz1, do, dvec, own1, other1, own2, other2 = middle(
        me, tokens, a1, o, cotangent, vec, g2, a1t, ot
    )
    head = attend_back_first(halves, qkv, o, do, lse, 1)
    dqkv = attend_back_rest(halves, qkv, o, do, lse, head, 1)
    own3, other3 = joint_grads(me, a1t, dqkv)
    dx, dvec = inputs(tokens, dqkv, dz1, part, vec, dvec, w, g2)

    def owners(own, other):
        return jnp.stack([own, other], axis=1).reshape((OWNERS,) + own.shape[1:]).astype(F32)

    return (y, dx) + unpack_whole(owners(own1, other1), owners(own2, other2), owners(own3, other3), dvec)


def general(n, tokens, cotangent, halves, *state):
    both = ("dp", "fsdp")
    rounded = [m.astype(BF16) for m in state[0::3]]
    one, g2 = pack_whole([lax.all_gather(w, both, axis=0, tiled=True) for w in rounded])
    g2 = g2.reshape((OWNERS // CORES, 1, CORES) + g2.shape[1:])
    me = jnp.zeros((2,), jnp.int32)
    y, dx, *terms = layer_general(me, tokens, cotangent, halves, one, g2)
    q, wo, wa, wu, wd, wf, nv = [
        lax.psum_scatter(t, both, scatter_dimension=0, tiled=True) for t in terms
    ]
    got = [
        jnp.concatenate(column_blocks(ordered(wu)) + [wf, wo, wd, wa], axis=0),
        jnp.concatenate([q, jnp.pad(nv, ((0, 0), (0, 128 - nv.shape[1])))], axis=1),
    ]
    *grads, squares = collect([[g[None]] for g in got], n)
    squares = lax.all_to_all(squares, both, 0, 0, tiled=True)
    norm, *new = adam(grads, squares, turn_norms(state))
    return (y, dx, norm[0, 0], *turn_norms(new))


def solution(mesh):
    rows = P(("dp", "fsdp"), None)
    nd, nf = mesh.shape["dp"], mesh.shape["fsdp"]
    return jax.shard_map(
        functools.partial(body, nd, nf),
        mesh=mesh,
        in_specs=(rows, rows, P(("dp", "fsdp"))) + (rows,) * 21,
        out_specs=(rows, rows, P()) + (rows,) * 21,
        check_vma=False,
    )
```

```python
import functools
import jax
import jax.numpy as jnp
from jax import lax
from jax.experimental import pallas as pl
from jax.experimental.pallas import tpu as pltpu
from jax.sharding import PartitionSpec as P

D = 512
H = 8
HD = 64
FF = 2048
STEP = 5
PAIRS = H // 2
SUB = 16
OWNERS = D // SUB
COLS = FF // D
F32 = jnp.float32
BF16 = jnp.bfloat16
MIB = 1024 * 1024
CORES = 2


def params(mib):
    return pltpu.CompilerParams(vmem_limit_bytes=mib * MIB)


def cost(flops, mib, trans=0):
    return pl.CostEstimate(flops=flops, bytes_accessed=int(mib * MIB), transcendentals=trans)


def dot(a, b):
    return lax.dot_general(a, b, (((1,), (0,)), ((), ())), preferred_element_type=F32)


def dot_nt(a, b):
    return lax.dot_general(a, b, (((1,), (1,)), ((), ())), preferred_element_type=F32)


def normed(values):
    center = values - jnp.mean(values, axis=-1, keepdims=True)
    scale = lax.rsqrt(jnp.mean(center * center, axis=-1, keepdims=True) + 1e-05)
    return center * scale, scale


def norm_back(grad, unit, scale, gain):
    inner = grad * gain
    first = jnp.mean(inner, axis=-1, keepdims=True)
    second = jnp.mean(inner * unit, axis=-1, keepdims=True)
    return scale * (inner - first - unit * second)


def full(shape, once=True):
    zeros = (0,) * len(shape)
    if once:
        return pl.BlockSpec(shape, lambda *_: zeros, pipeline_mode=pl.Buffered(1))
    return pl.BlockSpec(shape, lambda *_: zeros)


def turned(values):
    return values.T.reshape(OWNERS // CORES, CORES, SUB, values.shape[0])


def sds(shape, dtype):
    return jax.ShapeDtypeStruct(shape, dtype)


def hbm(value):
    return pltpu.with_memory_space_constraint(value, pltpu.HBM)


def launch(kernel, name, ins, outs, grid, scratch=(), price=None, deps=(), scalars=0, aliases=None, room=24):
    count = len(ins)

    def wrapped(*refs):
        kernel(*refs[:count], *refs[count + len(deps) :])

    in_specs = [s for _, s in ins[scalars:]] + [pl.BlockSpec(memory_space=pl.ANY)] * len(deps)
    return pl.pallas_call(
        wrapped if deps else kernel,
        grid_spec=pltpu.PrefetchScalarGridSpec(
            num_scalar_prefetch=scalars,
            grid=grid,
            in_specs=in_specs,
            out_specs=[s for _, s in outs],
            scratch_shapes=list(scratch),
        ),
        out_shape=[o for o, _ in outs],
        input_output_aliases=aliases or {},
        compiler_params=params(room),
        cost_estimate=price,
        name=name,
    )(*[a for a, _ in ins], *deps)


def local(kernel, name, me, ins, outs, deps=()):
    count = 1 + len(ins)

    def wrapped(*refs):
        kernel(*refs[:count], *refs[count + len(deps) :])

    vmem = pl.BlockSpec(memory_space=pltpu.VMEM)
    return pl.pallas_call(
        wrapped,
        in_specs=[pl.BlockSpec(memory_space=pltpu.SMEM)] + [vmem] * len(ins) + [pl.BlockSpec(memory_space=pl.ANY)] * len(deps),
        out_specs=[vmem] * len(outs),
        out_shape=outs,
        compiler_params=params(16),
        cost_estimate=cost(MIB, 4),
        name=name,
    )(me, *ins, *deps)


def project_kernel(me_ref, x_ref, *refs):
    parts = refs[:-5]
    a1t_ref, a_ref, qkv_ref, vec_ref, w_ref = refs[-5:]
    count = len(parts)

    @pl.when(pl.program_id(0) == 0)
    def _():
        for k, part in enumerate(parts):
            for d in range(OWNERS // count):
                owner = jnp.bitwise_xor(me_ref[5], d * count + k)
                w_ref[pl.ds(pl.multiple_of(owner * SUB, SUB), SUB), :] = part[d]
        vec_ref[...] = w_ref[:, 3 * D : 3 * D + 128].astype(F32).T[0:8, :]

    unit, _ = normed(x_ref[...].astype(F32))
    a1 = (unit * vec_ref[0:1, :] + vec_ref[1:2, :]).astype(BF16)
    a_ref[...] = a1
    a1t_ref[...] = turned(a1)
    for j in range(3):
        qkv_ref[j] = dot(a1, w_ref[:, j * D : (j + 1) * D]).astype(BF16)


def project(me, x, parts, rows=512):
    t = x.shape[0]
    width = parts[0].shape[-1]
    row = pl.BlockSpec((rows, D), lambda i, *_: (i, 0))
    pairs = OWNERS // CORES
    return launch(
        project_kernel,
        "project",
        [(me, None), (x, row)] + [(p, full(p.shape)) for p in parts],
        [
            (sds((pairs, CORES, SUB, t), BF16), pl.BlockSpec((pairs, CORES, SUB, rows), lambda i, *_: (0, 0, 0, i))),
            (sds((t, D), BF16), row),
            (sds((3, t, D), BF16), pl.BlockSpec((3, rows, D), lambda i, *_: (0, i, 0))),
            (sds((8, D), F32), full((8, D), False)),
            (sds((D, width), BF16), full((D, width), False)),
        ],
        grid=(t // rows,),
        price=cost(2 * t * D * 3 * D, 9),
        scalars=1,
    )


def by_head(values):
    lane = lax.broadcasted_iota(jnp.int32, values.shape, 1)
    zero = jnp.zeros_like(values)
    return jnp.concatenate(
        [jnp.where(lane < HD, values, zero), jnp.where(lane >= HD, values, zero)], axis=0
    )


def own_blocks(values, blk):
    return jnp.concatenate([values[:HD, :blk], values[HD:, blk:]], axis=0)


def diagonal(blk):
    row = lax.broadcasted_iota(jnp.int32, (blk, 2 * blk), 0)
    col = lax.broadcasted_iota(jnp.int32, (blk, 2 * blk), 1)
    return row <= jnp.where(col >= blk, col - blk, col)


def over_blocks(halves_ref, per, front, back):
    def path(firsts):
        ready = front(0, firsts[0])
        for i in range(per):
            later = front(i + 1, firsts[i + 1]) if i + 1 < per else None
            back(i, firsts[i], ready)
            ready = later

    @pl.when(halves_ref[0] == 0)
    def _():
        path([0] * per)

    @pl.when(halves_ref[0] != 0)
    def _():
        path([0] * (per // 2) + [per // 2] * (per // 2))


FORWARD_BLOCK = 512
BACK_BLOCK = 128


def attend_kernel(halves_ref, qkv_ref, o_ref, ot_ref, lse_ref, vt_ref):
    q_ref, k_ref, v_ref = (qkv_ref.at[j] for j in range(3))
    blk = FORWARD_BLOCK
    vt_ref[...] = v_ref[...].T
    allowed = diagonal(blk)

    def front(i, first):
        queries = by_head(q_ref[i * blk : (i + 1) * blk, :] * jnp.bfloat16(0.125))
        return dot_nt(k_ref[first * blk : (i + 1) * blk, :], queries)

    def back(i, first, st):
        rows = slice(i * blk, (i + 1) * blk)
        n = (i - first) * blk
        last = jnp.where(allowed, st[n:, :], -1e30)
        top = jnp.max(last, axis=0, keepdims=True)
        if n:
            top = jnp.maximum(top, jnp.max(st[:n, :], axis=0, keepdims=True))
        expo = jnp.exp(last - top)
        total = jnp.sum(expo, axis=0, keepdims=True)
        expo = expo.astype(BF16)
        if n:
            rest = jnp.exp(st[:n, :] - top)
            total = total + jnp.sum(rest, axis=0, keepdims=True)
            expo = jnp.concatenate([rest.astype(BF16), expo], axis=0)
        out = dot(vt_ref[:, first * blk : (i + 1) * blk], expo) * (1.0 / total)
        out = own_blocks(out, blk).astype(BF16)
        lse = top + jnp.log(total)
        lse_ref[0, 0:1, rows] = lse[:, :blk]
        lse_ref[0, 1:2, rows] = lse[:, blk:]
        ot_ref[:, :, :, rows] = out.reshape(128 // SUB // CORES, CORES, SUB, blk)
        o_ref[rows, :] = out.T

    over_blocks(halves_ref, q_ref.shape[0] // blk, front, back)


def attend(halves, qkv, deps=()):
    t = qkv.shape[1]
    pairs = OWNERS // CORES
    part = 128 // SUB // CORES
    return launch(
        attend_kernel,
        "attend",
        [
            (halves, None),
            (qkv, pl.BlockSpec((3, t, 128), lambda p, *_: (0, 0, p))),
        ],
        [
            (sds((t, D), BF16), pl.BlockSpec((t, 128), lambda p, *_: (0, p))),
            (sds((pairs, CORES, SUB, t), BF16), pl.BlockSpec((part, CORES, SUB, t), lambda p, *_: (p, 0, 0, 0))),
            (sds((PAIRS, 2, t), F32), pl.BlockSpec((1, 2, t), lambda p, *_: (p, 0, 0))),
        ],
        grid=(PAIRS,),
        scratch=[pltpu.VMEM((128, t), BF16)],
        price=cost(4 * t * t * D, 8, t * t * H),
        scalars=1,
        deps=deps,
    )


def attend_back_kernel(halves_ref, qkv_ref, o_ref, do_ref, lse_ref, dqkv_ref, kt_ref, dk_ref, dv_ref):
    q_ref, k_ref, v_ref = (qkv_ref.at[j] for j in range(3))
    blk = BACK_BLOCK
    kt_ref[...] = k_ref[...].T
    prod = (do_ref[...].astype(F32) * o_ref[...].astype(F32)).T
    delta = [jnp.sum(prod[h * HD : (h + 1) * HD, :], axis=0, keepdims=True) for h in range(2)]
    allowed = diagonal(blk)

    def front(i, first):
        rows, keys = slice(i * blk, (i + 1) * blk), slice(first * blk, (i + 1) * blk)
        queries = by_head(q_ref[rows, :] * jnp.bfloat16(0.125))
        grads = by_head(do_ref[rows, :])
        return queries, grads, dot_nt(k_ref[keys, :], queries), dot_nt(v_ref[keys, :], grads)

    def gather(ref, first, i, value):
        n = (i - first) * blk
        if n:
            ref[first * blk : i * blk, :] += value[:n]
        ref[i * blk : (i + 1) * blk, :] = value[n:]

    def back(i, first, ready):
        queries, grads, st, dpt = ready
        rows, keys = slice(i * blk, (i + 1) * blk), slice(first * blk, (i + 1) * blk)
        n = (i - first) * blk
        lse = jnp.concatenate([lse_ref[0, 0:1, rows], lse_ref[0, 1:2, rows]], axis=1)
        rowsum = jnp.concatenate([d[:, rows] for d in delta], axis=1)
        pt = jnp.where(allowed, jnp.exp(st[n:, :] - lse), 0.0)
        if n:
            pt = jnp.concatenate([jnp.exp(st[:n, :] - lse), pt], axis=0)
        dst = (pt * (dpt - rowsum)).astype(BF16)
        gather(dv_ref, first, i, dot(pt.astype(BF16), grads))
        gather(dk_ref, first, i, dot(dst, queries))
        dqt = dot(kt_ref[:, keys], dst) * 0.125
        dqkv_ref[0, rows, :] = own_blocks(dqt, blk).T.astype(BF16)

    over_blocks(halves_ref, q_ref.shape[0] // blk, front, back)
    dqkv_ref[1] = dk_ref[...].astype(BF16)
    dqkv_ref[2] = dv_ref[...].astype(BF16)


def attend_back_first(halves, qkv, o, do, lse, count):
    t = qkv.shape[1]
    col = pl.BlockSpec((t, 128), lambda p, *_: (0, p))
    three = pl.BlockSpec((3, t, 128), lambda p, *_: (0, 0, p))
    return launch(
        attend_back_kernel,
        "attend_back_first",
        [(halves, None), (hbm(qkv), three), (hbm(o), col), (hbm(do), col), (lse, pl.BlockSpec((1, 2, t), lambda p, *_: (p, 0, 0)))],
        [(sds((3, t, D), BF16), three)],
        grid=(count,),
        scratch=[pltpu.VMEM((128, t), BF16)] + [pltpu.VMEM((t, 128), F32)] * 2,
        price=cost(10 * t * t * 128 * count, 2.5 * count, t * t * 2 * count),
        scalars=1,
    )[0]


def attend_back_rest(halves, qkv, o, do, lse, into, first, deps=()):
    t = qkv.shape[1]
    col = pl.BlockSpec((t, 128), lambda p, *_: (0, first + p))
    three = pl.BlockSpec((3, t, 128), lambda p, *_: (0, 0, first + p))
    count = PAIRS - first
    return launch(
        attend_back_kernel,
        "attend_back_rest",
        [(halves, None), (hbm(qkv), three), (hbm(o), col), (hbm(do), col), (lse, pl.BlockSpec((1, 2, t), lambda p, *_: (first + p, 0, 0)))],
        [(sds((3, t, D), BF16), three)],
        grid=(count,),
        scratch=[pltpu.VMEM((128, t), BF16)] + [pltpu.VMEM((t, 128), F32)] * 2,
        price=cost(10 * t * t * 128 * count, 2.5 * count, t * t * 2 * count),
        scalars=1,
        deps=(into,) + tuple(deps),
        aliases={5: 0},
    )[0]


def joint_kernel(me_ref, a1t_ref, dqkv_ref, own_ref, other_ref):
    t = dqkv_ref.shape[1]
    split_cores(me_ref, dot(a1t_ref[...].reshape(D, t), dqkv_ref[0]), own_ref, other_ref)


def joint_grads(me, a1t, dqkv, deps=()):
    t = dqkv.shape[1]
    pairs = OWNERS // CORES
    out = (sds((pairs, SUB, 3 * D), BF16), pl.BlockSpec((pairs, SUB, D), lambda i, *_: (0, 0, i)))
    return launch(
        joint_kernel,
        "joint_grads",
        [(me, None), (a1t, full(a1t.shape)), (dqkv, pl.BlockSpec((1, t, D), lambda i, *_: (i, 0, 0)))],
        [out, out],
        grid=(3,),
        price=cost(2 * t * D * 3 * D, 6),
        scalars=1,
        deps=deps,
    )


NEAR = 3 * SUB
ROWS = NEAR + 2 * COLS * SUB
CUT = NEAR + 3 * SUB


def near_weight(ref, j):
    return ref[:, SUB * j : SUB * (j + 1), :].reshape(D, D)


def block_of(ref, j):
    return near_weight(ref, 3 + j)


def lower(ref, j):
    halfway = COLS // CORES
    core, part = j // halfway, j % halfway
    per = OWNERS // CORES // halfway
    rows = [ref[CORES * p + core, NEAR + COLS * SUB : ROWS, :] for p in range(per * part, per * (part + 1))]
    return jnp.concatenate(rows, axis=0)


def middle_rows(x_ref, a1_ref, o_ref, dy_ref, vec_ref, w_ref, y_ref, part_ref, dz1o_ref, do_ref, dvec_ref,
                a2t_ref, et_ref, df_ref, du_ref, dz2_ref, dz1_ref, datt_ref, step):
    rows = x_ref.shape[0]
    here = pl.ds(pl.multiple_of(step * rows, rows), rows)
    c1, g2, b2, c2 = (vec_ref[k : k + 1, :] for k in (2, 3, 4, 5))
    x = x_ref[...].astype(F32)
    att = dot(o_ref[...], near_weight(w_ref, 0))
    t1 = jax.nn.sigmoid(dot(a1_ref[...], near_weight(w_ref, 1)) + c1)
    h1 = t1 * att + (1.0 - t1) * x
    unit, scale = normed(h1)
    a2 = (unit * g2 + b2).astype(BF16)
    a2t_ref[:, :, :, here] = turned(a2)
    t2 = jax.nn.sigmoid(dot(a2, near_weight(w_ref, 2)) + c2)
    f = None
    slopes = []
    kc = 0.7978845608028654
    for j in range(COLS):
        u = dot(a2, block_of(w_ref, j))
        sq = u * u
        half = 0.5 * jnp.tanh(u * (kc + (kc * 0.044715) * sq)) + 0.5
        gel = u * half
        e = gel.astype(BF16)
        slopes.append(half + gel * (1.0 - half) * (2.0 * kc + (6.0 * kc * 0.044715) * sq))
        et_ref[j, :, :, here] = e.T.reshape(et_ref.shape[1:3] + (rows,))
        part = dot(e, lower(w_ref, j))
        f = part if f is None else f + part
    y_ref[...] = (t2 * f + (1.0 - t2) * h1).astype(BF16)
    dy = dy_ref[...].astype(F32)
    dz2 = (dy * (f - h1) * t2 * (1.0 - t2)).astype(BF16)
    df = (dy * t2).astype(BF16)
    dz2_ref[here, :] = dz2
    df_ref[here, :] = df
    da2 = dot_nt(dz2, near_weight(w_ref, 2))
    for j in range(COLS):
        du = (dot_nt(df, lower(w_ref, j)) * slopes[j]).astype(BF16)
        du_ref[j, here, :] = du
        da2 = da2 + dot_nt(du, block_of(w_ref, j))
    dh1 = dy_ref[...].astype(F32) * (1.0 - t2) + norm_back(da2, unit, scale, g2)
    dz1 = (dh1 * (att - x_ref[...].astype(F32)) * t1 * (1.0 - t1)).astype(BF16)
    datt = (dh1 * t1).astype(BF16)
    dz1_ref[here, :] = dz1
    dz1o_ref[...] = dz1
    datt_ref[here, :] = datt
    part_ref[...] = dh1 * (1.0 - t1)
    do_ref[...] = dot_nt(datt, near_weight(w_ref, 0)).astype(BF16)

    def total(v):
        return jnp.sum(v, axis=0, keepdims=True)

    dvec_ref[2:3, :] += total(dz1.astype(F32))
    dvec_ref[3:4, :] += total(da2 * unit)
    dvec_ref[4:5, :] += total(da2)
    dvec_ref[5:6, :] += total(dz2.astype(F32))


def split_cores(me_ref, value, own_ref, other_ref, at=slice(None)):
    value = value.reshape(OWNERS // CORES, CORES, SUB, D)
    low = me_ref[0] == 0
    own_ref[:, at, :] = jnp.where(low, value[:, 0], value[:, 1]).astype(BF16)
    other_ref[:, at, :] = jnp.where(low, value[:, 1], value[:, 0]).astype(BF16)


SETS = (2, 2, 1)


def middle_kernel(plan, *refs):
    count = len(plan)
    me_ref, x_ref, a1_ref, o_ref, dy_ref, vec_ref = refs[:6]
    sources = refs[6 : 6 + count]
    a1t_hbm, ot_hbm = refs[6 + count : 8 + count]
    y_ref, part_ref, dz1o_ref, do_ref, dvec_ref, wa_ref = refs[8 + count : 14 + count]
    own1, other1, own2, other2, own3, other3 = refs[14 + count : 20 + count]
    w_ref, a1t_ref, ot_ref, sem, a2t_ref, et_ref, df_ref, du_ref, dz2_ref, dz1_ref, datt_ref = refs[20 + count :]
    step = pl.program_id(0)
    t = df_ref.shape[0]
    blocks = t // x_ref.shape[0]

    def copies():
        return [
            pltpu.make_async_copy(a1t_hbm, a1t_ref, sem.at[0]),
            pltpu.make_async_copy(ot_hbm, ot_ref, sem.at[1]),
        ]

    @pl.when(step == 0)
    def _():
        gets = []
        for source, (first, rows, distances) in zip(sources, plan):
            for k, distance in enumerate(distances):
                owner = jnp.bitwise_xor(me_ref[5], distance)
                to = w_ref.at[owner, first : first + rows, :]
                gets.append(pltpu.make_async_copy(source.at[k], to, sem.at[2 + len(gets)]))
        for copy in gets + copies():
            copy.start()
        dvec_ref[...] = jnp.zeros_like(dvec_ref)
        for copy in gets:
            copy.wait()
        wa_ref[...] = near_weight(w_ref, 1)

    @pl.when(step < blocks)
    def _():
        middle_rows(x_ref, a1_ref, o_ref, dy_ref, vec_ref, w_ref, y_ref, part_ref, dz1o_ref, do_ref, dvec_ref,
                    a2t_ref, et_ref, df_ref, du_ref, dz2_ref, dz1_ref, datt_ref, step)

    def product(left, right, own_ref, other_ref, j):
        at = slice(SUB * j, SUB * (j + 1))
        split_cores(me_ref, dot(left.reshape(D, t), right), own_ref, other_ref, at)

    each = COLS // SETS[0]
    for k in range(SETS[0]):
        @pl.when(step == blocks + k)
        def _(k=k):
            for j in range(each):
                product(a2t_ref[...], du_ref[each * k + j], own1, other1, j)

    for k in range(SETS[1]):
        @pl.when(step == blocks + SETS[0] + k)
        def _(k=k):
            for j in range(each):
                at = SUB * (each * k + j)
                left = et_ref[:, :, at : at + SUB, :]
                left = left.reshape(CORES, OWNERS // CORES, SUB, t).swapaxes(0, 1)
                product(left, df_ref[...], own2, other2, j)

    @pl.when(step == blocks + SETS[0] + SETS[1])
    def _():
        for copy in copies():
            copy.wait()
        product(a2t_ref[...], dz2_ref[...], own3, other3, 0)
        product(ot_ref[...], datt_ref[...], own3, other3, 1)
        product(a1t_ref[...], dz1_ref[...], own3, other3, 2)


def middle(me, x, a1, o, dy, vec, sources, a1t, ot, rows=512):
    t = x.shape[0]
    blocks = t // rows
    pairs = OWNERS // CORES
    row = pl.BlockSpec((rows, D), lambda i, *_: (jnp.minimum(i, blocks - 1), 0))
    outs = []
    begin = blocks
    for steps, wide in zip(SETS, (COLS, COLS, 3)):
        block = (pairs, SUB * wide // steps, D)
        spec = pl.BlockSpec(block, lambda i, *_, begin=begin, steps=steps: (0, jnp.clip(i - begin, 0, steps - 1), 0))
        outs += [(sds((pairs, SUB * wide, D), BF16), spec)] * 2
        begin += steps
    wide = FF // OWNERS
    plan = tuple((first, v.shape[1], tuple(distances)) for v, first, distances in sources)
    hbm_ref = pl.BlockSpec(memory_space=pl.ANY)
    return launch(
        functools.partial(middle_kernel, plan),
        "middle",
        [(me, None)]
        + [(v, row) for v in (x, a1, o, dy)]
        + [(vec, full(vec.shape))]
        + [(v, hbm_ref) for v, _, _ in sources]
        + [(a1t, hbm_ref), (ot, hbm_ref)],
        [
            (sds((t, D), BF16), row),
            (sds((t, D), F32), row),
            (sds((t, D), BF16), row),
            (sds((t, D), BF16), row),
            (sds((8, D), F32), full((8, D), False)),
            (sds((D, D), BF16), full((D, D), False)),
        ]
        + outs,
        grid=(begin,),
        scratch=[
            pltpu.VMEM((OWNERS, ROWS, D), BF16),
            pltpu.VMEM((pairs, CORES, SUB, t), BF16),
            pltpu.VMEM((pairs, CORES, SUB, t), BF16),
            pltpu.SemaphoreType.DMA((2 + sum(len(p[2]) for p in plan),)),
            pltpu.VMEM((pairs, CORES, SUB, t), BF16),
            pltpu.VMEM((COLS, D // wide, wide, t), BF16),
            pltpu.VMEM((t, D), BF16),
            pltpu.VMEM((COLS, t, D), BF16),
            pltpu.VMEM((t, D), BF16),
            pltpu.VMEM((t, D), BF16),
            pltpu.VMEM((t, D), BF16),
        ],
        price=cost(2 * t * D * (6 * FF + 9 * D), 20, t * FF),
        scalars=1,
        room=60,
    )


def merge_kernel(bits, me_ref, *refs):
    count = len(bits)
    for k, bit in enumerate(bits):
        own_ref, got_ref = refs[2 * k], refs[2 * k + 1]
        keep_ref, send_ref = refs[2 * count + 2 * k], refs[2 * count + 2 * k + 1]
        sums = [own_ref[:, j].astype(F32) + got_ref[:, j].astype(F32) for j in range(2)]
        low = me_ref[bit] == 0
        keep_ref[...] = jnp.where(low, sums[0], sums[1]).astype(BF16)
        send_ref[...] = jnp.where(low, sums[1], sums[0]).astype(BF16)


def merge(me, items, deps=()):
    ins, outs, bits = [], [], []
    for own, got, bit, inner in items:
        blocks, rows, width = own.shape
        outer = blocks // (2 * inner)
        ins += [v.reshape(outer, 2, inner, rows, width) for v in (own, got)]
        outs += [sds((outer, inner, rows, width), BF16)] * 2
        bits.append(bit)
    done = local(functools.partial(merge_kernel, tuple(bits)), "merge", me, ins, outs, deps)
    return [v.reshape((v.shape[0] * v.shape[1],) + v.shape[2:]) for v in done]


def last_kernel(me_ref, *refs):
    keep_ref, send_ref = refs[-2:]
    begin = 0
    for k in range(0, len(refs) - 2, 2):
        rows = refs[k].shape[1]
        at = slice(begin, begin + rows)
        for j, out_ref in enumerate((keep_ref, send_ref)):
            block = jnp.bitwise_xor(me_ref[4], j)
            total = refs[k][block].astype(F32) + refs[k + 1][block].astype(F32)
            out_ref[at, :] = total.astype(BF16)
        begin += rows


def last_merge(me, items, deps=()):
    ins = [v for item in items for v in item]
    shape = (sum(one.shape[1] for one, _ in items), ins[0].shape[2])
    return local(last_kernel, "last_merge", me, ins, [sds(shape, BF16)] * 2, deps)


def joint_sum_kernel(count, me_ref, keep_ref, far_ref, *refs):
    outs = refs[count:]
    width = keep_ref.shape[2]
    vec = refs[0][...]
    for k in range(1, count):
        vec = vec + refs[k][...]
    vec = jnp.concatenate([vec, jnp.zeros((120, D), F32)], axis=0).T
    vec = vec.reshape(len(outs), 2, CORES, SUB, 128)
    mine = jnp.where(me_ref[1] == 0, vec[:, 0], vec[:, 1])
    mine = jnp.where(me_ref[0] == 0, mine[:, 0], mine[:, 1]).astype(BF16)
    for k in range(len(outs)):
        at = jnp.bitwise_xor(me_ref[6], k)
        total = keep_ref[at].astype(F32) + far_ref[at].astype(F32)
        outs[k][:, :width] = total.astype(BF16)
    for j in range(len(outs)):
        for k in range(len(outs)):
            @pl.when(me_ref[6] == j ^ k)
            def _(j=j, k=k):
                outs[k][:, width:] = mine[j]


def joint_sum(me, keep, far, vecs, deps=()):
    shape = (keep.shape[1], keep.shape[2] + 128)
    kernel = functools.partial(joint_sum_kernel, len(vecs))
    outs = [sds(shape, BF16)] * keep.shape[0]
    return local(kernel, "joint_sum", me, [keep, far] + list(vecs), outs, deps)


def inputs_kernel(x_ref, dqkv_ref, dz1_ref, part_ref, vec_ref, dvec_ref, w_ref, wa_ref, dx_ref, out_ref, acc_ref):
    step = pl.program_id(0)

    @pl.when(step == 0)
    def _():
        acc_ref[...] = dvec_ref[...]

    unit, scale = normed(x_ref[...].astype(F32))
    da1 = dot_nt(dz1_ref[...], wa_ref[...])
    for j in range(3):
        da1 = da1 + dot_nt(dqkv_ref[j], w_ref[:, D * j : D * (j + 1)])
    dx_ref[...] = part_ref[...] + norm_back(da1, unit, scale, vec_ref[0:1, :])
    acc_ref[0:1, :] += jnp.sum(da1 * unit, axis=0, keepdims=True)
    acc_ref[1:2, :] += jnp.sum(da1, axis=0, keepdims=True)

    @pl.when(step == pl.num_programs(0) - 1)
    def _():
        out_ref[...] = acc_ref[...]


def inputs(x, dqkv, dz1, part, vec, dvec, w, wa, rows=512, deps=()):
    t = x.shape[0]
    row = pl.BlockSpec((rows, D), lambda i: (i, 0))
    shape = (8, D)
    return launch(
        inputs_kernel,
        "inputs",
        [
            (x, row),
            (dqkv, pl.BlockSpec((3, rows, D), lambda i: (0, i, 0))),
            (dz1, row),
            (part, row),
            (vec, full((8, D))),
            (dvec, full((8, D))),
            (w, full(w.shape)),
            (wa, full(wa.shape)),
        ],
        [(sds((t, D), F32), row), (sds(shape, F32), full(shape, False))],
        grid=(t // rows,),
        scratch=[pltpu.VMEM((8, D), F32)],
        price=cost(2 * t * D * 4 * D, 12),
        deps=deps,
    )


def collect_kernel(counts, *refs):
    total = jnp.float32(0.0)
    begin = 0
    outs = refs[sum(counts) :]
    for k, count in enumerate(counts):
        parts = refs[begin : begin + count]
        begin += count
        if count == 1:
            value = jnp.sum(parts[0][...].astype(F32), axis=0)
        else:
            value = sum(p[...].astype(F32) for p in parts)
        outs[k][...] = value
        total = total + jnp.sum(value * value)
    outs[-1][...] = jnp.full(outs[-1].shape, total, F32)


def collect(groups, n):
    shapes = [g[0].shape[1:] if len(g) == 1 else g[0].shape for g in groups]
    return pl.pallas_call(
        functools.partial(collect_kernel, tuple(len(g) for g in groups)),
        out_shape=[sds(s, F32) for s in shapes] + [sds((n, 8, 128), F32)],
        compiler_params=params(16),
        cost_estimate=cost(MIB, 3),
        name="collect",
    )(*[v for g in groups for v in g])


RATES = (D ** (-0.5), (D // 16) ** (-0.5), D ** (-0.5), D ** (-0.5), FF ** (-0.5), D ** (-0.5), 0.5)


def update(grad, master, moment, square, clip, rate):
    clipped = grad * clip
    new_moment = 0.5 * moment + 0.5 * clipped
    new_square = 0.5 * square + 0.5 * clipped * clipped
    fix = 1.0 - 0.5**STEP
    stepped = new_moment / fix / (jnp.sqrt(new_square / fix) + 1e-08)
    return (master - rate * (stepped + 0.01 * master), new_moment, new_square)


def adam_kernel(*refs):
    down_ref, joint_ref, sq_ref = refs[:3]
    state = refs[3:24]
    norm_ref = refs[24]
    outs = refs[25:]
    sub = joint_ref.shape[0]
    norm = jnp.sqrt(jnp.sum(sq_ref[...], axis=0)[0:1, 0:1])
    norm_ref[...] = jnp.broadcast_to(norm, norm_ref.shape)
    clip = jnp.minimum(1.0, 1.0 / (norm + 1e-06))

    def piece(index, grad, at):
        old = [state[3 * index + k][at] for k in range(3)]
        new = update(grad, *old, clip, RATES[index])
        for k in range(3):
            outs[3 * index + k][at] = new[k]

    every = slice(None)
    piece(0, joint_ref[:, : 3 * D], (every, every))
    turned_vec = jnp.concatenate([joint_ref[:, 3 * D :], jnp.zeros((128 - sub, 128), F32)], axis=0).T
    piece(6, turned_vec[0:6, 0:sub], (every, every))

    def down(j, count=1):
        return down_ref[sub * j : sub * (j + count), :]

    up = jnp.concatenate([down(j) for j in range(COLS)], axis=1)
    step = FF // OWNERS
    order = [up[:, FF // CORES * c + step * p :][:, :step] for p in range(OWNERS // CORES) for c in range(CORES)]
    piece(3, jnp.concatenate(order, axis=1), (every, every))
    piece(4, down(COLS, COLS), (every, every))
    piece(5, down(2 * COLS), (every, every))
    piece(1, down(2 * COLS + 1), (every, every))
    piece(2, down(2 * COLS + 2), (every, every))


def adam(grads, squares, state):
    return pl.pallas_call(
        adam_kernel,
        out_shape=[sds((1, 128), F32)] + [sds(s.shape, F32) for s in state],
        compiler_params=params(24),
        cost_estimate=cost(4 * MIB, 4),
        name="adam",
    )(*grads, squares, *state)


def ordered(up):
    rows = up.shape[0]
    return up.reshape(rows, OWNERS // CORES, CORES, FF // OWNERS).swapaxes(1, 2).reshape(rows, FF)


def turn_norms(state):
    return tuple(state[:18]) + tuple(s.T for s in state[18:])


def column_blocks(w):
    return [w[..., D * j : D * (j + 1)] for j in range(w.shape[-1] // D)]


def pack_kernel(qkv_ref, attn_ref, gate_ref, up_ref, down_ref, fgate_ref, norms_ref, one_ref, rest_ref):
    sub = qkv_ref.shape[0]
    norms = jnp.concatenate([norms_ref[...], jnp.zeros((128 - norms_ref.shape[0], sub), F32)], axis=0)
    norms = jnp.concatenate([norms, jnp.zeros((128, 128 - sub), F32)], axis=1).T[0:sub]
    one = jnp.concatenate([qkv_ref[...], norms], axis=1).astype(BF16)
    one_ref[...] = one
    for j, ref in enumerate((attn_ref, gate_ref, fgate_ref)):
        rest_ref[0, sub * j : sub * (j + 1), :] = ref[...].astype(BF16)
    step = FF // OWNERS
    up = up_ref[...]
    order = [up[:, step * (CORES * p + c) :][:, :step] for c in range(CORES) for p in range(OWNERS // CORES)]
    up = jnp.concatenate(order, axis=1).astype(BF16)
    for j in range(COLS):
        rest_ref[0, sub * (3 + j) : sub * (4 + j), :] = up[:, D * j : D * (j + 1)]
    rest_ref[0, sub * (3 + COLS) :, :] = down_ref[...].astype(BF16)


def pack(masters):
    sub = masters[0].shape[0]
    ins = [(hbm(v), full(v.shape)) for v in [*masters[:6], masters[6].T]]
    shapes = [(sub, 3 * D + 128), (1, (3 + 2 * COLS) * sub, D)]
    outs = [(sds(s, BF16), full(s, False)) for s in shapes]
    return launch(pack_kernel, "pack", ins, outs, grid=(1,), price=cost(MIB, 3))


def stack_kernel(me_ref, *refs):
    for k, ref in enumerate(refs[:-1]):
        refs[-1][k] = ref[...]


def stack(me, values, deps):
    return local(stack_kernel, "stack", me, values, [sds((len(values),) + values[0].shape, BF16)], deps)[0]


def join_kernel(cuts, me_ref, *refs):
    outs = refs[len(refs) - len(cuts) :]
    for k, (item, first, rows) in enumerate(cuts):
        for j in range(2):
            half = refs[2 * item + j]
            n = half.shape[0]
            outs[k][n * j : n * (j + 1)] = half[:, first : first + rows, :]


def join(me, items, cuts, deps=()):
    ins = [v for item in items for v in item]
    outs = [sds((2 * items[i][0].shape[0], rows, items[i][0].shape[2]), BF16) for i, _, rows in cuts]
    return local(functools.partial(join_kernel, tuple(cuts)), "join", me, ins, outs, deps)


def pack_whole(weights):
    qkv, attn, gate, up, down, fgate, norms = weights
    one = jnp.concatenate([qkv, jnp.pad(norms, ((0, 0), (0, 128 - norms.shape[1])))], axis=1)
    rest = [attn, gate, fgate] + column_blocks(ordered(up))
    rest = [p.reshape(OWNERS, SUB, D) for p in rest] + [down.reshape(OWNERS, COLS * SUB, D)]
    return one.reshape(OWNERS, SUB, one.shape[1]), jnp.concatenate(rest, axis=1)


def unpack_whole(one, two, three, joint, vec):
    def blocks(g, start, count):
        parts = [g[:, SUB * j : SUB * (j + 1), :].reshape(D, D) for j in range(start, start + count)]
        return jnp.concatenate(parts, axis=1)

    up = blocks(one, 0, COLS).reshape(D, CORES, OWNERS // CORES, FF // OWNERS)
    return (
        joint.reshape(D, 3 * D),
        blocks(three, 1, 1),
        blocks(three, 2, 1),
        up.swapaxes(1, 2).reshape(D, FF),
        two.reshape(FF, D),
        blocks(three, 0, 1),
        vec[:6].T,
    )


def swap(value, axis, size, bit):
    return lax.ppermute(value, axis, [(i, i ^ bit) for i in range(size)])


def body(nd, nf, tokens, cotangent, halves, *state):
    n = nd * nf
    if n == OWNERS and nf == 2 * CORES:
        return direct(nd, nf, tokens, cotangent, halves, *state)
    return general(n, tokens, cotangent, halves, *state)


def direct(nd, nf, tokens, cotangent, halves, *state):
    both = ("dp", "fsdp")
    nx = nf // CORES
    f = lax.axis_index("fsdp").astype(jnp.int32)
    d = lax.axis_index("dp").astype(jnp.int32)
    me = jnp.stack([f % 2, f // 2, d % 2, (d // 2) % 2, d // 4, d * nf + f, d])

    def to(v, bit):
        axis, size, step = (("fsdp", nf, 1), ("fsdp", nf, 2), ("dp", nd, 1), ("dp", nd, 2), ("dp", nd, 4))[bit]
        return swap(v, axis, size, step)

    one, rest = pack(state[0::3])
    rest_z = to(rest, 4)
    own = stack(me, [one] + [swap(one, "dp", nd, k) for k in range(1, nd)], (rest_z,))
    (rest,) = join(me, [(rest, rest_z)], [(0, 0, ROWS)])
    rest_z = to(rest, 3)
    far = to(own, 1)
    parts = [own, to(own, 0), far, to(far, 0)]
    first, second = join(me, [(rest, rest_z)], [(0, 0, CUT), (0, CUT, ROWS - CUT)])
    got = to(first, 2), to(second, 1)
    a1t, a1, qkv, vec, w = project(me, tokens, parts)
    first, second = join(me, [(first, got[0]), (second, got[1])], [(0, 0, CUT), (1, 0, ROWS - CUT)], (a1t,))
    got = to(first, 1), to(second, 2)
    o, ot, lse = attend(halves, qkv, (first,))
    first, second = join(me, [(first, got[0]), (second, got[1])], [(0, 0, CUT), (1, 0, ROWS - CUT)], (o,))
    sources = []
    for value, bits, row in ((first, (16, 8, 4, 2), 0), (second, (16, 8, 2, 4), CUT)):
        owners = [0]
        for bit in bits:
            owners = owners + [k + bit for k in owners]
        sources += [(value, row, owners), (to(value, 0), row, [k + 1 for k in owners])]
    y, part, dz1, do, dvec, wa, *terms = middle(me, tokens, a1, o, cotangent, vec, sources, a1t, ot)
    orders = ((1, 2, 3), (2, 3, 1), (3, 2, 1))
    inner = ((1, 1, 1), (nx, nx, 1), (2 * nx, nx, 1))
    own, arrived = terms[0::2], [to(v, 0) for v in terms[1::2]]

    def stage(k, own, arrived, deps, more=()):
        items = [(own[i], arrived[i], orders[i][k], inner[i][k]) for i in range(3)]
        done = merge(me, items + list(more), deps)
        own, out = done[0::2], done[1::2]
        bits = [orders[i][k] for i in range(3)] + [item[2] for item in more]
        return own, [to(v, bit) for v, bit in zip(out, bits)]

    head = attend_back_first(halves, qkv, o, do, lse, 1)
    own, arrived = stage(0, own, arrived, (head,))
    dqkv = attend_back_rest(halves, qkv, o, do, lse, head, 1, deps=(own[0],))
    own3, other3 = joint_grads(me, a1t, dqkv, deps=tuple(arrived))
    own, arrived = stage(1, own, arrived, (), [(own3, to(other3, 0), 1, 1)])
    keep3, far3 = own.pop(), arrived.pop()
    dx, dvec = inputs(tokens, dqkv, dz1, part, vec, dvec, w, wa, deps=(own[0],))
    vecs = [dvec] + [swap(dvec, "fsdp", nf, k) for k in range(1, nf)]
    own, arrived = stage(2, own, arrived, (dvec,))
    keep, send = last_merge(me, list(zip(own, arrived)))
    in1 = [keep, to(send, 4)]
    out3 = joint_sum(me, keep3, far3, vecs, deps=(keep,))
    in3 = [out3[0]] + [swap(v, "dp", nd, k) for k, v in enumerate(out3) if k]

    *grads, squares = collect([in1, in3], nd * nf)
    squares = lax.all_to_all(squares, both, 0, 0, tiled=True)
    norm, *new = adam(grads, squares, turn_norms(state))
    return (y, dx, norm[0, 0], *turn_norms(new))


def layer_general(me, tokens, cotangent, halves, one, rest):
    a1t, a1, qkv, vec, w = project(me, tokens, [one])
    o, ot, lse = attend(halves, qkv)
    sources = [(rest, 0, range(OWNERS))]
    y, part, dz1, do, dvec, wa, *terms = middle(me, tokens, a1, o, cotangent, vec, sources, a1t, ot)
    head = attend_back_first(halves, qkv, o, do, lse, 1)
    dqkv = attend_back_rest(halves, qkv, o, do, lse, head, 1)
    terms += joint_grads(me, a1t, dqkv)
    dx, dvec = inputs(tokens, dqkv, dz1, part, vec, dvec, w, wa)
    terms = [
        jnp.stack([own, other], axis=1).reshape((OWNERS,) + own.shape[1:]).astype(F32)
        for own, other in zip(terms[0::2], terms[1::2])
    ]
    return (y, dx) + unpack_whole(*terms, dvec)


def general(n, tokens, cotangent, halves, *state):
    both = ("dp", "fsdp")
    rounded = [m.astype(BF16) for m in state[0::3]]
    packed = pack_whole([lax.all_gather(w, both, axis=0, tiled=True) for w in rounded])
    me = jnp.zeros((7,), jnp.int32)
    y, dx, *terms = layer_general(me, tokens, cotangent, halves, *packed)
    q, wo, wa, wu, wd, wf, nv = [
        lax.psum_scatter(t, both, scatter_dimension=0, tiled=True) for t in terms
    ]
    got = [
        jnp.concatenate(column_blocks(ordered(wu)) + [wd, wf, wo, wa], axis=0),
        jnp.concatenate([q, jnp.pad(nv, ((0, 0), (0, 128 - nv.shape[1])))], axis=1),
    ]
    *grads, squares = collect([[g[None]] for g in got], n)
    squares = lax.all_to_all(squares, both, 0, 0, tiled=True)
    norm, *new = adam(grads, squares, turn_norms(state))
    return (y, dx, norm[0, 0], *turn_norms(new))


def solution(mesh):
    rows = P(("dp", "fsdp"), None)
    nd, nf = mesh.shape["dp"], mesh.shape["fsdp"]
    return jax.shard_map(
        functools.partial(body, nd, nf),
        mesh=mesh,
        in_specs=(rows, rows, P(("dp", "fsdp"))) + (rows,) * 21,
        out_specs=(rows, rows, P()) + (rows,) * 21,
        check_vma=False,
    )
```

```python
import functools
import jax
import jax.numpy as jnp
from jax import lax
from jax.experimental import pallas as pl
from jax.experimental.pallas import tpu as pltpu
from jax.sharding import PartitionSpec as P

D = 512
H = 8
HD = 64
FF = 2048
STEP = 5
PAIRS = H // 2
SUB = 16
OWNERS = D // SUB
COLS = FF // D
F32 = jnp.float32
BF16 = jnp.bfloat16
MIB = 1024 * 1024
CORES = 2


def params(mib):
    return pltpu.CompilerParams(vmem_limit_bytes=mib * MIB)


def cost(flops, mib, trans=0):
    return pl.CostEstimate(flops=flops, bytes_accessed=int(mib * MIB), transcendentals=trans)


def dot(a, b):
    return lax.dot_general(a, b, (((1,), (0,)), ((), ())), preferred_element_type=F32)


def dot_nt(a, b):
    return lax.dot_general(a, b, (((1,), (1,)), ((), ())), preferred_element_type=F32)


def normed(values):
    center = values - jnp.mean(values, axis=-1, keepdims=True)
    scale = lax.rsqrt(jnp.mean(center * center, axis=-1, keepdims=True) + 1e-05)
    return center * scale, scale


def norm_back(grad, unit, scale, gain):
    inner = grad * gain
    first = jnp.mean(inner, axis=-1, keepdims=True)
    second = jnp.mean(inner * unit, axis=-1, keepdims=True)
    return scale * (inner - first - unit * second)


def full(shape, once=True):
    zeros = (0,) * len(shape)
    if once:
        return pl.BlockSpec(shape, lambda *_: zeros, pipeline_mode=pl.Buffered(1))
    return pl.BlockSpec(shape, lambda *_: zeros)


def turned(values):
    return values.T.reshape(OWNERS // CORES, CORES, SUB, values.shape[0])


def sds(shape, dtype):
    return jax.ShapeDtypeStruct(shape, dtype)


def hbm(value):
    return pltpu.with_memory_space_constraint(value, pltpu.HBM)


def launch(kernel, name, ins, outs, grid, scratch=(), price=None, deps=(), scalars=0, aliases=None, room=24):
    count = len(ins)

    def wrapped(*refs):
        kernel(*refs[:count], *refs[count + len(deps) :])

    in_specs = [s for _, s in ins[scalars:]] + [pl.BlockSpec(memory_space=pl.ANY)] * len(deps)
    return pl.pallas_call(
        wrapped if deps else kernel,
        grid_spec=pltpu.PrefetchScalarGridSpec(
            num_scalar_prefetch=scalars,
            grid=grid,
            in_specs=in_specs,
            out_specs=[s for _, s in outs],
            scratch_shapes=list(scratch),
        ),
        out_shape=[o for o, _ in outs],
        input_output_aliases=aliases or {},
        compiler_params=params(room),
        cost_estimate=price,
        name=name,
    )(*[a for a, _ in ins], *deps)


def local(kernel, name, me, ins, outs, deps=()):
    count = 1 + len(ins)

    def wrapped(*refs):
        kernel(*refs[:count], *refs[count + len(deps) :])

    vmem = pl.BlockSpec(memory_space=pltpu.VMEM)
    return pl.pallas_call(
        wrapped,
        in_specs=[pl.BlockSpec(memory_space=pltpu.SMEM)] + [vmem] * len(ins) + [pl.BlockSpec(memory_space=pl.ANY)] * len(deps),
        out_specs=[vmem] * len(outs),
        out_shape=outs,
        compiler_params=params(16),
        cost_estimate=cost(MIB, 4),
        name=name,
    )(me, *ins, *deps)


def project_kernel(places, me_ref, x_ref, *refs):
    parts = refs[:-5]
    a1t_ref, a_ref, qkv_ref, vec_ref, w_ref = refs[-5:]

    @pl.when(pl.program_id(0) == 0)
    def _():
        for part, distances in zip(parts, places):
            for k, distance in enumerate(distances):
                owner = jnp.bitwise_xor(me_ref[5], distance)
                w_ref[pl.ds(pl.multiple_of(owner * SUB, SUB), SUB), :] = part[k]
        vec_ref[...] = w_ref[:, 3 * D : 3 * D + 128].astype(F32).T[0:8, :]

    unit, _ = normed(x_ref[...].astype(F32))
    a1 = (unit * vec_ref[0:1, :] + vec_ref[1:2, :]).astype(BF16)
    a_ref[...] = a1
    a1t_ref[...] = turned(a1)
    for j in range(3):
        qkv_ref[j] = dot(a1, w_ref[:, j * D : (j + 1) * D]).astype(BF16)


def project(me, x, parts, rows=512):
    t = x.shape[0]
    width = parts[0][0].shape[-1]
    places = tuple(tuple(distances) for _, distances in parts)
    row = pl.BlockSpec((rows, D), lambda i, *_: (i, 0))
    pairs = OWNERS // CORES
    return launch(
        functools.partial(project_kernel, places),
        "project",
        [(me, None), (x, row)] + [(p, full(p.shape)) for p, _ in parts],
        [
            (sds((pairs, CORES, SUB, t), BF16), pl.BlockSpec((pairs, CORES, SUB, rows), lambda i, *_: (0, 0, 0, i))),
            (sds((t, D), BF16), row),
            (sds((3, t, D), BF16), pl.BlockSpec((3, rows, D), lambda i, *_: (0, i, 0))),
            (sds((8, D), F32), full((8, D), False)),
            (sds((D, width), BF16), full((D, width), False)),
        ],
        grid=(t // rows,),
        price=cost(2 * t * D * 3 * D, 9),
        scalars=1,
    )


def by_head(values):
    lane = lax.broadcasted_iota(jnp.int32, values.shape, 1)
    zero = jnp.zeros_like(values)
    return jnp.concatenate(
        [jnp.where(lane < HD, values, zero), jnp.where(lane >= HD, values, zero)], axis=0
    )


def own_blocks(values, blk):
    return jnp.concatenate([values[:HD, :blk], values[HD:, blk:]], axis=0)


def diagonal(blk):
    row = lax.broadcasted_iota(jnp.int32, (blk, 2 * blk), 0)
    col = lax.broadcasted_iota(jnp.int32, (blk, 2 * blk), 1)
    return row <= jnp.where(col >= blk, col - blk, col)


def over_blocks(halves_ref, per, front, back):
    def path(firsts):
        ready = front(0, firsts[0])
        for i in range(per):
            later = front(i + 1, firsts[i + 1]) if i + 1 < per else None
            back(i, firsts[i], ready)
            ready = later

    @pl.when(halves_ref[0] == 0)
    def _():
        path([0] * per)

    @pl.when(halves_ref[0] != 0)
    def _():
        path([0] * (per // 2) + [per // 2] * (per // 2))


FORWARD_BLOCK = 512
BACK_BLOCK = 128


def attend_kernel(halves_ref, qkv_ref, o_ref, ot_ref, lse_ref, vt_ref):
    q_ref, k_ref, v_ref = (qkv_ref.at[j] for j in range(3))
    blk = FORWARD_BLOCK
    vt_ref[...] = v_ref[...].T
    allowed = diagonal(blk)

    def front(i, first):
        queries = by_head(q_ref[i * blk : (i + 1) * blk, :] * jnp.bfloat16(0.125))
        return dot_nt(k_ref[first * blk : (i + 1) * blk, :], queries)

    def back(i, first, st):
        rows = slice(i * blk, (i + 1) * blk)
        n = (i - first) * blk
        last = jnp.where(allowed, st[n:, :], -1e30)
        top = jnp.max(last, axis=0, keepdims=True)
        if n:
            top = jnp.maximum(top, jnp.max(st[:n, :], axis=0, keepdims=True))
        expo = jnp.exp(last - top)
        total = jnp.sum(expo, axis=0, keepdims=True)
        expo = expo.astype(BF16)
        if n:
            rest = jnp.exp(st[:n, :] - top)
            total = total + jnp.sum(rest, axis=0, keepdims=True)
            expo = jnp.concatenate([rest.astype(BF16), expo], axis=0)
        out = dot(vt_ref[:, first * blk : (i + 1) * blk], expo) * (1.0 / total)
        out = own_blocks(out, blk).astype(BF16)
        lse = top + jnp.log(total)
        lse_ref[0, 0:1, rows] = lse[:, :blk]
        lse_ref[0, 1:2, rows] = lse[:, blk:]
        ot_ref[:, :, :, rows] = out.reshape(128 // SUB // CORES, CORES, SUB, blk)
        o_ref[rows, :] = out.T

    over_blocks(halves_ref, q_ref.shape[0] // blk, front, back)


def attend(halves, qkv, deps=()):
    t = qkv.shape[1]
    pairs = OWNERS // CORES
    part = 128 // SUB // CORES
    return launch(
        attend_kernel,
        "attend",
        [
            (halves, None),
            (qkv, pl.BlockSpec((3, t, 128), lambda p, *_: (0, 0, p))),
        ],
        [
            (sds((t, D), BF16), pl.BlockSpec((t, 128), lambda p, *_: (0, p))),
            (sds((pairs, CORES, SUB, t), BF16), pl.BlockSpec((part, CORES, SUB, t), lambda p, *_: (p, 0, 0, 0))),
            (sds((PAIRS, 2, t), F32), pl.BlockSpec((1, 2, t), lambda p, *_: (p, 0, 0))),
        ],
        grid=(PAIRS,),
        scratch=[pltpu.VMEM((128, t), BF16)],
        price=cost(4 * t * t * D, 8, t * t * H),
        scalars=1,
        deps=deps,
    )


def attend_back_kernel(halves_ref, qkv_ref, o_ref, do_ref, lse_ref, dqkv_ref, kt_ref, dk_ref, dv_ref):
    q_ref, k_ref, v_ref = (qkv_ref.at[j] for j in range(3))
    blk = BACK_BLOCK
    kt_ref[...] = k_ref[...].T
    prod = (do_ref[...].astype(F32) * o_ref[...].astype(F32)).T
    delta = [jnp.sum(prod[h * HD : (h + 1) * HD, :], axis=0, keepdims=True) for h in range(2)]
    allowed = diagonal(blk)

    def front(i, first):
        rows, keys = slice(i * blk, (i + 1) * blk), slice(first * blk, (i + 1) * blk)
        queries = by_head(q_ref[rows, :] * jnp.bfloat16(0.125))
        grads = by_head(do_ref[rows, :])
        return queries, grads, dot_nt(k_ref[keys, :], queries), dot_nt(v_ref[keys, :], grads)

    def gather(ref, first, i, value):
        n = (i - first) * blk
        if n:
            ref[first * blk : i * blk, :] += value[:n]
        ref[i * blk : (i + 1) * blk, :] = value[n:]

    def back(i, first, ready):
        queries, grads, st, dpt = ready
        rows, keys = slice(i * blk, (i + 1) * blk), slice(first * blk, (i + 1) * blk)
        n = (i - first) * blk
        lse = jnp.concatenate([lse_ref[0, 0:1, rows], lse_ref[0, 1:2, rows]], axis=1)
        rowsum = jnp.concatenate([d[:, rows] for d in delta], axis=1)
        pt = jnp.where(allowed, jnp.exp(st[n:, :] - lse), 0.0)
        if n:
            pt = jnp.concatenate([jnp.exp(st[:n, :] - lse), pt], axis=0)
        dst = (pt * (dpt - rowsum)).astype(BF16)
        gather(dv_ref, first, i, dot(pt.astype(BF16), grads))
        gather(dk_ref, first, i, dot(dst, queries))
        dqt = dot(kt_ref[:, keys], dst) * 0.125
        dqkv_ref[0, rows, :] = own_blocks(dqt, blk).T.astype(BF16)

    over_blocks(halves_ref, q_ref.shape[0] // blk, front, back)
    dqkv_ref[1] = dk_ref[...].astype(BF16)
    dqkv_ref[2] = dv_ref[...].astype(BF16)


def attend_back_first(halves, qkv, o, do, lse, count):
    t = qkv.shape[1]
    col = pl.BlockSpec((t, 128), lambda p, *_: (0, p))
    three = pl.BlockSpec((3, t, 128), lambda p, *_: (0, 0, p))
    return launch(
        attend_back_kernel,
        "attend_back_first",
        [(halves, None), (hbm(qkv), three), (hbm(o), col), (hbm(do), col), (lse, pl.BlockSpec((1, 2, t), lambda p, *_: (p, 0, 0)))],
        [(sds((3, t, D), BF16), three)],
        grid=(count,),
        scratch=[pltpu.VMEM((128, t), BF16)] + [pltpu.VMEM((t, 128), F32)] * 2,
        price=cost(10 * t * t * 128 * count, 2.5 * count, t * t * 2 * count),
        scalars=1,
    )[0]


def attend_back_rest(halves, qkv, o, do, lse, into, first, deps=()):
    t = qkv.shape[1]
    col = pl.BlockSpec((t, 128), lambda p, *_: (0, first + p))
    three = pl.BlockSpec((3, t, 128), lambda p, *_: (0, 0, first + p))
    count = PAIRS - first
    return launch(
        attend_back_kernel,
        "attend_back_rest",
        [(halves, None), (hbm(qkv), three), (hbm(o), col), (hbm(do), col), (lse, pl.BlockSpec((1, 2, t), lambda p, *_: (first + p, 0, 0)))],
        [(sds((3, t, D), BF16), three)],
        grid=(count,),
        scratch=[pltpu.VMEM((128, t), BF16)] + [pltpu.VMEM((t, 128), F32)] * 2,
        price=cost(10 * t * t * 128 * count, 2.5 * count, t * t * 2 * count),
        scalars=1,
        deps=(into,) + tuple(deps),
        aliases={5: 0},
    )[0]


def joint_kernel(me_ref, a1t_ref, dqkv_ref, own_ref, other_ref):
    t = dqkv_ref.shape[1]
    split_cores(me_ref, dot(a1t_ref[...].reshape(D, t), dqkv_ref[0]), own_ref, other_ref)


def joint_grads(me, a1t, dqkv, deps=()):
    t = dqkv.shape[1]
    pairs = OWNERS // CORES
    out = (sds((pairs, SUB, 3 * D), BF16), pl.BlockSpec((pairs, SUB, D), lambda i, *_: (0, 0, i)))
    return launch(
        joint_kernel,
        "joint_grads",
        [(me, None), (a1t, full(a1t.shape)), (dqkv, pl.BlockSpec((1, t, D), lambda i, *_: (i, 0, 0)))],
        [out, out],
        grid=(3,),
        price=cost(2 * t * D * 3 * D, 6),
        scalars=1,
        deps=deps,
    )


NEAR = 3 * SUB
ROWS = NEAR + 2 * COLS * SUB
WIDE = COLS * SUB


def near_weight(ref, j):
    return ref[:, SUB * j : SUB * (j + 1), :].reshape(D, D)


def block_of(ref, j):
    return near_weight(ref, 3 + j)


def lower(ref, j):
    halfway = COLS // CORES
    core, part = j // halfway, j % halfway
    per = OWNERS // CORES // halfway
    rows = [ref[CORES * p + core, NEAR + COLS * SUB : ROWS, :] for p in range(per * part, per * (part + 1))]
    return jnp.concatenate(rows, axis=0)


def middle_rows(x_ref, a1_ref, o_ref, dy_ref, vec_ref, w_ref, y_ref, part_ref, dz1o_ref, do_ref, dvec_ref,
                a2t_ref, et_ref, df_ref, du_ref, dz2_ref, dz1_ref, datt_ref, step, late):
    rows = x_ref.shape[0]
    here = pl.ds(pl.multiple_of(step * rows, rows), rows)
    c1, g2, b2, c2 = (vec_ref[k : k + 1, :] for k in (2, 3, 4, 5))
    x = x_ref[...].astype(F32)
    att = dot(o_ref[...], near_weight(w_ref, 0))
    t1 = jax.nn.sigmoid(dot(a1_ref[...], near_weight(w_ref, 1)) + c1)
    h1 = t1 * att + (1.0 - t1) * x
    unit, scale = normed(h1)
    a2 = (unit * g2 + b2).astype(BF16)
    a2t_ref[:, :, :, here] = turned(a2)
    t2 = jax.nn.sigmoid(dot(a2, near_weight(w_ref, 2)) + c2)
    late()
    f = None
    slopes = []
    kc = 0.7978845608028654
    for j in range(COLS):
        u = dot(a2, block_of(w_ref, j))
        sq = u * u
        half = 0.5 * jnp.tanh(u * (kc + (kc * 0.044715) * sq)) + 0.5
        gel = u * half
        e = gel.astype(BF16)
        slopes.append(half + gel * (1.0 - half) * (2.0 * kc + (6.0 * kc * 0.044715) * sq))
        et_ref[j, :, :, here] = e.T.reshape(et_ref.shape[1:3] + (rows,))
        part = dot(e, lower(w_ref, j))
        f = part if f is None else f + part
    y_ref[...] = (t2 * f + (1.0 - t2) * h1).astype(BF16)
    dy = dy_ref[...].astype(F32)
    dz2 = (dy * (f - h1) * t2 * (1.0 - t2)).astype(BF16)
    df = (dy * t2).astype(BF16)
    dz2_ref[here, :] = dz2
    df_ref[here, :] = df
    da2 = dot_nt(dz2, near_weight(w_ref, 2))
    for j in range(COLS):
        du = (dot_nt(df, lower(w_ref, j)) * slopes[j]).astype(BF16)
        du_ref[j, here, :] = du
        da2 = da2 + dot_nt(du, block_of(w_ref, j))
    dh1 = dy_ref[...].astype(F32) * (1.0 - t2) + norm_back(da2, unit, scale, g2)
    dz1 = (dh1 * (att - x_ref[...].astype(F32)) * t1 * (1.0 - t1)).astype(BF16)
    datt = (dh1 * t1).astype(BF16)
    dz1_ref[here, :] = dz1
    dz1o_ref[...] = dz1
    datt_ref[here, :] = datt
    part_ref[...] = dh1 * (1.0 - t1)
    do_ref[...] = dot_nt(datt, near_weight(w_ref, 0)).astype(BF16)

    def total(v):
        return jnp.sum(v, axis=0, keepdims=True)

    dvec_ref[2:3, :] += total(dz1.astype(F32))
    dvec_ref[3:4, :] += total(da2 * unit)
    dvec_ref[4:5, :] += total(da2)
    dvec_ref[5:6, :] += total(dz2.astype(F32))


def split_cores(me_ref, value, own_ref, other_ref, at=slice(None)):
    value = value.reshape(OWNERS // CORES, CORES, SUB, D)
    low = me_ref[0] == 0
    own_ref[:, at, :] = jnp.where(low, value[:, 0], value[:, 1]).astype(BF16)
    other_ref[:, at, :] = jnp.where(low, value[:, 1], value[:, 0]).astype(BF16)


SETS = (2, 2, 1)


def middle_kernel(plan, *refs):
    count = len(plan)
    me_ref, x_ref, a1_ref, o_ref, dy_ref, vec_ref = refs[:6]
    sources = refs[6 : 6 + count]
    a1t_hbm, ot_hbm = refs[6 + count : 8 + count]
    y_ref, part_ref, dz1o_ref, do_ref, dvec_ref, wa_ref = refs[8 + count : 14 + count]
    own1, other1, own2, other2, own3, other3 = refs[14 + count : 20 + count]
    w_ref, a1t_ref, ot_ref, sem, a2t_ref, et_ref, df_ref, du_ref, dz2_ref, dz1_ref, datt_ref = refs[20 + count :]
    step = pl.program_id(0)
    t = df_ref.shape[0]
    blocks = t // x_ref.shape[0]

    def copies():
        return [
            pltpu.make_async_copy(a1t_hbm, a1t_ref, sem.at[0]),
            pltpu.make_async_copy(ot_hbm, ot_ref, sem.at[1]),
        ]

    def gets(early):
        found, count = [], 2
        for source, (first, rows, distances) in zip(sources, plan):
            for k, distance in enumerate(distances):
                owner = jnp.bitwise_xor(me_ref[5], distance)
                if early == (first < NEAR):
                    to = w_ref.at[owner, first : first + rows, :]
                    found.append(pltpu.make_async_copy(source.at[k], to, sem.at[count]))
                count += 1
        return found

    def late():
        @pl.when(step == 0)
        def _():
            for copy in gets(False):
                copy.wait()

    @pl.when(step == 0)
    def _():
        for copy in gets(True) + gets(False) + copies():
            copy.start()
        dvec_ref[...] = jnp.zeros_like(dvec_ref)
        for copy in gets(True):
            copy.wait()
        wa_ref[...] = near_weight(w_ref, 1)

    @pl.when(step < blocks)
    def _():
        middle_rows(x_ref, a1_ref, o_ref, dy_ref, vec_ref, w_ref, y_ref, part_ref, dz1o_ref, do_ref, dvec_ref,
                    a2t_ref, et_ref, df_ref, du_ref, dz2_ref, dz1_ref, datt_ref, step, late)

    def product(left, right, own_ref, other_ref, j):
        at = slice(SUB * j, SUB * (j + 1))
        split_cores(me_ref, dot(left.reshape(D, t), right), own_ref, other_ref, at)

    each = COLS // SETS[0]
    for k in range(SETS[0]):
        @pl.when(step == blocks + k)
        def _(k=k):
            for j in range(each):
                product(a2t_ref[...], du_ref[each * k + j], own1, other1, j)

    for k in range(SETS[1]):
        @pl.when(step == blocks + SETS[0] + k)
        def _(k=k):
            for j in range(each):
                at = SUB * (each * k + j)
                left = et_ref[:, :, at : at + SUB, :]
                left = left.reshape(CORES, OWNERS // CORES, SUB, t).swapaxes(0, 1)
                product(left, df_ref[...], own2, other2, j)

    @pl.when(step == blocks + SETS[0] + SETS[1])
    def _():
        for copy in copies():
            copy.wait()
        product(a2t_ref[...], dz2_ref[...], own3, other3, 0)
        product(ot_ref[...], datt_ref[...], own3, other3, 1)
        product(a1t_ref[...], dz1_ref[...], own3, other3, 2)


def middle(me, x, a1, o, dy, vec, sources, a1t, ot, rows=512):
    t = x.shape[0]
    blocks = t // rows
    pairs = OWNERS // CORES
    row = pl.BlockSpec((rows, D), lambda i, *_: (jnp.minimum(i, blocks - 1), 0))
    outs = []
    begin = blocks
    for steps, wide in zip(SETS, (COLS, COLS, 3)):
        block = (pairs, SUB * wide // steps, D)
        spec = pl.BlockSpec(block, lambda i, *_, begin=begin, steps=steps: (0, jnp.clip(i - begin, 0, steps - 1), 0))
        outs += [(sds((pairs, SUB * wide, D), BF16), spec)] * 2
        begin += steps
    wide = FF // OWNERS
    plan = tuple((first, v.shape[1], tuple(distances)) for v, first, distances in sources)
    hbm_ref = pl.BlockSpec(memory_space=pl.ANY)
    return launch(
        functools.partial(middle_kernel, plan),
        "middle",
        [(me, None)]
        + [(v, row) for v in (x, a1, o, dy)]
        + [(vec, full(vec.shape))]
        + [(v, hbm_ref) for v, _, _ in sources]
        + [(a1t, hbm_ref), (ot, hbm_ref)],
        [
            (sds((t, D), BF16), row),
            (sds((t, D), F32), row),
            (sds((t, D), BF16), row),
            (sds((t, D), BF16), row),
            (sds((8, D), F32), full((8, D), False)),
            (sds((D, D), BF16), full((D, D), False)),
        ]
        + outs,
        grid=(begin,),
        scratch=[
            pltpu.VMEM((OWNERS, ROWS, D), BF16),
            pltpu.VMEM((pairs, CORES, SUB, t), BF16),
            pltpu.VMEM((pairs, CORES, SUB, t), BF16),
            pltpu.SemaphoreType.DMA((2 + sum(len(p[2]) for p in plan),)),
            pltpu.VMEM((pairs, CORES, SUB, t), BF16),
            pltpu.VMEM((COLS, D // wide, wide, t), BF16),
            pltpu.VMEM((t, D), BF16),
            pltpu.VMEM((COLS, t, D), BF16),
            pltpu.VMEM((t, D), BF16),
            pltpu.VMEM((t, D), BF16),
            pltpu.VMEM((t, D), BF16),
        ],
        price=cost(2 * t * D * (6 * FF + 9 * D), 20, t * FF),
        scalars=1,
        room=60,
    )


def merge_kernel(bits, beside, me_ref, *refs):
    count = len(bits)
    outs = refs[2 * count + beside :]
    for k, bit in enumerate(bits):
        own_ref, got_ref = refs[2 * k], refs[2 * k + 1]
        keep_ref, send_ref = outs[2 * k], outs[2 * k + 1]
        width = own_ref.shape[-1]
        sums = [own_ref[:, j].astype(F32) + got_ref[:, j].astype(F32) for j in range(2)]
        low = me_ref[bit] == 0
        keep_ref[..., :width] = jnp.where(low, sums[0], sums[1]).astype(BF16)
        send_ref[..., :width] = jnp.where(low, sums[1], sums[0]).astype(BF16)
    if beside:
        vec = jnp.sum(refs[2 * count][...], axis=0)
        vec = jnp.concatenate([vec, jnp.zeros((120, D), F32)], axis=0).T
        vec = vec.reshape(OWNERS // (2 * CORES), 2, CORES, SUB, 128)
        vec = jnp.where(me_ref[1] == 0, vec[:, 0], vec[:, 1])
        vec = jnp.where(me_ref[0] == 0, vec[:, 0], vec[:, 1])
        vec = vec.reshape((vec.shape[0] // 2, 2, 1, SUB, 128))
        keep_ref[..., width:] = jnp.where(low, vec[:, 0], vec[:, 1]).astype(BF16)
        send_ref[..., width:] = jnp.where(low, vec[:, 1], vec[:, 0]).astype(BF16)


def merge(me, items, deps=(), vecs=()):
    ins, outs, bits = [], [], []
    for k, (own, got, bit, inner) in enumerate(items):
        blocks, rows, width = own.shape
        outer = blocks // (2 * inner)
        ins += [v.reshape(outer, 2, inner, rows, width) for v in (own, got)]
        width += 128 if vecs and k == len(items) - 1 else 0
        outs += [sds((outer, inner, rows, width), BF16)] * 2
        bits.append(bit)
    kernel = functools.partial(merge_kernel, tuple(bits), len(vecs))
    done = local(kernel, "merge", me, ins + list(vecs), outs, deps)
    return [v.reshape((v.shape[0] * v.shape[1],) + v.shape[2:]) for v in done]


def last_kernel(bit, me_ref, *refs):
    own_ref, got_ref = refs[-6:-4]
    keep_ref, send_ref = refs[-4:-2]
    begin = 0
    for k in range(0, len(refs) - 6, 2):
        rows = refs[k].shape[1]
        at = slice(begin, begin + rows)
        for j, out_ref in enumerate((keep_ref, send_ref)):
            block = jnp.bitwise_xor(me_ref[4], j)
            total = refs[k][block].astype(F32) + refs[k + 1][block].astype(F32)
            out_ref[at, :] = total.astype(BF16)
        begin += rows
    merge_kernel((bit,), 0, me_ref, own_ref, got_ref, *refs[-2:])


def last_merge(me, items, other, bit):
    ins = [v for item in items for v in item]
    outs = [sds((sum(one.shape[1] for one, _ in items), ins[0].shape[2]), BF16)] * 2
    blocks, rows, width = other[0].shape
    ins += [v.reshape(blocks // 2, 2, 1, rows, width) for v in other]
    outs += [sds((blocks // 2, 1, rows, width), BF16)] * 2
    keep, send, keep3, send3 = local(functools.partial(last_kernel, bit), "last_merge", me, ins, outs)
    return keep, send, keep3[:, 0], send3[:, 0]


def inputs_kernel(x_ref, dqkv_ref, dz1_ref, part_ref, vec_ref, dvec_ref, w_ref, wa_ref, dx_ref, out_ref, acc_ref):
    step = pl.program_id(0)

    @pl.when(step == 0)
    def _():
        acc_ref[...] = dvec_ref[...]

    unit, scale = normed(x_ref[...].astype(F32))
    da1 = dot_nt(dz1_ref[...], wa_ref[...])
    for j in range(3):
        da1 = da1 + dot_nt(dqkv_ref[j], w_ref[:, D * j : D * (j + 1)])
    dx_ref[...] = part_ref[...] + norm_back(da1, unit, scale, vec_ref[0:1, :])
    acc_ref[0:1, :] += jnp.sum(da1 * unit, axis=0, keepdims=True)
    acc_ref[1:2, :] += jnp.sum(da1, axis=0, keepdims=True)

    @pl.when(step == pl.num_programs(0) - 1)
    def _():
        out_ref[...] = acc_ref[...]


def inputs(x, dqkv, dz1, part, vec, dvec, w, wa, rows=512, deps=()):
    t = x.shape[0]
    row = pl.BlockSpec((rows, D), lambda i: (i, 0))
    shape = (8, D)
    return launch(
        inputs_kernel,
        "inputs",
        [
            (x, row),
            (dqkv, pl.BlockSpec((3, rows, D), lambda i: (0, i, 0))),
            (dz1, row),
            (part, row),
            (vec, full((8, D))),
            (dvec, full((8, D))),
            (w, full(w.shape)),
            (wa, full(wa.shape)),
        ],
        [(sds((t, D), F32), row), (sds(shape, F32), full(shape, False))],
        grid=(t // rows,),
        scratch=[pltpu.VMEM((8, D), F32)],
        price=cost(2 * t * D * 4 * D, 12),
        deps=deps,
    )


def collect_kernel(counts, *refs):
    total = jnp.float32(0.0)
    begin = 0
    outs = refs[sum(counts) :]
    for k, count in enumerate(counts):
        parts = refs[begin : begin + count]
        begin += count
        if count == 1:
            value = jnp.sum(parts[0][...].astype(F32), axis=0)
        else:
            value = sum(p[...].astype(F32) for p in parts)
        outs[k][...] = value
        total = total + jnp.sum(value * value)
    outs[-1][...] = jnp.full(outs[-1].shape, total, F32)


def collect(groups, n):
    shapes = [g[0].shape[1:] if len(g) == 1 else g[0].shape for g in groups]
    return pl.pallas_call(
        functools.partial(collect_kernel, tuple(len(g) for g in groups)),
        out_shape=[sds(s, F32) for s in shapes] + [sds((n, 8, 128), F32)],
        compiler_params=params(16),
        cost_estimate=cost(MIB, 3),
        name="collect",
    )(*[v for g in groups for v in g])


RATES = (D ** (-0.5), (D // 16) ** (-0.5), D ** (-0.5), D ** (-0.5), FF ** (-0.5), D ** (-0.5), 0.5)


def update(grad, master, moment, square, clip, rate):
    clipped = grad * clip
    new_moment = 0.5 * moment + 0.5 * clipped
    new_square = 0.5 * square + 0.5 * clipped * clipped
    fix = 1.0 - 0.5**STEP
    stepped = new_moment / fix / (jnp.sqrt(new_square / fix) + 1e-08)
    return (master - rate * (stepped + 0.01 * master), new_moment, new_square)


def adam_kernel(*refs):
    down_ref, joint_ref, sq_ref = refs[:3]
    state = refs[3:24]
    norm_ref = refs[24]
    outs = refs[25:]
    sub = joint_ref.shape[0]
    norm = jnp.sqrt(jnp.sum(sq_ref[...], axis=0)[0:1, 0:1])
    norm_ref[...] = jnp.broadcast_to(norm, norm_ref.shape)
    clip = jnp.minimum(1.0, 1.0 / (norm + 1e-06))

    def piece(index, grad, at):
        old = [state[3 * index + k][at] for k in range(3)]
        new = update(grad, *old, clip, RATES[index])
        for k in range(3):
            outs[3 * index + k][at] = new[k]

    every = slice(None)
    piece(0, joint_ref[:, : 3 * D], (every, every))
    turned_vec = jnp.concatenate([joint_ref[:, 3 * D :], jnp.zeros((128 - sub, 128), F32)], axis=0).T
    piece(6, turned_vec[0:6, 0:sub], (every, every))

    def down(j, count=1):
        return down_ref[sub * j : sub * (j + count), :]

    up = jnp.concatenate([down(j) for j in range(COLS)], axis=1)
    step = FF // OWNERS
    order = [up[:, FF // CORES * c + step * p :][:, :step] for p in range(OWNERS // CORES) for c in range(CORES)]
    piece(3, jnp.concatenate(order, axis=1), (every, every))
    piece(4, down(COLS, COLS), (every, every))
    piece(5, down(2 * COLS), (every, every))
    piece(1, down(2 * COLS + 1), (every, every))
    piece(2, down(2 * COLS + 2), (every, every))


def adam(grads, squares, state):
    return pl.pallas_call(
        adam_kernel,
        out_shape=[sds((1, 128), F32)] + [sds(s.shape, F32) for s in state],
        compiler_params=params(24),
        cost_estimate=cost(4 * MIB, 4),
        name="adam",
    )(*grads, squares, *state)


def ordered(up):
    rows = up.shape[0]
    return up.reshape(rows, OWNERS // CORES, CORES, FF // OWNERS).swapaxes(1, 2).reshape(rows, FF)


def turn_norms(state):
    return tuple(state[:18]) + tuple(s.T for s in state[18:])


def column_blocks(w):
    return [w[..., D * j : D * (j + 1)] for j in range(w.shape[-1] // D)]


def pack_kernel(qkv_ref, attn_ref, gate_ref, up_ref, down_ref, fgate_ref, norms_ref, one_ref, near_ref, rest_ref):
    sub = qkv_ref.shape[0]
    norms = jnp.concatenate([norms_ref[...], jnp.zeros((128 - norms_ref.shape[0], sub), F32)], axis=0)
    norms = jnp.concatenate([norms, jnp.zeros((128, 128 - sub), F32)], axis=1).T[0:sub]
    one = jnp.concatenate([qkv_ref[...], norms], axis=1).astype(BF16)
    one_ref[...] = one
    for j, ref in enumerate((attn_ref, gate_ref, fgate_ref)):
        near_ref[0, sub * j : sub * (j + 1), :] = ref[...].astype(BF16)
    step = FF // OWNERS
    up = up_ref[...]
    order = [up[:, step * (CORES * p + c) :][:, :step] for c in range(CORES) for p in range(OWNERS // CORES)]
    up = jnp.concatenate(order, axis=1).astype(BF16)
    for j in range(COLS):
        rest_ref[0, sub * j : sub * (j + 1), :] = up[:, D * j : D * (j + 1)]
    rest_ref[0, sub * COLS :, :] = down_ref[...].astype(BF16)


def pack(masters):
    sub = masters[0].shape[0]
    ins = [(hbm(v), full(v.shape)) for v in [*masters[:6], masters[6].T]]
    shapes = [(sub, 3 * D + 128), (1, 3 * sub, D), (1, 2 * COLS * sub, D)]
    outs = [(sds(s, BF16), full(s, False)) for s in shapes]
    return launch(pack_kernel, "pack", ins, outs, grid=(1,), price=cost(MIB, 3))


def join_kernel(cuts, count, me_ref, *refs):
    outs = refs[len(refs) - len(cuts) - (1 if count else 0) :]
    for k, (item, first, rows) in enumerate(cuts):
        for j in range(2):
            half = refs[2 * item + j]
            n = half.shape[0]
            outs[k][n * j : n * (j + 1)] = half[:, first : first + rows, :]
    for k in range(count):
        outs[-1][k] = refs[len(refs) - len(outs) - count + k][...]


def join(me, items, cuts, deps=(), singles=()):
    ins = [v for item in items for v in item] + list(singles)
    outs = [sds((2 * items[i][0].shape[0], rows, items[i][0].shape[2]), BF16) for i, _, rows in cuts]
    if singles:
        outs.append(sds((len(singles),) + singles[0].shape, BF16))
    return local(functools.partial(join_kernel, tuple(cuts), len(singles)), "join", me, ins, outs, deps)


def pack_whole(weights):
    qkv, attn, gate, up, down, fgate, norms = weights
    one = jnp.concatenate([qkv, jnp.pad(norms, ((0, 0), (0, 128 - norms.shape[1])))], axis=1)
    rest = [attn, gate, fgate] + column_blocks(ordered(up))
    rest = [p.reshape(OWNERS, SUB, D) for p in rest] + [down.reshape(OWNERS, COLS * SUB, D)]
    return one.reshape(OWNERS, SUB, one.shape[1]), jnp.concatenate(rest, axis=1)


def unpack_whole(one, two, three, joint, vec):
    def blocks(g, start, count):
        parts = [g[:, SUB * j : SUB * (j + 1), :].reshape(D, D) for j in range(start, start + count)]
        return jnp.concatenate(parts, axis=1)

    up = blocks(one, 0, COLS).reshape(D, CORES, OWNERS // CORES, FF // OWNERS)
    return (
        joint.reshape(D, 3 * D),
        blocks(three, 1, 1),
        blocks(three, 2, 1),
        up.swapaxes(1, 2).reshape(D, FF),
        two.reshape(FF, D),
        blocks(three, 0, 1),
        vec[:6].T,
    )


def swap(value, axis, size, bit):
    return lax.ppermute(value, axis, [(i, i ^ bit) for i in range(size)])


def body(nd, nf, tokens, cotangent, halves, *state):
    n = nd * nf
    if n == OWNERS and nf == 2 * CORES:
        return direct(nd, nf, tokens, cotangent, halves, *state)
    return general(n, tokens, cotangent, halves, *state)


def direct(nd, nf, tokens, cotangent, halves, *state):
    both = ("dp", "fsdp")
    nx = nf // CORES
    f = lax.axis_index("fsdp").astype(jnp.int32)
    d = lax.axis_index("dp").astype(jnp.int32)
    me = jnp.stack([f % 2, f // 2, d % 2, (d // 2) % 2, d // 4, d * nf + f, d])

    def to(v, bit):
        axis, size, step = (("fsdp", nf, 1), ("fsdp", nf, 2), ("dp", nd, 1), ("dp", nd, 2), ("dp", nd, 4))[bit]
        return swap(v, axis, size, step)

    one, near, rest = pack(state[0::3])
    ones = [one] + [swap(one, "dp", nd, k) for k in range(1, nd)]
    rest, near, own = join(
        me, [(rest, to(rest, 4)), (near, to(near, 1))], [(0, 0, 2 * WIDE), (1, 0, NEAR)], singles=ones
    )
    up, down, near, own = join(
        me,
        [(rest, to(rest, 3)), (near, to(near, 2)), (own, to(own, 1))],
        [(0, 0, WIDE), (0, WIDE, WIDE), (1, 0, NEAR), (2, 0, SUB)],
    )
    got = to(up, 2), to(down, 1), to(near, 4)
    beside = [nf * k + j for j in (0, CORES) for k in range(nd)]
    parts = [(own, beside), (to(own, 0), [k + 1 for k in beside])]
    every = [(0, 0, WIDE), (1, 0, WIDE), (2, 0, NEAR)]
    a1t, a1, qkv, vec, w = project(me, tokens, parts)
    up, down, near = join(me, list(zip((up, down, near), got)), every, (a1t,))
    got = to(up, 1), to(down, 2), to(near, 3)
    o, ot, lse = attend(halves, qkv, (up,))
    up, down, near = join(me, list(zip((up, down, near), got)), every, (o,))
    sources = []
    for value, bits, row in (
        (near, (2, 4, 16, 8), 0),
        (up, (16, 8, 4, 2), NEAR),
        (down, (16, 8, 2, 4), NEAR + WIDE),
    ):
        owners = [0]
        for bit in bits:
            owners = owners + [k + bit for k in owners]
        sources += [(value, row, owners), (to(value, 0), row, [k + 1 for k in owners])]
    y, part, dz1, do, dvec, wa, *terms = middle(me, tokens, a1, o, cotangent, vec, sources, a1t, ot)
    orders = ((1, 2, 3), (2, 3, 1), (3, 2, 1))
    inner = ((1, 1, 1), (nx, nx, 1), (2 * nx, nx, 1))
    own, arrived = terms[0::2], [to(v, 0) for v in terms[1::2]]

    def stage(k, own, arrived, deps, more=(), vecs=()):
        items = [(own[i], arrived[i], orders[i][k], inner[i][k]) for i in range(3)]
        done = merge(me, items + list(more), deps, vecs)
        own, out = done[0::2], done[1::2]
        bits = [orders[i][k] for i in range(3)] + [item[2] for item in more]
        return own, [to(v, bit) for v, bit in zip(out, bits)]

    head = attend_back_first(halves, qkv, o, do, lse, 1)
    own, arrived = stage(0, own, arrived, (head,))
    dqkv = attend_back_rest(halves, qkv, o, do, lse, head, 1, deps=(own[0],))
    own3, other3 = joint_grads(me, a1t, dqkv, deps=tuple(arrived))
    own, arrived = stage(1, own, arrived, (), [(own3, to(other3, 0), 1, 1)])
    dx, dvec = inputs(tokens, dqkv, dz1, part, vec, dvec, w, wa, deps=(own[0],))
    vecs = [lax.all_gather(dvec, "fsdp", axis=0)]
    own, arrived = stage(2, own, arrived, (), [(own.pop(), arrived.pop(), 2, 1)], vecs)
    keep3, far3 = own.pop(), arrived.pop()
    keep, send, keep3, send3 = last_merge(me, list(zip(own, arrived)), (keep3, far3), 3)
    sums = [keep, to(send, 4)]
    keep3, send3 = merge(me, [(keep3, to(send3, 3), 4, 1)])
    far3 = to(send3, 4)

    *grads, squares = collect([sums, [keep3[0], far3[0]]], nd * nf)
    squares = lax.all_to_all(squares, both, 0, 0, tiled=True)
    norm, *new = adam(grads, squares, turn_norms(state))
    return (y, dx, norm[0, 0], *turn_norms(new))


def layer_general(me, tokens, cotangent, halves, one, rest):
    a1t, a1, qkv, vec, w = project(me, tokens, [(one, range(OWNERS))])
    o, ot, lse = attend(halves, qkv)
    sources = [(rest, 0, range(OWNERS))]
    y, part, dz1, do, dvec, wa, *terms = middle(me, tokens, a1, o, cotangent, vec, sources, a1t, ot)
    head = attend_back_first(halves, qkv, o, do, lse, 1)
    dqkv = attend_back_rest(halves, qkv, o, do, lse, head, 1)
    terms += joint_grads(me, a1t, dqkv)
    dx, dvec = inputs(tokens, dqkv, dz1, part, vec, dvec, w, wa)
    terms = [
        jnp.stack([own, other], axis=1).reshape((OWNERS,) + own.shape[1:]).astype(F32)
        for own, other in zip(terms[0::2], terms[1::2])
    ]
    return (y, dx) + unpack_whole(*terms, dvec)


def general(n, tokens, cotangent, halves, *state):
    both = ("dp", "fsdp")
    rounded = [m.astype(BF16) for m in state[0::3]]
    packed = pack_whole([lax.all_gather(w, both, axis=0, tiled=True) for w in rounded])
    me = jnp.zeros((7,), jnp.int32)
    y, dx, *terms = layer_general(me, tokens, cotangent, halves, *packed)
    q, wo, wa, wu, wd, wf, nv = [
        lax.psum_scatter(t, both, scatter_dimension=0, tiled=True) for t in terms
    ]
    got = [
        jnp.concatenate(column_blocks(ordered(wu)) + [wd, wf, wo, wa], axis=0),
        jnp.concatenate([q, jnp.pad(nv, ((0, 0), (0, 128 - nv.shape[1])))], axis=1),
    ]
    *grads, squares = collect([[g[None]] for g in got], n)
    squares = lax.all_to_all(squares, both, 0, 0, tiled=True)
    norm, *new = adam(grads, squares, turn_norms(state))
    return (y, dx, norm[0, 0], *turn_norms(new))


def solution(mesh):
    rows = P(("dp", "fsdp"), None)
    nd, nf = mesh.shape["dp"], mesh.shape["fsdp"]
    return jax.shard_map(
        functools.partial(body, nd, nf),
        mesh=mesh,
        in_specs=(rows, rows, P(("dp", "fsdp"))) + (rows,) * 21,
        out_specs=(rows, rows, P()) + (rows,) * 21,
        check_vma=False,
    )
```

```python
import functools
import jax
import jax.numpy as jnp
from jax import lax
from jax.experimental import pallas as pl
from jax.experimental.pallas import tpu as pltpu
from jax.sharding import PartitionSpec as P

D = 512
H = 8
HD = 64
FF = 2048
STEP = 5
PAIRS = H // 2
SUB = 16
OWNERS = D // SUB
COLS = FF // D
F32 = jnp.float32
BF16 = jnp.bfloat16
MIB = 1024 * 1024
CORES = 2


def params(mib):
    return pltpu.CompilerParams(vmem_limit_bytes=mib * MIB)


def cost(flops, mib, trans=0):
    return pl.CostEstimate(flops=flops, bytes_accessed=int(mib * MIB), transcendentals=trans)


def dot(a, b):
    return lax.dot_general(a, b, (((1,), (0,)), ((), ())), preferred_element_type=F32)


def dot_nt(a, b):
    return lax.dot_general(a, b, (((1,), (1,)), ((), ())), preferred_element_type=F32)


def normed(values):
    center = values - jnp.mean(values, axis=-1, keepdims=True)
    scale = lax.rsqrt(jnp.mean(center * center, axis=-1, keepdims=True) + 1e-05)
    return center * scale, scale


def norm_back(grad, unit, scale, gain):
    inner = grad * gain
    first = jnp.mean(inner, axis=-1, keepdims=True)
    second = jnp.mean(inner * unit, axis=-1, keepdims=True)
    return scale * (inner - first - unit * second)


def full(shape, once=True):
    zeros = (0,) * len(shape)
    if once:
        return pl.BlockSpec(shape, lambda *_: zeros, pipeline_mode=pl.Buffered(1))
    return pl.BlockSpec(shape, lambda *_: zeros)


def turned(values):
    return values.T.reshape(OWNERS // CORES, CORES, SUB, values.shape[0])


def sds(shape, dtype):
    return jax.ShapeDtypeStruct(shape, dtype)


def hbm(value):
    return pltpu.with_memory_space_constraint(value, pltpu.HBM)


def launch(kernel, name, ins, outs, grid, scratch=(), price=None, deps=(), scalars=0, aliases=None, room=24):
    count = len(ins)

    def wrapped(*refs):
        kernel(*refs[:count], *refs[count + len(deps) :])

    in_specs = [s for _, s in ins[scalars:]] + [pl.BlockSpec(memory_space=pl.ANY)] * len(deps)
    return pl.pallas_call(
        wrapped if deps else kernel,
        grid_spec=pltpu.PrefetchScalarGridSpec(
            num_scalar_prefetch=scalars,
            grid=grid,
            in_specs=in_specs,
            out_specs=[s for _, s in outs],
            scratch_shapes=list(scratch),
        ),
        out_shape=[o for o, _ in outs],
        input_output_aliases=aliases or {},
        compiler_params=params(room),
        cost_estimate=price,
        name=name,
    )(*[a for a, _ in ins], *deps)


def local(kernel, name, me, ins, outs, deps=()):
    count = 1 + len(ins)

    def wrapped(*refs):
        kernel(*refs[:count], *refs[count + len(deps) :])

    vmem = pl.BlockSpec(memory_space=pltpu.VMEM)
    return pl.pallas_call(
        wrapped,
        in_specs=[pl.BlockSpec(memory_space=pltpu.SMEM)] + [vmem] * len(ins) + [pl.BlockSpec(memory_space=pl.ANY)] * len(deps),
        out_specs=[vmem] * len(outs),
        out_shape=outs,
        compiler_params=params(16),
        cost_estimate=cost(MIB, 4),
        name=name,
    )(me, *ins, *deps)


def project_kernel(places, me_ref, x_ref, *refs):
    parts = refs[:-5]
    a1t_ref, a_ref, qkv_ref, vec_ref, w_ref = refs[-5:]

    @pl.when(pl.program_id(0) == 0)
    def _():
        for part, distances in zip(parts, places):
            for k, distance in enumerate(distances):
                owner = jnp.bitwise_xor(me_ref[5], distance)
                w_ref[pl.ds(pl.multiple_of(owner * SUB, SUB), SUB), :] = part[k]
        vec_ref[...] = w_ref[:, 3 * D : 3 * D + 128].astype(F32).T[0:8, :]

    unit, _ = normed(x_ref[...].astype(F32))
    a1 = (unit * vec_ref[0:1, :] + vec_ref[1:2, :]).astype(BF16)
    a_ref[...] = a1
    a1t_ref[...] = turned(a1)
    for j in range(3):
        qkv_ref[j] = dot(a1, w_ref[:, j * D : (j + 1) * D]).astype(BF16)


def project(me, x, parts, rows=512):
    t = x.shape[0]
    width = parts[0][0].shape[-1]
    places = tuple(tuple(distances) for _, distances in parts)
    row = pl.BlockSpec((rows, D), lambda i, *_: (i, 0))
    pairs = OWNERS // CORES
    return launch(
        functools.partial(project_kernel, places),
        "project",
        [(me, None), (x, row)] + [(p, full(p.shape)) for p, _ in parts],
        [
            (sds((pairs, CORES, SUB, t), BF16), pl.BlockSpec((pairs, CORES, SUB, rows), lambda i, *_: (0, 0, 0, i))),
            (sds((t, D), BF16), row),
            (sds((3, t, D), BF16), pl.BlockSpec((3, rows, D), lambda i, *_: (0, i, 0))),
            (sds((8, D), F32), full((8, D), False)),
            (sds((D, width), BF16), full((D, width), False)),
        ],
        grid=(t // rows,),
        price=cost(2 * t * D * 3 * D, 9),
        scalars=1,
    )


def by_head(values):
    lane = lax.broadcasted_iota(jnp.int32, values.shape, 1)
    zero = jnp.zeros_like(values)
    return jnp.concatenate(
        [jnp.where(lane < HD, values, zero), jnp.where(lane >= HD, values, zero)], axis=0
    )


def own_blocks(values, blk):
    return jnp.concatenate([values[:HD, :blk], values[HD:, blk:]], axis=0)


def diagonal(blk):
    row = lax.broadcasted_iota(jnp.int32, (blk, 2 * blk), 0)
    col = lax.broadcasted_iota(jnp.int32, (blk, 2 * blk), 1)
    return row <= jnp.where(col >= blk, col - blk, col)


def over_blocks(halves_ref, per, front, back):
    def path(firsts):
        ready = front(0, firsts[0])
        for i in range(per):
            later = front(i + 1, firsts[i + 1]) if i + 1 < per else None
            back(i, firsts[i], ready)
            ready = later

    @pl.when(halves_ref[0] == 0)
    def _():
        path([0] * per)

    @pl.when(halves_ref[0] != 0)
    def _():
        path([0] * (per // 2) + [per // 2] * (per // 2))


FORWARD_BLOCK = 512
BACK_BLOCK = 128


def attend_kernel(halves_ref, qkv_ref, o_ref, ot_ref, lse_ref, vt_ref):
    q_ref, k_ref, v_ref = (qkv_ref.at[j] for j in range(3))
    blk = FORWARD_BLOCK
    vt_ref[...] = v_ref[...].T
    allowed = diagonal(blk)

    def front(i, first):
        queries = by_head(q_ref[i * blk : (i + 1) * blk, :] * jnp.bfloat16(0.125))
        return dot_nt(k_ref[first * blk : (i + 1) * blk, :], queries)

    def back(i, first, st):
        rows = slice(i * blk, (i + 1) * blk)
        n = (i - first) * blk
        last = jnp.where(allowed, st[n:, :], -1e30)
        top = jnp.max(last, axis=0, keepdims=True)
        if n:
            top = jnp.maximum(top, jnp.max(st[:n, :], axis=0, keepdims=True))
        expo = jnp.exp(last - top)
        total = jnp.sum(expo, axis=0, keepdims=True)
        expo = expo.astype(BF16)
        if n:
            rest = jnp.exp(st[:n, :] - top)
            total = total + jnp.sum(rest, axis=0, keepdims=True)
            expo = jnp.concatenate([rest.astype(BF16), expo], axis=0)
        out = dot(vt_ref[:, first * blk : (i + 1) * blk], expo) * (1.0 / total)
        out = own_blocks(out, blk).astype(BF16)
        lse = top + jnp.log(total)
        lse_ref[0, 0:1, rows] = lse[:, :blk]
        lse_ref[0, 1:2, rows] = lse[:, blk:]
        ot_ref[:, :, :, rows] = out.reshape(128 // SUB // CORES, CORES, SUB, blk)
        o_ref[rows, :] = out.T

    over_blocks(halves_ref, q_ref.shape[0] // blk, front, back)


def attend(halves, qkv, deps=()):
    t = qkv.shape[1]
    pairs = OWNERS // CORES
    part = 128 // SUB // CORES
    return launch(
        attend_kernel,
        "attend",
        [
            (halves, None),
            (qkv, pl.BlockSpec((3, t, 128), lambda p, *_: (0, 0, p))),
        ],
        [
            (sds((t, D), BF16), pl.BlockSpec((t, 128), lambda p, *_: (0, p))),
            (sds((pairs, CORES, SUB, t), BF16), pl.BlockSpec((part, CORES, SUB, t), lambda p, *_: (p, 0, 0, 0))),
            (sds((PAIRS, 2, t), F32), pl.BlockSpec((1, 2, t), lambda p, *_: (p, 0, 0))),
        ],
        grid=(PAIRS,),
        scratch=[pltpu.VMEM((128, t), BF16)],
        price=cost(4 * t * t * D, 8, t * t * H),
        scalars=1,
        deps=deps,
    )


def attend_back_kernel(halves_ref, qkv_ref, o_ref, do_ref, lse_ref, dqkv_ref, kt_ref, dk_ref, dv_ref):
    q_ref, k_ref, v_ref = (qkv_ref.at[j] for j in range(3))
    blk = BACK_BLOCK
    kt_ref[...] = k_ref[...].T
    prod = (do_ref[...].astype(F32) * o_ref[...].astype(F32)).T
    delta = [jnp.sum(prod[h * HD : (h + 1) * HD, :], axis=0, keepdims=True) for h in range(2)]
    allowed = diagonal(blk)

    def front(i, first):
        rows, keys = slice(i * blk, (i + 1) * blk), slice(first * blk, (i + 1) * blk)
        queries = by_head(q_ref[rows, :] * jnp.bfloat16(0.125))
        grads = by_head(do_ref[rows, :])
        return queries, grads, dot_nt(k_ref[keys, :], queries), dot_nt(v_ref[keys, :], grads)

    def gather(ref, first, i, value):
        n = (i - first) * blk
        if n:
            ref[first * blk : i * blk, :] += value[:n]
        ref[i * blk : (i + 1) * blk, :] = value[n:]

    def back(i, first, ready):
        queries, grads, st, dpt = ready
        rows, keys = slice(i * blk, (i + 1) * blk), slice(first * blk, (i + 1) * blk)
        n = (i - first) * blk
        lse = jnp.concatenate([lse_ref[0, 0:1, rows], lse_ref[0, 1:2, rows]], axis=1)
        rowsum = jnp.concatenate([d[:, rows] for d in delta], axis=1)
        pt = jnp.where(allowed, jnp.exp(st[n:, :] - lse), 0.0)
        if n:
            pt = jnp.concatenate([jnp.exp(st[:n, :] - lse), pt], axis=0)
        dst = (pt * (dpt - rowsum)).astype(BF16)
        gather(dv_ref, first, i, dot(pt.astype(BF16), grads))
        gather(dk_ref, first, i, dot(dst, queries))
        dqt = dot(kt_ref[:, keys], dst) * 0.125
        dqkv_ref[0, rows, :] = own_blocks(dqt, blk).T.astype(BF16)

    over_blocks(halves_ref, q_ref.shape[0] // blk, front, back)
    dqkv_ref[1] = dk_ref[...].astype(BF16)
    dqkv_ref[2] = dv_ref[...].astype(BF16)


def attend_back_first(halves, qkv, o, do, lse, count):
    t = qkv.shape[1]
    col = pl.BlockSpec((t, 128), lambda p, *_: (0, p))
    three = pl.BlockSpec((3, t, 128), lambda p, *_: (0, 0, p))
    return launch(
        attend_back_kernel,
        "attend_back_first",
        [(halves, None), (hbm(qkv), three), (hbm(o), col), (hbm(do), col), (lse, pl.BlockSpec((1, 2, t), lambda p, *_: (p, 0, 0)))],
        [(sds((3, t, D), BF16), three)],
        grid=(count,),
        scratch=[pltpu.VMEM((128, t), BF16)] + [pltpu.VMEM((t, 128), F32)] * 2,
        price=cost(10 * t * t * 128 * count, 2.5 * count, t * t * 2 * count),
        scalars=1,
    )[0]


def attend_back_rest(halves, qkv, o, do, lse, into, first, deps=()):
    t = qkv.shape[1]
    col = pl.BlockSpec((t, 128), lambda p, *_: (0, first + p))
    three = pl.BlockSpec((3, t, 128), lambda p, *_: (0, 0, first + p))
    count = PAIRS - first
    return launch(
        attend_back_kernel,
        "attend_back_rest",
        [(halves, None), (hbm(qkv), three), (hbm(o), col), (hbm(do), col), (lse, pl.BlockSpec((1, 2, t), lambda p, *_: (first + p, 0, 0)))],
        [(sds((3, t, D), BF16), three)],
        grid=(count,),
        scratch=[pltpu.VMEM((128, t), BF16)] + [pltpu.VMEM((t, 128), F32)] * 2,
        price=cost(10 * t * t * 128 * count, 2.5 * count, t * t * 2 * count),
        scalars=1,
        deps=(into,) + tuple(deps),
        aliases={5: 0},
    )[0]


def joint_kernel(me_ref, a1t_ref, dqkv_ref, own_ref, other_ref):
    t = dqkv_ref.shape[1]
    split_cores(me_ref, dot(a1t_ref[...].reshape(D, t), dqkv_ref[0]), own_ref, other_ref)


def joint_grads(me, a1t, dqkv, deps=()):
    t = dqkv.shape[1]
    pairs = OWNERS // CORES
    out = (sds((pairs, SUB, 3 * D), BF16), pl.BlockSpec((pairs, SUB, D), lambda i, *_: (0, 0, i)))
    return launch(
        joint_kernel,
        "joint_grads",
        [(me, None), (a1t, full(a1t.shape)), (dqkv, pl.BlockSpec((1, t, D), lambda i, *_: (i, 0, 0)))],
        [out, out],
        grid=(3,),
        price=cost(2 * t * D * 3 * D, 6),
        scalars=1,
        deps=deps,
    )


NEAR = 3 * SUB
ROWS = NEAR + 2 * COLS * SUB
WIDE = COLS * SUB


def near_weight(ref, j):
    return ref[:, SUB * j : SUB * (j + 1), :].reshape(D, D)


def block_of(ref, j):
    return near_weight(ref, 3 + j)


def lower(ref, j):
    halfway = COLS // CORES
    core, part = j // halfway, j % halfway
    per = OWNERS // CORES // halfway
    rows = [ref[CORES * p + core, NEAR + COLS * SUB : ROWS, :] for p in range(per * part, per * (part + 1))]
    return jnp.concatenate(rows, axis=0)


def middle_rows(x_ref, a1_ref, o_ref, dy_ref, vec_ref, w_ref, y_ref, part_ref, dz1o_ref, do_ref, dvec_ref,
                a2t_ref, et_ref, df_ref, du_ref, dz2_ref, dz1_ref, datt_ref, step, late):
    rows = x_ref.shape[0]
    here = pl.ds(pl.multiple_of(step * rows, rows), rows)
    c1, g2, b2, c2 = (vec_ref[k : k + 1, :] for k in (2, 3, 4, 5))
    x = x_ref[...].astype(F32)
    att = dot(o_ref[...], near_weight(w_ref, 0))
    t1 = jax.nn.sigmoid(dot(a1_ref[...], near_weight(w_ref, 1)) + c1)
    h1 = t1 * att + (1.0 - t1) * x
    unit, scale = normed(h1)
    a2 = (unit * g2 + b2).astype(BF16)
    a2t_ref[:, :, :, here] = turned(a2)
    t2 = jax.nn.sigmoid(dot(a2, near_weight(w_ref, 2)) + c2)
    late()
    f = None
    slopes = []
    kc = 0.7978845608028654
    for j in range(COLS):
        u = dot(a2, block_of(w_ref, j))
        sq = u * u
        half = 0.5 * jnp.tanh(u * (kc + (kc * 0.044715) * sq)) + 0.5
        gel = u * half
        e = gel.astype(BF16)
        slopes.append(half + gel * (1.0 - half) * (2.0 * kc + (6.0 * kc * 0.044715) * sq))
        et_ref[j, :, :, here] = e.T.reshape(et_ref.shape[1:3] + (rows,))
        part = dot(e, lower(w_ref, j))
        f = part if f is None else f + part
    y_ref[...] = (t2 * f + (1.0 - t2) * h1).astype(BF16)
    dy = dy_ref[...].astype(F32)
    dz2 = (dy * (f - h1) * t2 * (1.0 - t2)).astype(BF16)
    df = (dy * t2).astype(BF16)
    dz2_ref[here, :] = dz2
    df_ref[here, :] = df
    da2 = dot_nt(dz2, near_weight(w_ref, 2))
    for j in range(COLS):
        du = (dot_nt(df, lower(w_ref, j)) * slopes[j]).astype(BF16)
        du_ref[j, here, :] = du
        da2 = da2 + dot_nt(du, block_of(w_ref, j))
    dh1 = dy_ref[...].astype(F32) * (1.0 - t2) + norm_back(da2, unit, scale, g2)
    dz1 = (dh1 * (att - x_ref[...].astype(F32)) * t1 * (1.0 - t1)).astype(BF16)
    datt = (dh1 * t1).astype(BF16)
    dz1_ref[here, :] = dz1
    dz1o_ref[...] = dz1
    datt_ref[here, :] = datt
    part_ref[...] = dh1 * (1.0 - t1)
    do_ref[...] = dot_nt(datt, near_weight(w_ref, 0)).astype(BF16)

    def total(v):
        return jnp.sum(v, axis=0, keepdims=True)

    dvec_ref[2:3, :] += total(dz1.astype(F32))
    dvec_ref[3:4, :] += total(da2 * unit)
    dvec_ref[4:5, :] += total(da2)
    dvec_ref[5:6, :] += total(dz2.astype(F32))


def split_cores(me_ref, value, own_ref, other_ref, at=slice(None)):
    value = value.reshape(OWNERS // CORES, CORES, SUB, D)
    low = me_ref[0] == 0
    own_ref[:, at, :] = jnp.where(low, value[:, 0], value[:, 1]).astype(BF16)
    other_ref[:, at, :] = jnp.where(low, value[:, 1], value[:, 0]).astype(BF16)


SETS = (2, 2, 1)


def middle_kernel(plan, *refs):
    count = len(plan)
    me_ref, x_ref, a1_ref, o_ref, dy_ref, vec_ref = refs[:6]
    sources = refs[6 : 6 + count]
    a1t_hbm, ot_hbm = refs[6 + count : 8 + count]
    y_ref, part_ref, dz1o_ref, do_ref, dvec_ref, wa_ref = refs[8 + count : 14 + count]
    own1, other1, own2, other2, own3, other3 = refs[14 + count : 20 + count]
    w_ref, a1t_ref, ot_ref, sem, a2t_ref, et_ref, df_ref, du_ref, dz2_ref, dz1_ref, datt_ref = refs[20 + count :]
    step = pl.program_id(0)
    t = df_ref.shape[0]
    blocks = t // x_ref.shape[0]

    def copies():
        return [
            pltpu.make_async_copy(a1t_hbm, a1t_ref, sem.at[0]),
            pltpu.make_async_copy(ot_hbm, ot_ref, sem.at[1]),
        ]

    def gets(early):
        found, count = [], 2
        for source, ranges in zip(sources, plan):
            for first, rows, distances in ranges:
                at = slice(first, first + rows)
                for k, distance in enumerate(distances):
                    owner = jnp.bitwise_xor(me_ref[5], distance)
                    if early == (first < NEAR):
                        to = w_ref.at[owner, at, :]
                        found.append(pltpu.make_async_copy(source.at[k, at, :], to, sem.at[count]))
                    count += 1
        return found

    def late():
        @pl.when(step == 0)
        def _():
            for copy in gets(False):
                copy.wait()

    @pl.when(step == 0)
    def _():
        for copy in gets(True) + gets(False) + copies():
            copy.start()
        dvec_ref[...] = jnp.zeros_like(dvec_ref)
        for copy in gets(True):
            copy.wait()
        wa_ref[...] = near_weight(w_ref, 1)

    @pl.when(step < blocks)
    def _():
        middle_rows(x_ref, a1_ref, o_ref, dy_ref, vec_ref, w_ref, y_ref, part_ref, dz1o_ref, do_ref, dvec_ref,
                    a2t_ref, et_ref, df_ref, du_ref, dz2_ref, dz1_ref, datt_ref, step, late)

    def product(left, right, own_ref, other_ref, j):
        at = slice(SUB * j, SUB * (j + 1))
        split_cores(me_ref, dot(left.reshape(D, t), right), own_ref, other_ref, at)

    each = COLS // SETS[0]
    for k in range(SETS[0]):
        @pl.when(step == blocks + k)
        def _(k=k):
            for j in range(each):
                product(a2t_ref[...], du_ref[each * k + j], own1, other1, j)

    for k in range(SETS[1]):
        @pl.when(step == blocks + SETS[0] + k)
        def _(k=k):
            for j in range(each):
                at = SUB * (each * k + j)
                left = et_ref[:, :, at : at + SUB, :]
                left = left.reshape(CORES, OWNERS // CORES, SUB, t).swapaxes(0, 1)
                product(left, df_ref[...], own2, other2, j)

    @pl.when(step == blocks + SETS[0] + SETS[1])
    def _():
        for copy in copies():
            copy.wait()
        product(a2t_ref[...], dz2_ref[...], own3, other3, 0)
        product(ot_ref[...], datt_ref[...], own3, other3, 1)
        product(a1t_ref[...], dz1_ref[...], own3, other3, 2)


def middle(me, x, a1, o, dy, vec, sources, a1t, ot, rows=512):
    t = x.shape[0]
    blocks = t // rows
    pairs = OWNERS // CORES
    row = pl.BlockSpec((rows, D), lambda i, *_: (jnp.minimum(i, blocks - 1), 0))
    outs = []
    begin = blocks
    for steps, wide in zip(SETS, (COLS, COLS, 3)):
        block = (pairs, SUB * wide // steps, D)
        spec = pl.BlockSpec(block, lambda i, *_, begin=begin, steps=steps: (0, jnp.clip(i - begin, 0, steps - 1), 0))
        outs += [(sds((pairs, SUB * wide, D), BF16), spec)] * 2
        begin += steps
    wide = FF // OWNERS
    plan = tuple(ranges for _, ranges in sources)
    count = sum(len(distances) for ranges in plan for _, _, distances in ranges)
    hbm_ref = pl.BlockSpec(memory_space=pl.ANY)
    return launch(
        functools.partial(middle_kernel, plan),
        "middle",
        [(me, None)]
        + [(v, row) for v in (x, a1, o, dy)]
        + [(vec, full(vec.shape))]
        + [(v, hbm_ref) for v, _ in sources]
        + [(a1t, hbm_ref), (ot, hbm_ref)],
        [
            (sds((t, D), BF16), row),
            (sds((t, D), F32), row),
            (sds((t, D), BF16), row),
            (sds((t, D), BF16), row),
            (sds((8, D), F32), full((8, D), False)),
            (sds((D, D), BF16), full((D, D), False)),
        ]
        + outs,
        grid=(begin,),
        scratch=[
            pltpu.VMEM((OWNERS, ROWS, D), BF16),
            pltpu.VMEM((pairs, CORES, SUB, t), BF16),
            pltpu.VMEM((pairs, CORES, SUB, t), BF16),
            pltpu.SemaphoreType.DMA((2 + count,)),
            pltpu.VMEM((pairs, CORES, SUB, t), BF16),
            pltpu.VMEM((COLS, D // wide, wide, t), BF16),
            pltpu.VMEM((t, D), BF16),
            pltpu.VMEM((COLS, t, D), BF16),
            pltpu.VMEM((t, D), BF16),
            pltpu.VMEM((t, D), BF16),
            pltpu.VMEM((t, D), BF16),
        ],
        price=cost(2 * t * D * (6 * FF + 9 * D), 20, t * FF),
        scalars=1,
        room=60,
    )


def merge_kernel(plan, groups, gots, beside, me_ref, *refs):
    count = len(plan)
    outs = refs[count + gots + beside :]
    for group, members in enumerate(groups):
        begin = 0
        for k in members:
            arrived, first, bit = plan[k]
            own_ref, got_ref = refs[k], refs[count + arrived]
            keep_ref, send_ref = outs[k], outs[count + group]
            rows, width = own_ref.shape[-2:]
            at, to = slice(first, first + rows), slice(begin, begin + rows)
            total = own_ref[...].astype(F32) + got_ref[:, at, :].astype(F32).reshape(own_ref.shape)
            blocks = send_ref.shape[0]
            low = me_ref[bit] == 0
            keep = jnp.where(low, total[:, 0], total[:, 1]).astype(BF16)
            send = jnp.where(low, total[:, 1], total[:, 0]).astype(BF16)
            keep_ref[:, :, :width] = keep.reshape(blocks, rows, width)
            send_ref[:, to, :width] = send.reshape(blocks, rows, width)
            begin += rows
    if beside:
        vec = jnp.sum(refs[count + gots][...], axis=0)
        vec = jnp.concatenate([vec, jnp.zeros((120, D), F32)], axis=0).T
        vec = vec.reshape(OWNERS // (2 * CORES), 2, CORES, SUB, 128)
        vec = jnp.where(me_ref[1] == 0, vec[:, 0], vec[:, 1])
        vec = jnp.where(me_ref[0] == 0, vec[:, 0], vec[:, 1])
        vec = vec.reshape((vec.shape[0] // 2, 2, SUB, 128))
        keep_ref[:, :, width:] = jnp.where(low, vec[:, 0], vec[:, 1]).astype(BF16)
        send_ref[:, :, width:] = jnp.where(low, vec[:, 1], vec[:, 0]).astype(BF16)


def merge(me, items, groups, deps=(), vecs=()):
    owns, gots, plan, keeps = [], [], [], []
    for k, (own, got, first, bit, inner) in enumerate(items):
        blocks, rows, width = own.shape
        outer = blocks // (2 * inner)
        owns.append(own.reshape(outer, 2, inner, rows, width))
        known = [j for j, other in enumerate(gots) if other is got]
        if not known:
            known = [len(gots)]
            gots.append(got)
        plan.append((known[0], first, bit))
        width += 128 if vecs and k == len(items) - 1 else 0
        keeps.append(sds((blocks // 2, rows, width), BF16))
    sends = []
    for members in groups:
        blocks, _, width = keeps[members[0]].shape
        sends.append(sds((blocks, sum(keeps[k].shape[1] for k in members), width), BF16))
    kernel = functools.partial(merge_kernel, tuple(plan), groups, len(gots), len(vecs))
    done = local(kernel, "merge", me, owns + gots + list(vecs), keeps + sends, deps)
    return done[: len(items)], done[len(items) :]


def last_kernel(places, bit, me_ref, *refs):
    count = len(places)
    outs = refs[-4:]
    begin = 0
    for k, (arrived, first) in enumerate(places):
        rows = refs[k].shape[1]
        at = slice(begin, begin + rows)
        for j in range(2):
            block = jnp.bitwise_xor(me_ref[4], j)
            got = refs[count + arrived][block, first : first + rows, :]
            outs[j][at, :] = (refs[k][block].astype(F32) + got.astype(F32)).astype(BF16)
        begin += rows
    merge_kernel(((0, 0, bit),), ((0,),), 1, 0, me_ref, *refs[-6:-4], *outs[2:])


def last_merge(me, items, other, bit):
    gots, places = [], []
    for _, got, first in items:
        known = [j for j, value in enumerate(gots) if value is got]
        if not known:
            known = [len(gots)]
            gots.append(got)
        places.append((known[0], first))
    ins = [own for own, _, _ in items] + gots
    outs = [sds((sum(own.shape[1] for own, _, _ in items), D), BF16)] * 2
    blocks, rows, width = other[0].shape
    ins += [other[0].reshape(blocks // 2, 2, 1, rows, width), other[1]]
    outs += [sds((blocks // 2, rows, width), BF16)] * 2
    return local(functools.partial(last_kernel, tuple(places), bit), "last_merge", me, ins, outs)


def inputs_kernel(x_ref, dqkv_ref, dz1_ref, part_ref, vec_ref, dvec_ref, w_ref, wa_ref, dx_ref, out_ref, acc_ref):
    step = pl.program_id(0)

    @pl.when(step == 0)
    def _():
        acc_ref[...] = dvec_ref[...]

    unit, scale = normed(x_ref[...].astype(F32))
    da1 = dot_nt(dz1_ref[...], wa_ref[...])
    for j in range(3):
        da1 = da1 + dot_nt(dqkv_ref[j], w_ref[:, D * j : D * (j + 1)])
    dx_ref[...] = part_ref[...] + norm_back(da1, unit, scale, vec_ref[0:1, :])
    acc_ref[0:1, :] += jnp.sum(da1 * unit, axis=0, keepdims=True)
    acc_ref[1:2, :] += jnp.sum(da1, axis=0, keepdims=True)

    @pl.when(step == pl.num_programs(0) - 1)
    def _():
        out_ref[...] = acc_ref[...]


def inputs(x, dqkv, dz1, part, vec, dvec, w, wa, rows=512, deps=()):
    t = x.shape[0]
    row = pl.BlockSpec((rows, D), lambda i: (i, 0))
    shape = (8, D)
    return launch(
        inputs_kernel,
        "inputs",
        [
            (x, row),
            (dqkv, pl.BlockSpec((3, rows, D), lambda i: (0, i, 0))),
            (dz1, row),
            (part, row),
            (vec, full((8, D))),
            (dvec, full((8, D))),
            (w, full(w.shape)),
            (wa, full(wa.shape)),
        ],
        [(sds((t, D), F32), row), (sds(shape, F32), full(shape, False))],
        grid=(t // rows,),
        scratch=[pltpu.VMEM((8, D), F32)],
        price=cost(2 * t * D * 4 * D, 12),
        deps=deps,
    )


def collect_kernel(counts, *refs):
    total = jnp.float32(0.0)
    begin = 0
    outs = refs[sum(counts) :]
    for k, count in enumerate(counts):
        parts = refs[begin : begin + count]
        begin += count
        if count == 1:
            value = jnp.sum(parts[0][...].astype(F32), axis=0)
        else:
            value = sum(p[...].astype(F32) for p in parts)
        outs[k][...] = value
        total = total + jnp.sum(value * value)
    outs[-1][...] = jnp.full(outs[-1].shape, total, F32)


def collect(groups, n):
    shapes = [g[0].shape[1:] if len(g) == 1 else g[0].shape for g in groups]
    return pl.pallas_call(
        functools.partial(collect_kernel, tuple(len(g) for g in groups)),
        out_shape=[sds(s, F32) for s in shapes] + [sds((n, 1, 128), F32)],
        compiler_params=params(16),
        cost_estimate=cost(MIB, 3),
        name="collect",
    )(*[v for g in groups for v in g])


RATES = (D ** (-0.5), (D // 16) ** (-0.5), D ** (-0.5), D ** (-0.5), FF ** (-0.5), D ** (-0.5), 0.5)


def update(grad, master, moment, square, clip, rate):
    clipped = grad * clip
    new_moment = 0.5 * moment + 0.5 * clipped
    new_square = 0.5 * square + 0.5 * clipped * clipped
    fix = 1.0 - 0.5**STEP
    stepped = new_moment / fix / (jnp.sqrt(new_square / fix) + 1e-08)
    return (master - rate * (stepped + 0.01 * master), new_moment, new_square)


def adam_kernel(*refs):
    down_ref, joint_ref, sq_ref = refs[:3]
    state = refs[3:24]
    norm_ref = refs[24]
    outs = refs[25:]
    sub = joint_ref.shape[0]
    norm = jnp.sqrt(jnp.sum(sq_ref[...], axis=0)[0:1, 0:1])
    norm_ref[...] = jnp.broadcast_to(norm, norm_ref.shape)
    clip = jnp.minimum(1.0, 1.0 / (norm + 1e-06))

    def piece(index, grad, at):
        old = [state[3 * index + k][at] for k in range(3)]
        new = update(grad, *old, clip, RATES[index])
        for k in range(3):
            outs[3 * index + k][at] = new[k]

    every = slice(None)
    piece(0, joint_ref[:, : 3 * D], (every, every))
    turned_vec = jnp.concatenate([joint_ref[:, 3 * D :], jnp.zeros((128 - sub, 128), F32)], axis=0).T
    piece(6, turned_vec[0:6, 0:sub], (every, every))

    def down(j, count=1):
        return down_ref[sub * j : sub * (j + count), :]

    up = jnp.concatenate([down(j) for j in range(COLS)], axis=1)
    step = FF // OWNERS
    order = [up[:, FF // CORES * c + step * p :][:, :step] for p in range(OWNERS // CORES) for c in range(CORES)]
    piece(3, jnp.concatenate(order, axis=1), (every, every))
    piece(4, down(COLS, COLS), (every, every))
    piece(5, down(2 * COLS), (every, every))
    piece(1, down(2 * COLS + 1), (every, every))
    piece(2, down(2 * COLS + 2), (every, every))


def adam(grads, squares, state):
    return pl.pallas_call(
        adam_kernel,
        out_shape=[sds((1, 128), F32)] + [sds(s.shape, F32) for s in state],
        compiler_params=params(24),
        cost_estimate=cost(4 * MIB, 4),
        name="adam",
    )(*grads, squares, *state)


def ordered(up):
    rows = up.shape[0]
    return up.reshape(rows, OWNERS // CORES, CORES, FF // OWNERS).swapaxes(1, 2).reshape(rows, FF)


def turn_norms(state):
    return tuple(state[:18]) + tuple(s.T for s in state[18:])


def column_blocks(w):
    return [w[..., D * j : D * (j + 1)] for j in range(w.shape[-1] // D)]


def pack_kernel(qkv_ref, attn_ref, gate_ref, up_ref, down_ref, fgate_ref, norms_ref, one_ref, near_ref, rest_ref):
    sub = qkv_ref.shape[0]
    norms = jnp.concatenate([norms_ref[...], jnp.zeros((128 - norms_ref.shape[0], sub), F32)], axis=0)
    norms = jnp.concatenate([norms, jnp.zeros((128, 128 - sub), F32)], axis=1).T[0:sub]
    one = jnp.concatenate([qkv_ref[...], norms], axis=1).astype(BF16)
    one_ref[...] = one
    for j, ref in enumerate((attn_ref, gate_ref, fgate_ref)):
        near_ref[0, sub * j : sub * (j + 1), :] = ref[...].astype(BF16)
    step = FF // OWNERS
    up = up_ref[...]
    order = [up[:, step * (CORES * p + c) :][:, :step] for c in range(CORES) for p in range(OWNERS // CORES)]
    up = jnp.concatenate(order, axis=1).astype(BF16)
    for j in range(COLS):
        rest_ref[0, sub * j : sub * (j + 1), :] = up[:, D * j : D * (j + 1)]
    rest_ref[0, sub * COLS :, :] = down_ref[...].astype(BF16)


def pack(masters):
    sub = masters[0].shape[0]
    ins = [(hbm(v), full(v.shape)) for v in [*masters[:6], masters[6].T]]
    shapes = [(sub, 3 * D + 128), (1, 3 * sub, D), (1, 2 * COLS * sub, D)]
    outs = [(sds(s, BF16), full(s, False)) for s in shapes]
    return launch(pack_kernel, "pack", ins, outs, grid=(1,), price=cost(MIB, 3))


def beside_kernel(per, me_ref, *refs):
    out_ref = refs[-1]
    begin = 0
    for k in range(0, len(refs) - 1, per):
        n, rows, _ = refs[k].shape
        for j in range(per):
            out_ref[n * j : n * (j + 1), begin : begin + rows, :] = refs[k + j][...]
        begin += rows


def beside(me, items, deps=()):
    ins = [v for item in items for v in item]
    shape = (sum(v.shape[0] for v in items[0]), sum(item[0].shape[1] for item in items), D)
    return local(functools.partial(beside_kernel, len(items[0])), "beside", me, ins, [sds(shape, BF16)], deps)[0]


def join_kernel(cuts, count, me_ref, *refs):
    outs = refs[len(refs) - len(cuts) - (1 if count else 0) :]
    for k, (item, first, rows) in enumerate(cuts):
        for j in range(2):
            half = refs[2 * item + j]
            n = half.shape[0]
            outs[k][n * j : n * (j + 1)] = half[:, first : first + rows, :]
    for k in range(count):
        outs[-1][k] = refs[len(refs) - len(outs) - count + k][...]


def join(me, items, cuts, deps=(), singles=()):
    ins = [v for item in items for v in item] + list(singles)
    outs = [sds((2 * items[i][0].shape[0], rows, items[i][0].shape[2]), BF16) for i, _, rows in cuts]
    if singles:
        outs.append(sds((len(singles),) + singles[0].shape, BF16))
    return local(functools.partial(join_kernel, tuple(cuts), len(singles)), "join", me, ins, outs, deps)


def pack_whole(weights):
    qkv, attn, gate, up, down, fgate, norms = weights
    one = jnp.concatenate([qkv, jnp.pad(norms, ((0, 0), (0, 128 - norms.shape[1])))], axis=1)
    rest = [attn, gate, fgate] + column_blocks(ordered(up))
    rest = [p.reshape(OWNERS, SUB, D) for p in rest] + [down.reshape(OWNERS, COLS * SUB, D)]
    return one.reshape(OWNERS, SUB, one.shape[1]), jnp.concatenate(rest, axis=1)


def unpack_whole(one, two, three, joint, vec):
    def blocks(g, start, count):
        parts = [g[:, SUB * j : SUB * (j + 1), :].reshape(D, D) for j in range(start, start + count)]
        return jnp.concatenate(parts, axis=1)

    up = blocks(one, 0, COLS).reshape(D, CORES, OWNERS // CORES, FF // OWNERS)
    return (
        joint.reshape(D, 3 * D),
        blocks(three, 1, 1),
        blocks(three, 2, 1),
        up.swapaxes(1, 2).reshape(D, FF),
        two.reshape(FF, D),
        blocks(three, 0, 1),
        vec[:6].T,
    )


def swap(value, axis, size, bit):
    return lax.ppermute(value, axis, [(i, i ^ bit) for i in range(size)])


def body(nd, nf, tokens, cotangent, halves, *state):
    n = nd * nf
    if n == OWNERS and nf == 2 * CORES:
        return direct(nd, nf, tokens, cotangent, halves, *state)
    return general(n, tokens, cotangent, halves, *state)


def direct(nd, nf, tokens, cotangent, halves, *state):
    both = ("dp", "fsdp")
    nx = nf // CORES
    f = lax.axis_index("fsdp").astype(jnp.int32)
    d = lax.axis_index("dp").astype(jnp.int32)
    me = jnp.stack([f % 2, f // 2, d % 2, (d // 2) % 2, d // 4, d * nf + f, d])

    def to(v, bit):
        axis, size, step = (("fsdp", nf, 1), ("fsdp", nf, 2), ("dp", nd, 1), ("dp", nd, 2), ("dp", nd, 4))[bit]
        return swap(v, axis, size, step)

    one, near, rest = pack(state[0::3])
    ones = [one] + [swap(one, "dp", nd, k) for k in range(1, nd)]
    rest, near, own = join(
        me, [(rest, to(rest, 4)), (near, to(near, 1))], [(0, 0, 2 * WIDE), (1, 0, NEAR)], singles=ones
    )
    up, down, near, own = join(
        me,
        [(rest, to(rest, 3)), (near, to(near, 2)), (own, to(own, 1))],
        [(0, 0, WIDE), (0, WIDE, WIDE), (1, 0, NEAR), (2, 0, SUB)],
    )
    got = to(up, 2), to(down, 1), to(near, 4)
    spots = [nf * k + j for j in (0, CORES) for k in range(nd)]
    parts = [(own, spots), (to(own, 0), [k + 1 for k in spots])]
    every = [(0, 0, WIDE), (1, 0, WIDE), (2, 0, NEAR)]
    a1t, a1, qkv, vec, w = project(me, tokens, parts)
    up, down, near = join(me, list(zip((up, down, near), got)), every, (a1t,))
    got = to(near, 3), to(up, 1), to(down, 2)
    here = beside(me, [(near,), (up,), (down,)])
    crossed = to(here, 0)
    o, ot, lse = attend(halves, qkv, (here,))
    there = beside(me, [(v,) for v in got], (o, crossed))
    sources = []
    parts = ((0, NEAR, (2, 4, 16, 8)), (NEAR, WIDE, (16, 8, 4, 2)), (NEAR + WIDE, WIDE, (16, 8, 2, 4)))
    for value, far, core in ((here, 0, 0), (crossed, 0, 1), (there, 1, 0), (to(there, 0), 1, 1)):
        ranges = []
        for first, rows, bits in parts:
            owners = [far * bits[3] + core]
            for bit in bits[:3]:
                owners = owners + [k + bit for k in owners]
            ranges.append((first, rows, tuple(owners)))
        sources.append((value, tuple(ranges)))
    y, part, dz1, do, dvec, wa, *terms = middle(me, tokens, a1, o, cotangent, vec, sources, a1t, ot)
    first, second, third = ((own, to(other, 0)) for own, other in zip(terms[0::2], terms[1::2]))
    head = attend_back_first(halves, qkv, o, do, lse, 1)
    (first, second, third), sends = merge(
        me, [(*first, 0, 1, 1), (*second, 0, 2, nx), (*third, 0, 3, 2 * nx)], ((0,), (1,), (2,)), (head,)
    )
    got = [to(v, bit) for v, bit in zip(sends, (1, 2, 3))]
    dqkv = attend_back_rest(halves, qkv, o, do, lse, head, 1, deps=(first,))
    own, other = joint_grads(me, a1t, dqkv, deps=tuple(got))
    (first, second, third, joint), sends = merge(
        me,
        [(first, got[0], 0, 2, 1), (second, got[1], 0, 3, nx), (third, got[2], 0, 2, nx), (own, to(other, 0), 0, 1, 1)],
        ((0, 2), (1,), (3,)),
    )
    got = [to(v, bit) for v, bit in zip(sends, (2, 3, 1))]
    dx, dvec = inputs(tokens, dqkv, dz1, part, vec, dvec, w, wa, deps=(first,))
    vecs = [lax.all_gather(dvec, "fsdp", axis=0)]
    below = first.shape[1]
    (first, second, third, joint), sends = merge(
        me,
        [(first, got[0], 0, 3, 1), (second, got[1], 0, 1, 1), (third, got[0], below, 1, 1), (joint, got[2], 0, 2, 1)],
        ((0,), (1, 2), (3,)),
        vecs=vecs,
    )
    got = [to(v, bit) for v, bit in zip(sends, (3, 1, 2))]
    below = second.shape[1]
    keep, send, joint, far = last_merge(
        me, [(first, got[0], 0), (second, got[1], 0), (third, got[1], below)], (joint, got[2]), 3
    )
    sums = [keep, to(send, 4)]
    (joint,), (far,) = merge(me, [(joint, to(far, 3), 0, 4, 1)], ((0,),))
    keep3, far3 = joint, to(far, 4)

    *grads, squares = collect([sums, [keep3[0], far3[0]]], nd * nf)
    squares = lax.all_to_all(squares, both, 0, 0, tiled=True)
    norm, *new = adam(grads, squares, turn_norms(state))
    return (y, dx, norm[0, 0], *turn_norms(new))


def layer_general(me, tokens, cotangent, halves, one, rest):
    a1t, a1, qkv, vec, w = project(me, tokens, [(one, range(OWNERS))])
    o, ot, lse = attend(halves, qkv)
    sources = [(rest, ((0, ROWS, tuple(range(OWNERS))),))]
    y, part, dz1, do, dvec, wa, *terms = middle(me, tokens, a1, o, cotangent, vec, sources, a1t, ot)
    head = attend_back_first(halves, qkv, o, do, lse, 1)
    dqkv = attend_back_rest(halves, qkv, o, do, lse, head, 1)
    terms += joint_grads(me, a1t, dqkv)
    dx, dvec = inputs(tokens, dqkv, dz1, part, vec, dvec, w, wa)
    terms = [
        jnp.stack([own, other], axis=1).reshape((OWNERS,) + own.shape[1:]).astype(F32)
        for own, other in zip(terms[0::2], terms[1::2])
    ]
    return (y, dx) + unpack_whole(*terms, dvec)


def general(n, tokens, cotangent, halves, *state):
    both = ("dp", "fsdp")
    rounded = [m.astype(BF16) for m in state[0::3]]
    packed = pack_whole([lax.all_gather(w, both, axis=0, tiled=True) for w in rounded])
    me = jnp.zeros((7,), jnp.int32)
    y, dx, *terms = layer_general(me, tokens, cotangent, halves, *packed)
    q, wo, wa, wu, wd, wf, nv = [
        lax.psum_scatter(t, both, scatter_dimension=0, tiled=True) for t in terms
    ]
    got = [
        jnp.concatenate(column_blocks(ordered(wu)) + [wd, wf, wo, wa], axis=0),
        jnp.concatenate([q, jnp.pad(nv, ((0, 0), (0, 128 - nv.shape[1])))], axis=1),
    ]
    *grads, squares = collect([[g[None]] for g in got], n)
    squares = lax.all_to_all(squares, both, 0, 0, tiled=True)
    norm, *new = adam(grads, squares, turn_norms(state))
    return (y, dx, norm[0, 0], *turn_norms(new))


def solution(mesh):
    rows = P(("dp", "fsdp"), None)
    nd, nf = mesh.shape["dp"], mesh.shape["fsdp"]
    return jax.shard_map(
        functools.partial(body, nd, nf),
        mesh=mesh,
        in_specs=(rows, rows, P(("dp", "fsdp"))) + (rows,) * 21,
        out_specs=(rows, rows, P()) + (rows,) * 21,
        check_vma=False,
    )
```

```python
import functools
import jax
import jax.numpy as jnp
from jax import lax
from jax.experimental import pallas as pl
from jax.experimental.pallas import tpu as pltpu
from jax.sharding import PartitionSpec as P

D = 512
H = 8
HD = 64
FF = 2048
STEP = 5
PAIRS = H // 2
SUB = 16
OWNERS = D // SUB
COLS = FF // D
F32 = jnp.float32
BF16 = jnp.bfloat16
MIB = 1024 * 1024
CORES = 2


def params(mib):
    return pltpu.CompilerParams(vmem_limit_bytes=mib * MIB)


def cost(flops, mib, trans=0):
    return pl.CostEstimate(flops=flops, bytes_accessed=int(mib * MIB), transcendentals=trans)


def dot(a, b):
    return lax.dot_general(a, b, (((1,), (0,)), ((), ())), preferred_element_type=F32)


def dot_nt(a, b):
    return lax.dot_general(a, b, (((1,), (1,)), ((), ())), preferred_element_type=F32)


def normed(values):
    center = values - jnp.mean(values, axis=-1, keepdims=True)
    scale = lax.rsqrt(jnp.mean(center * center, axis=-1, keepdims=True) + 1e-05)
    return center * scale, scale


def norm_back(grad, unit, scale, gain):
    inner = grad * gain
    first = jnp.mean(inner, axis=-1, keepdims=True)
    second = jnp.mean(inner * unit, axis=-1, keepdims=True)
    return scale * (inner - first - unit * second)


def full(shape, once=True):
    zeros = (0,) * len(shape)
    if once:
        return pl.BlockSpec(shape, lambda *_: zeros, pipeline_mode=pl.Buffered(1))
    return pl.BlockSpec(shape, lambda *_: zeros)


def turned(values):
    return values.T.reshape(OWNERS // CORES, CORES, SUB, values.shape[0])


def sds(shape, dtype):
    return jax.ShapeDtypeStruct(shape, dtype)


def hbm(value):
    return pltpu.with_memory_space_constraint(value, pltpu.HBM)


def launch(kernel, name, ins, outs, grid, scratch=(), price=None, deps=(), scalars=0, aliases=None, room=24):
    count = len(ins)

    def wrapped(*refs):
        kernel(*refs[:count], *refs[count + len(deps) :])

    in_specs = [s for _, s in ins[scalars:]] + [pl.BlockSpec(memory_space=pl.ANY)] * len(deps)
    return pl.pallas_call(
        wrapped if deps else kernel,
        grid_spec=pltpu.PrefetchScalarGridSpec(
            num_scalar_prefetch=scalars,
            grid=grid,
            in_specs=in_specs,
            out_specs=[s for _, s in outs],
            scratch_shapes=list(scratch),
        ),
        out_shape=[o for o, _ in outs],
        input_output_aliases=aliases or {},
        compiler_params=params(room),
        cost_estimate=price,
        name=name,
    )(*[a for a, _ in ins], *deps)


def local(kernel, name, me, ins, outs, deps=()):
    count = 1 + len(ins)

    def wrapped(*refs):
        kernel(*refs[:count], *refs[count + len(deps) :])

    vmem = pl.BlockSpec(memory_space=pltpu.VMEM)
    return pl.pallas_call(
        wrapped,
        in_specs=[pl.BlockSpec(memory_space=pltpu.SMEM)] + [vmem] * len(ins) + [pl.BlockSpec(memory_space=pl.ANY)] * len(deps),
        out_specs=[vmem] * len(outs),
        out_shape=outs,
        compiler_params=params(16),
        cost_estimate=cost(MIB, 4),
        name=name,
    )(me, *ins, *deps)


def project_kernel(places, me_ref, x_ref, *refs):
    parts = refs[:-5]
    a1t_ref, a_ref, qkv_ref, vec_ref, w_ref = refs[-5:]

    @pl.when(pl.program_id(0) == 0)
    def _():
        for part, distances in zip(parts, places):
            for k, distance in enumerate(distances):
                owner = jnp.bitwise_xor(me_ref[5], distance)
                w_ref[pl.ds(pl.multiple_of(owner * SUB, SUB), SUB), :] = part[k]
        vec_ref[...] = w_ref[:, 3 * D : 3 * D + 128].astype(F32).T[0:8, :]

    unit, _ = normed(x_ref[...].astype(F32))
    a1 = (unit * vec_ref[0:1, :] + vec_ref[1:2, :]).astype(BF16)
    a_ref[...] = a1
    a1t_ref[...] = turned(a1)
    for j in range(3):
        qkv_ref[j] = dot(a1, w_ref[:, j * D : (j + 1) * D]).astype(BF16)


def project(me, x, parts, rows=512):
    t = x.shape[0]
    width = parts[0][0].shape[-1]
    places = tuple(tuple(distances) for _, distances in parts)
    row = pl.BlockSpec((rows, D), lambda i, *_: (i, 0))
    pairs = OWNERS // CORES
    return launch(
        functools.partial(project_kernel, places),
        "project",
        [(me, None), (x, row)] + [(p, full(p.shape)) for p, _ in parts],
        [
            (sds((pairs, CORES, SUB, t), BF16), pl.BlockSpec((pairs, CORES, SUB, rows), lambda i, *_: (0, 0, 0, i))),
            (sds((t, D), BF16), row),
            (sds((3, t, D), BF16), pl.BlockSpec((3, rows, D), lambda i, *_: (0, i, 0))),
            (sds((8, D), F32), full((8, D), False)),
            (sds((D, width), BF16), full((D, width), False)),
        ],
        grid=(t // rows,),
        price=cost(2 * t * D * 3 * D, 9),
        scalars=1,
    )


def by_head(values):
    lane = lax.broadcasted_iota(jnp.int32, values.shape, 1)
    zero = jnp.zeros_like(values)
    return jnp.concatenate(
        [jnp.where(lane < HD, values, zero), jnp.where(lane >= HD, values, zero)], axis=0
    )


def own_blocks(values, blk):
    return jnp.concatenate([values[:HD, :blk], values[HD:, blk:]], axis=0)


def diagonal(blk):
    row = lax.broadcasted_iota(jnp.int32, (blk, 2 * blk), 0)
    col = lax.broadcasted_iota(jnp.int32, (blk, 2 * blk), 1)
    return row <= jnp.where(col >= blk, col - blk, col)


def over_blocks(halves_ref, per, front, back):
    def path(firsts):
        ready = front(0, firsts[0])
        for i in range(per):
            later = front(i + 1, firsts[i + 1]) if i + 1 < per else None
            back(i, firsts[i], ready)
            ready = later

    @pl.when(halves_ref[0] == 0)
    def _():
        path([0] * per)

    @pl.when(halves_ref[0] != 0)
    def _():
        path([0] * (per // 2) + [per // 2] * (per // 2))


FORWARD_BLOCK = 512
BACK_BLOCK = 128


def attend_kernel(halves_ref, qkv_ref, o_ref, ot_ref, lse_ref, vt_ref):
    q_ref, k_ref, v_ref = (qkv_ref.at[j] for j in range(3))
    blk = FORWARD_BLOCK
    vt_ref[...] = v_ref[...].T
    allowed = diagonal(blk)

    def front(i, first):
        queries = by_head(q_ref[i * blk : (i + 1) * blk, :] * jnp.bfloat16(0.125))
        return dot_nt(k_ref[first * blk : (i + 1) * blk, :], queries)

    def back(i, first, st):
        rows = slice(i * blk, (i + 1) * blk)
        n = (i - first) * blk
        last = jnp.where(allowed, st[n:, :], -1e30)
        top = jnp.max(last, axis=0, keepdims=True)
        if n:
            top = jnp.maximum(top, jnp.max(st[:n, :], axis=0, keepdims=True))
        expo = jnp.exp(last - top)
        total = jnp.sum(expo, axis=0, keepdims=True)
        expo = expo.astype(BF16)
        if n:
            rest = jnp.exp(st[:n, :] - top)
            total = total + jnp.sum(rest, axis=0, keepdims=True)
            expo = jnp.concatenate([rest.astype(BF16), expo], axis=0)
        out = dot(vt_ref[:, first * blk : (i + 1) * blk], expo) * (1.0 / total)
        out = own_blocks(out, blk).astype(BF16)
        lse = top + jnp.log(total)
        lse_ref[0, 0:1, rows] = lse[:, :blk]
        lse_ref[0, 1:2, rows] = lse[:, blk:]
        ot_ref[:, :, :, rows] = out.reshape(128 // SUB // CORES, CORES, SUB, blk)
        o_ref[rows, :] = out.T

    over_blocks(halves_ref, q_ref.shape[0] // blk, front, back)


def attend(halves, qkv, deps=()):
    t = qkv.shape[1]
    pairs = OWNERS // CORES
    part = 128 // SUB // CORES
    return launch(
        attend_kernel,
        "attend",
        [
            (halves, None),
            (qkv, pl.BlockSpec((3, t, 128), lambda p, *_: (0, 0, p))),
        ],
        [
            (sds((t, D), BF16), pl.BlockSpec((t, 128), lambda p, *_: (0, p))),
            (sds((pairs, CORES, SUB, t), BF16), pl.BlockSpec((part, CORES, SUB, t), lambda p, *_: (p, 0, 0, 0))),
            (sds((PAIRS, 2, t), F32), pl.BlockSpec((1, 2, t), lambda p, *_: (p, 0, 0))),
        ],
        grid=(PAIRS,),
        scratch=[pltpu.VMEM((128, t), BF16)],
        price=cost(4 * t * t * D, 8, t * t * H),
        scalars=1,
        deps=deps,
    )


def attend_back_kernel(halves_ref, qkv_ref, o_ref, do_ref, lse_ref, dqkv_ref, kt_ref, dk_ref, dv_ref):
    q_ref, k_ref, v_ref = (qkv_ref.at[j] for j in range(3))
    blk = BACK_BLOCK
    kt_ref[...] = k_ref[...].T
    prod = (do_ref[...].astype(F32) * o_ref[...].astype(F32)).T
    delta = [jnp.sum(prod[h * HD : (h + 1) * HD, :], axis=0, keepdims=True) for h in range(2)]
    allowed = diagonal(blk)

    def front(i, first):
        rows, keys = slice(i * blk, (i + 1) * blk), slice(first * blk, (i + 1) * blk)
        queries = by_head(q_ref[rows, :] * jnp.bfloat16(0.125))
        grads = by_head(do_ref[rows, :])
        return queries, grads, dot_nt(k_ref[keys, :], queries), dot_nt(v_ref[keys, :], grads)

    def gather(ref, first, i, value):
        n = (i - first) * blk
        if n:
            ref[first * blk : i * blk, :] += value[:n]
        ref[i * blk : (i + 1) * blk, :] = value[n:]

    def back(i, first, ready):
        queries, grads, st, dpt = ready
        rows, keys = slice(i * blk, (i + 1) * blk), slice(first * blk, (i + 1) * blk)
        n = (i - first) * blk
        lse = jnp.concatenate([lse_ref[0, 0:1, rows], lse_ref[0, 1:2, rows]], axis=1)
        rowsum = jnp.concatenate([d[:, rows] for d in delta], axis=1)
        pt = jnp.where(allowed, jnp.exp(st[n:, :] - lse), 0.0)
        if n:
            pt = jnp.concatenate([jnp.exp(st[:n, :] - lse), pt], axis=0)
        dst = (pt * (dpt - rowsum)).astype(BF16)
        gather(dv_ref, first, i, dot(pt.astype(BF16), grads))
        gather(dk_ref, first, i, dot(dst, queries))
        dqt = dot(kt_ref[:, keys], dst) * 0.125
        dqkv_ref[0, rows, :] = own_blocks(dqt, blk).T.astype(BF16)

    over_blocks(halves_ref, q_ref.shape[0] // blk, front, back)
    dqkv_ref[1] = dk_ref[...].astype(BF16)
    dqkv_ref[2] = dv_ref[...].astype(BF16)


def attend_back_first(halves, qkv, o, do, lse, count):
    t = qkv.shape[1]
    col = pl.BlockSpec((t, 128), lambda p, *_: (0, p))
    three = pl.BlockSpec((3, t, 128), lambda p, *_: (0, 0, p))
    return launch(
        attend_back_kernel,
        "attend_back_first",
        [(halves, None), (hbm(qkv), three), (o, col), (do, col), (lse, pl.BlockSpec((1, 2, t), lambda p, *_: (p, 0, 0)))],
        [(sds((3, t, D), BF16), three)],
        grid=(count,),
        scratch=[pltpu.VMEM((128, t), BF16)] + [pltpu.VMEM((t, 128), F32)] * 2,
        price=cost(10 * t * t * 128 * count, 2.5 * count, t * t * 2 * count),
        scalars=1,
    )[0]


def attend_back_rest(halves, qkv, o, do, lse, into, first, deps=()):
    t = qkv.shape[1]
    col = pl.BlockSpec((t, 128), lambda p, *_: (0, first + p))
    three = pl.BlockSpec((3, t, 128), lambda p, *_: (0, 0, first + p))
    count = PAIRS - first
    return launch(
        attend_back_kernel,
        "attend_back_rest",
        [(halves, None), (hbm(qkv), three), (o, col), (do, col), (lse, pl.BlockSpec((1, 2, t), lambda p, *_: (first + p, 0, 0)))],
        [(sds((3, t, D), BF16), three)],
        grid=(count,),
        scratch=[pltpu.VMEM((128, t), BF16)] + [pltpu.VMEM((t, 128), F32)] * 2,
        price=cost(10 * t * t * 128 * count, 2.5 * count, t * t * 2 * count),
        scalars=1,
        deps=(into,) + tuple(deps),
        aliases={5: 0},
    )[0]


def joint_kernel(me_ref, a1t_ref, dqkv_ref, own_ref, other_ref):
    t = dqkv_ref.shape[1]
    split_cores(me_ref, dot(a1t_ref[...].reshape(D, t), dqkv_ref[0]), own_ref, other_ref)


def joint_grads(me, a1t, dqkv, deps=()):
    t = dqkv.shape[1]
    pairs = OWNERS // CORES
    out = (sds((pairs, SUB, 3 * D), BF16), pl.BlockSpec((pairs, SUB, D), lambda i, *_: (0, 0, i)))
    return launch(
        joint_kernel,
        "joint_grads",
        [(me, None), (a1t, full(a1t.shape)), (dqkv, pl.BlockSpec((1, t, D), lambda i, *_: (i, 0, 0)))],
        [out, out],
        grid=(3,),
        price=cost(2 * t * D * 3 * D, 6),
        scalars=1,
        deps=deps,
    )


NEAR = 3 * SUB
ROWS = NEAR + 2 * COLS * SUB
WIDE = COLS * SUB


def near_weight(ref, j):
    return ref[:, SUB * j : SUB * (j + 1), :].reshape(D, D)


def block_of(ref, j):
    return near_weight(ref, 3 + j)


def lower(ref, j):
    halfway = COLS // CORES
    core, part = j // halfway, j % halfway
    per = OWNERS // CORES // halfway
    rows = [ref[CORES * p + core, NEAR + COLS * SUB : ROWS, :] for p in range(per * part, per * (part + 1))]
    return jnp.concatenate(rows, axis=0)


def middle_rows(x_ref, a1_ref, o_ref, dy_ref, vec_ref, w_ref, y_ref, part_ref, dz1o_ref, do_ref, dvec_ref,
                a2t_ref, et_ref, df_ref, du_ref, dz2_ref, dz1_ref, datt_ref, step, late):
    rows = x_ref.shape[0]
    here = pl.ds(pl.multiple_of(step * rows, rows), rows)
    c1, g2, b2, c2 = (vec_ref[k : k + 1, :] for k in (2, 3, 4, 5))
    x = x_ref[...].astype(F32)
    att = dot(o_ref[...], near_weight(w_ref, 0))
    t1 = jax.nn.sigmoid(dot(a1_ref[...], near_weight(w_ref, 1)) + c1)
    h1 = t1 * att + (1.0 - t1) * x
    unit, scale = normed(h1)
    a2 = (unit * g2 + b2).astype(BF16)
    a2t_ref[:, :, :, here] = turned(a2)
    t2 = jax.nn.sigmoid(dot(a2, near_weight(w_ref, 2)) + c2)
    df = (dy_ref[...].astype(F32) * t2).astype(BF16)
    df_ref[here, :] = df
    late()
    kc = 0.7978845608028654

    def ahead(j):
        return dot(a2, block_of(w_ref, j)), dot_nt(df, lower(w_ref, j))

    f = da2 = None
    ready = ahead(0)
    for j in range(COLS):
        u, de = ready
        if j + 1 < COLS:
            ready = ahead(j + 1)
        sq = u * u
        half = 0.5 * jnp.tanh(u * (kc + (kc * 0.044715) * sq)) + 0.5
        gel = u * half
        e = gel.astype(BF16)
        slope = half + gel * (1.0 - half) * (2.0 * kc + (6.0 * kc * 0.044715) * sq)
        du = (de * slope).astype(BF16)
        et_ref[j, :, :, here] = e.T.reshape(et_ref.shape[1:3] + (rows,))
        du_ref[j, here, :] = du
        part = dot(e, lower(w_ref, j))
        f = part if f is None else f + part
        part = dot_nt(du, block_of(w_ref, j))
        da2 = part if da2 is None else da2 + part
    y_ref[...] = (t2 * f + (1.0 - t2) * h1).astype(BF16)
    dz2 = (dy_ref[...].astype(F32) * (f - h1) * t2 * (1.0 - t2)).astype(BF16)
    dz2_ref[here, :] = dz2
    da2 = da2 + dot_nt(dz2, near_weight(w_ref, 2))
    dh1 = dy_ref[...].astype(F32) * (1.0 - t2) + norm_back(da2, unit, scale, g2)
    dz1 = (dh1 * (att - x_ref[...].astype(F32)) * t1 * (1.0 - t1)).astype(BF16)
    datt = (dh1 * t1).astype(BF16)
    dz1_ref[here, :] = dz1
    dz1o_ref[...] = dz1
    datt_ref[here, :] = datt
    part_ref[...] = dh1 * (1.0 - t1)
    do_ref[...] = dot_nt(datt, near_weight(w_ref, 0)).astype(BF16)

    def total(v):
        return jnp.sum(v, axis=0, keepdims=True)

    dvec_ref[2:3, :] += total(dz1.astype(F32))
    dvec_ref[3:4, :] += total(da2 * unit)
    dvec_ref[4:5, :] += total(da2)
    dvec_ref[5:6, :] += total(dz2.astype(F32))


def split_cores(me_ref, value, own_ref, other_ref, at=slice(None)):
    value = value.reshape(OWNERS // CORES, CORES, SUB, D)
    low = me_ref[0] == 0
    own_ref[:, at, :] = jnp.where(low, value[:, 0], value[:, 1]).astype(BF16)
    other_ref[:, at, :] = jnp.where(low, value[:, 1], value[:, 0]).astype(BF16)


SETS = (2, 2, 1)


def middle_kernel(plan, *refs):
    count = len(plan)
    me_ref, x_ref, a1_ref, o_ref, dy_ref, vec_ref = refs[:6]
    sources = refs[6 : 6 + count]
    a1t_hbm, ot_hbm = refs[6 + count : 8 + count]
    y_ref, part_ref, dz1o_ref, do_ref, dvec_ref, wa_ref = refs[8 + count : 14 + count]
    own1, other1, own2, other2, own3, other3 = refs[14 + count : 20 + count]
    w_ref, a1t_ref, ot_ref, sem, a2t_ref, et_ref, df_ref, du_ref, dz2_ref, dz1_ref, datt_ref = refs[20 + count :]
    step = pl.program_id(0)
    t = df_ref.shape[0]
    blocks = t // x_ref.shape[0]

    def copies():
        return [
            pltpu.make_async_copy(a1t_hbm, a1t_ref, sem.at[0]),
            pltpu.make_async_copy(ot_hbm, ot_ref, sem.at[1]),
        ]

    def gets(early):
        found, count = [], 2
        for source, ranges in zip(sources, plan):
            for first, rows, distances in ranges:
                at = slice(first, first + rows)
                for k, distance in enumerate(distances):
                    owner = jnp.bitwise_xor(me_ref[5], distance)
                    if early == (first < NEAR):
                        to = w_ref.at[owner, at, :]
                        found.append(pltpu.make_async_copy(source.at[k, at, :], to, sem.at[count]))
                    count += 1
        return found

    def late():
        @pl.when(step == 0)
        def _():
            for copy in gets(False):
                copy.wait()

    @pl.when(step == 0)
    def _():
        for copy in gets(True) + gets(False) + copies():
            copy.start()
        dvec_ref[...] = jnp.zeros_like(dvec_ref)
        for copy in gets(True):
            copy.wait()
        wa_ref[...] = near_weight(w_ref, 1)

    @pl.when(step < blocks)
    def _():
        middle_rows(x_ref, a1_ref, o_ref, dy_ref, vec_ref, w_ref, y_ref, part_ref, dz1o_ref, do_ref, dvec_ref,
                    a2t_ref, et_ref, df_ref, du_ref, dz2_ref, dz1_ref, datt_ref, step, late)

    def product(left, right, own_ref, other_ref, j):
        at = slice(SUB * j, SUB * (j + 1))
        split_cores(me_ref, dot(left.reshape(D, t), right), own_ref, other_ref, at)

    each = COLS // SETS[0]
    for k in range(SETS[0]):
        @pl.when(step == blocks + k)
        def _(k=k):
            for j in range(each):
                product(a2t_ref[...], du_ref[each * k + j], own1, other1, j)

    for k in range(SETS[1]):
        @pl.when(step == blocks + SETS[0] + k)
        def _(k=k):
            for j in range(each):
                at = SUB * (each * k + j)
                left = et_ref[:, :, at : at + SUB, :]
                left = left.reshape(CORES, OWNERS // CORES, SUB, t).swapaxes(0, 1)
                product(left, df_ref[...], own2, other2, j)

    @pl.when(step == blocks + SETS[0] + SETS[1])
    def _():
        for copy in copies():
            copy.wait()
        product(a2t_ref[...], dz2_ref[...], own3, other3, 0)
        product(ot_ref[...], datt_ref[...], own3, other3, 1)
        product(a1t_ref[...], dz1_ref[...], own3, other3, 2)


def middle(me, x, a1, o, dy, vec, sources, a1t, ot, rows=512):
    t = x.shape[0]
    blocks = t // rows
    pairs = OWNERS // CORES
    row = pl.BlockSpec((rows, D), lambda i, *_: (jnp.minimum(i, blocks - 1), 0))
    outs = []
    begin = blocks
    for steps, wide in zip(SETS, (COLS, COLS, 3)):
        block = (pairs, SUB * wide // steps, D)
        spec = pl.BlockSpec(block, lambda i, *_, begin=begin, steps=steps: (0, jnp.clip(i - begin, 0, steps - 1), 0))
        outs += [(sds((pairs, SUB * wide, D), BF16), spec)] * 2
        begin += steps
    wide = FF // OWNERS
    plan = tuple(ranges for _, ranges in sources)
    count = sum(len(distances) for ranges in plan for _, _, distances in ranges)
    hbm_ref = pl.BlockSpec(memory_space=pl.ANY)
    return launch(
        functools.partial(middle_kernel, plan),
        "middle",
        [(me, None)]
        + [(v, row) for v in (x, a1, o, dy)]
        + [(vec, full(vec.shape))]
        + [(v, hbm_ref) for v, _ in sources]
        + [(a1t, hbm_ref), (ot, hbm_ref)],
        [
            (sds((t, D), BF16), row),
            (sds((t, D), F32), row),
            (sds((t, D), BF16), row),
            (sds((t, D), BF16), row),
            (sds((8, D), F32), full((8, D), False)),
            (sds((D, D), BF16), full((D, D), False)),
        ]
        + outs,
        grid=(begin,),
        scratch=[
            pltpu.VMEM((OWNERS, ROWS, D), BF16),
            pltpu.VMEM((pairs, CORES, SUB, t), BF16),
            pltpu.VMEM((pairs, CORES, SUB, t), BF16),
            pltpu.SemaphoreType.DMA((2 + count,)),
            pltpu.VMEM((pairs, CORES, SUB, t), BF16),
            pltpu.VMEM((COLS, D // wide, wide, t), BF16),
            pltpu.VMEM((t, D), BF16),
            pltpu.VMEM((COLS, t, D), BF16),
            pltpu.VMEM((t, D), BF16),
            pltpu.VMEM((t, D), BF16),
            pltpu.VMEM((t, D), BF16),
        ],
        price=cost(2 * t * D * (6 * FF + 9 * D), 20, t * FF),
        scalars=1,
        room=46,
    )


def merge_kernel(plan, groups, gots, beside, me_ref, *refs):
    count = len(plan)
    outs = refs[count + gots + beside :]
    for group, members in enumerate(groups):
        begin = 0
        for k in members:
            arrived, first, bit = plan[k]
            own_ref, got_ref = refs[k], refs[count + arrived]
            keep_ref, send_ref = outs[k], outs[count + group]
            rows, width = own_ref.shape[-2:]
            at, to = slice(first, first + rows), slice(begin, begin + rows)
            total = own_ref[...].astype(F32) + got_ref[:, at, :].astype(F32).reshape(own_ref.shape)
            blocks = send_ref.shape[0]
            low = me_ref[bit] == 0
            keep = jnp.where(low, total[:, 0], total[:, 1]).astype(BF16)
            send = jnp.where(low, total[:, 1], total[:, 0]).astype(BF16)
            keep_ref[:, :, :width] = keep.reshape(blocks, rows, width)
            send_ref[:, to, :width] = send.reshape(blocks, rows, width)
            begin += rows
    if beside:
        vec = jnp.sum(refs[count + gots][...], axis=0)
        vec = jnp.concatenate([vec, jnp.zeros((120, D), F32)], axis=0).T
        vec = vec.reshape(OWNERS // (2 * CORES), 2, CORES, SUB, 128)
        vec = jnp.where(me_ref[1] == 0, vec[:, 0], vec[:, 1])
        vec = jnp.where(me_ref[0] == 0, vec[:, 0], vec[:, 1])
        vec = vec.reshape((vec.shape[0] // 2, 2, SUB, 128))
        keep_ref[:, :, width:] = jnp.where(low, vec[:, 0], vec[:, 1]).astype(BF16)
        send_ref[:, :, width:] = jnp.where(low, vec[:, 1], vec[:, 0]).astype(BF16)


def merge(me, items, groups, deps=(), vecs=()):
    owns, gots, plan, keeps = [], [], [], []
    for k, (own, got, first, bit, inner) in enumerate(items):
        blocks, rows, width = own.shape
        outer = blocks // (2 * inner)
        owns.append(own.reshape(outer, 2, inner, rows, width))
        known = [j for j, other in enumerate(gots) if other is got]
        if not known:
            known = [len(gots)]
            gots.append(got)
        plan.append((known[0], first, bit))
        width += 128 if vecs and k == len(items) - 1 else 0
        keeps.append(sds((blocks // 2, rows, width), BF16))
    sends = []
    for members in groups:
        blocks, _, width = keeps[members[0]].shape
        sends.append(sds((blocks, sum(keeps[k].shape[1] for k in members), width), BF16))
    kernel = functools.partial(merge_kernel, tuple(plan), groups, len(gots), len(vecs))
    done = local(kernel, "merge", me, owns + gots + list(vecs), keeps + sends, deps)
    return done[: len(items)], done[len(items) :]


def last_kernel(places, bit, me_ref, *refs):
    count = len(places)
    outs = refs[-4:]
    begin = 0
    for k, (arrived, first) in enumerate(places):
        rows = refs[k].shape[1]
        at = slice(begin, begin + rows)
        for j in range(2):
            block = jnp.bitwise_xor(me_ref[4], j)
            got = refs[count + arrived][block, first : first + rows, :]
            outs[j][at, :] = (refs[k][block].astype(F32) + got.astype(F32)).astype(BF16)
        begin += rows
    merge_kernel(((0, 0, bit),), ((0,),), 1, 0, me_ref, *refs[-6:-4], *outs[2:])


def last_merge(me, items, other, bit):
    gots, places = [], []
    for _, got, first in items:
        known = [j for j, value in enumerate(gots) if value is got]
        if not known:
            known = [len(gots)]
            gots.append(got)
        places.append((known[0], first))
    ins = [own for own, _, _ in items] + gots
    outs = [sds((sum(own.shape[1] for own, _, _ in items), D), BF16)] * 2
    blocks, rows, width = other[0].shape
    ins += [other[0].reshape(blocks // 2, 2, 1, rows, width), other[1]]
    outs += [sds((blocks // 2, rows, width), BF16)] * 2
    return local(functools.partial(last_kernel, tuple(places), bit), "last_merge", me, ins, outs)


def inputs_kernel(x_ref, dqkv_ref, dz1_ref, part_ref, vec_ref, dvec_ref, w_ref, wa_ref, dx_ref, out_ref, acc_ref):
    step = pl.program_id(0)

    @pl.when(step == 0)
    def _():
        acc_ref[...] = dvec_ref[...]

    unit, scale = normed(x_ref[...].astype(F32))
    da1 = dot_nt(dz1_ref[...], wa_ref[...])
    for j in range(3):
        da1 = da1 + dot_nt(dqkv_ref[j], w_ref[:, D * j : D * (j + 1)])
    dx_ref[...] = part_ref[...] + norm_back(da1, unit, scale, vec_ref[0:1, :])
    acc_ref[0:1, :] += jnp.sum(da1 * unit, axis=0, keepdims=True)
    acc_ref[1:2, :] += jnp.sum(da1, axis=0, keepdims=True)

    @pl.when(step == pl.num_programs(0) - 1)
    def _():
        out_ref[...] = acc_ref[...]


def inputs(x, dqkv, dz1, part, vec, dvec, w, wa, rows=512, deps=()):
    t = x.shape[0]
    row = pl.BlockSpec((rows, D), lambda i: (i, 0))
    shape = (8, D)
    return launch(
        inputs_kernel,
        "inputs",
        [
            (x, row),
            (dqkv, pl.BlockSpec((3, rows, D), lambda i: (0, i, 0))),
            (dz1, row),
            (part, row),
            (vec, full((8, D))),
            (dvec, full((8, D))),
            (w, full(w.shape)),
            (wa, full(wa.shape)),
        ],
        [(sds((t, D), F32), row), (sds(shape, F32), full(shape, False))],
        grid=(t // rows,),
        scratch=[pltpu.VMEM((8, D), F32)],
        price=cost(2 * t * D * 4 * D, 12),
        deps=deps,
    )


def collect_kernel(counts, *refs):
    total = jnp.float32(0.0)
    begin = 0
    outs = refs[sum(counts) :]
    for k, count in enumerate(counts):
        parts = refs[begin : begin + count]
        begin += count
        if count == 1:
            value = jnp.sum(parts[0][...].astype(F32), axis=0)
        else:
            value = sum(p[...].astype(F32) for p in parts)
        outs[k][...] = value
        total = total + jnp.sum(value * value)
    outs[-1][...] = jnp.full(outs[-1].shape, total, F32)


def collect(groups, n):
    shapes = [g[0].shape[1:] if len(g) == 1 else g[0].shape for g in groups]
    return pl.pallas_call(
        functools.partial(collect_kernel, tuple(len(g) for g in groups)),
        out_shape=[sds(s, F32) for s in shapes] + [sds((n, 1, 128), F32)],
        compiler_params=params(16),
        cost_estimate=cost(MIB, 3),
        name="collect",
    )(*[v for g in groups for v in g])


RATES = (D ** (-0.5), (D // 16) ** (-0.5), D ** (-0.5), D ** (-0.5), FF ** (-0.5), D ** (-0.5), 0.5)


def update(grad, master, moment, square, clip, rate):
    clipped = grad * clip
    new_moment = 0.5 * moment + 0.5 * clipped
    new_square = 0.5 * square + 0.5 * clipped * clipped
    fix = 1.0 - 0.5**STEP
    stepped = new_moment / fix / (jnp.sqrt(new_square / fix) + 1e-08)
    return (master - rate * (stepped + 0.01 * master), new_moment, new_square)


def adam_kernel(*refs):
    down_ref, joint_ref, sq_ref = refs[:3]
    state = refs[3:24]
    norm_ref = refs[24]
    outs = refs[25:]
    sub = joint_ref.shape[0]
    norm = jnp.sqrt(jnp.sum(sq_ref[...], axis=0)[0:1, 0:1])
    norm_ref[...] = jnp.broadcast_to(norm, norm_ref.shape)
    clip = jnp.minimum(1.0, 1.0 / (norm + 1e-06))

    def piece(index, grad, at):
        old = [state[3 * index + k][at] for k in range(3)]
        new = update(grad, *old, clip, RATES[index])
        for k in range(3):
            outs[3 * index + k][at] = new[k]

    every = slice(None)
    piece(0, joint_ref[:, : 3 * D], (every, every))
    turned_vec = jnp.concatenate([joint_ref[:, 3 * D :], jnp.zeros((128 - sub, 128), F32)], axis=0).T
    piece(6, turned_vec[0:6, 0:sub], (every, every))

    def down(j, count=1):
        return down_ref[sub * j : sub * (j + count), :]

    up = jnp.concatenate([down(j) for j in range(COLS)], axis=1)
    step = FF // OWNERS
    order = [up[:, FF // CORES * c + step * p :][:, :step] for p in range(OWNERS // CORES) for c in range(CORES)]
    piece(3, jnp.concatenate(order, axis=1), (every, every))
    piece(4, down(COLS, COLS), (every, every))
    piece(5, down(2 * COLS), (every, every))
    piece(1, down(2 * COLS + 1), (every, every))
    piece(2, down(2 * COLS + 2), (every, every))


def adam(grads, squares, state):
    return pl.pallas_call(
        adam_kernel,
        out_shape=[sds((1, 128), F32)] + [sds(s.shape, F32) for s in state],
        compiler_params=params(24),
        cost_estimate=cost(4 * MIB, 4),
        name="adam",
    )(*grads, squares, *state)


def ordered(up):
    rows = up.shape[0]
    return up.reshape(rows, OWNERS // CORES, CORES, FF // OWNERS).swapaxes(1, 2).reshape(rows, FF)


def turn_norms(state):
    return tuple(state[:18]) + tuple(s.T for s in state[18:])


def column_blocks(w):
    return [w[..., D * j : D * (j + 1)] for j in range(w.shape[-1] // D)]


def pack_kernel(qkv_ref, attn_ref, gate_ref, up_ref, down_ref, fgate_ref, norms_ref, one_ref, near_ref, rest_ref):
    sub = qkv_ref.shape[0]
    norms = jnp.concatenate([norms_ref[...], jnp.zeros((128 - norms_ref.shape[0], sub), F32)], axis=0)
    norms = jnp.concatenate([norms, jnp.zeros((128, 128 - sub), F32)], axis=1).T[0:sub]
    one = jnp.concatenate([qkv_ref[...], norms], axis=1).astype(BF16)
    one_ref[...] = one
    for j, ref in enumerate((attn_ref, gate_ref, fgate_ref)):
        near_ref[0, sub * j : sub * (j + 1), :] = ref[...].astype(BF16)
    step = FF // OWNERS
    up = up_ref[...]
    order = [up[:, step * (CORES * p + c) :][:, :step] for c in range(CORES) for p in range(OWNERS // CORES)]
    up = jnp.concatenate(order, axis=1).astype(BF16)
    for j in range(COLS):
        rest_ref[0, sub * j : sub * (j + 1), :] = up[:, D * j : D * (j + 1)]
    rest_ref[0, sub * COLS :, :] = down_ref[...].astype(BF16)


def pack(masters):
    sub = masters[0].shape[0]
    ins = [(hbm(v), full(v.shape)) for v in [*masters[:6], masters[6].T]]
    shapes = [(sub, 3 * D + 128), (1, 3 * sub, D), (1, 2 * COLS * sub, D)]
    outs = [(sds(s, BF16), full(s, False)) for s in shapes]
    return launch(pack_kernel, "pack", ins, outs, grid=(1,), price=cost(MIB, 3))


def beside_kernel(per, me_ref, *refs):
    out_ref = refs[-1]
    begin = 0
    for k in range(0, len(refs) - 1, per):
        n, rows, _ = refs[k].shape
        for j in range(per):
            out_ref[n * j : n * (j + 1), begin : begin + rows, :] = refs[k + j][...]
        begin += rows


def beside(me, items, deps=()):
    ins = [v for item in items for v in item]
    shape = (sum(v.shape[0] for v in items[0]), sum(item[0].shape[1] for item in items), D)
    return local(functools.partial(beside_kernel, len(items[0])), "beside", me, ins, [sds(shape, BF16)], deps)[0]


def join_kernel(cuts, count, me_ref, *refs):
    outs = refs[len(refs) - len(cuts) - (1 if count else 0) :]
    for k, (item, first, rows) in enumerate(cuts):
        for j in range(2):
            half = refs[2 * item + j]
            n = half.shape[0]
            outs[k][n * j : n * (j + 1)] = half[:, first : first + rows, :]
    for k in range(count):
        outs[-1][k] = refs[len(refs) - len(outs) - count + k][...]


def join(me, items, cuts, deps=(), singles=()):
    ins = [v for item in items for v in item] + list(singles)
    outs = [sds((2 * items[i][0].shape[0], rows, items[i][0].shape[2]), BF16) for i, _, rows in cuts]
    if singles:
        outs.append(sds((len(singles),) + singles[0].shape, BF16))
    return local(functools.partial(join_kernel, tuple(cuts), len(singles)), "join", me, ins, outs, deps)


def pack_whole(weights):
    qkv, attn, gate, up, down, fgate, norms = weights
    one = jnp.concatenate([qkv, jnp.pad(norms, ((0, 0), (0, 128 - norms.shape[1])))], axis=1)
    rest = [attn, gate, fgate] + column_blocks(ordered(up))
    rest = [p.reshape(OWNERS, SUB, D) for p in rest] + [down.reshape(OWNERS, COLS * SUB, D)]
    return one.reshape(OWNERS, SUB, one.shape[1]), jnp.concatenate(rest, axis=1)


def unpack_whole(one, two, three, joint, vec):
    def blocks(g, start, count):
        parts = [g[:, SUB * j : SUB * (j + 1), :].reshape(D, D) for j in range(start, start + count)]
        return jnp.concatenate(parts, axis=1)

    up = blocks(one, 0, COLS).reshape(D, CORES, OWNERS // CORES, FF // OWNERS)
    return (
        joint.reshape(D, 3 * D),
        blocks(three, 1, 1),
        blocks(three, 2, 1),
        up.swapaxes(1, 2).reshape(D, FF),
        two.reshape(FF, D),
        blocks(three, 0, 1),
        vec[:6].T,
    )


def swap(value, axis, size, bit):
    return lax.ppermute(value, axis, [(i, i ^ bit) for i in range(size)])


def body(nd, nf, tokens, cotangent, halves, *state):
    n = nd * nf
    if n == OWNERS and nf == 2 * CORES:
        return direct(nd, nf, tokens, cotangent, halves, *state)
    return general(n, tokens, cotangent, halves, *state)


def direct(nd, nf, tokens, cotangent, halves, *state):
    both = ("dp", "fsdp")
    nx = nf // CORES
    f = lax.axis_index("fsdp").astype(jnp.int32)
    d = lax.axis_index("dp").astype(jnp.int32)
    me = jnp.stack([f % 2, f // 2, d % 2, (d // 2) % 2, d // 4, d * nf + f, d])

    def to(v, bit):
        axis, size, step = (("fsdp", nf, 1), ("fsdp", nf, 2), ("dp", nd, 1), ("dp", nd, 2), ("dp", nd, 4))[bit]
        return swap(v, axis, size, step)

    one, near, rest = pack(state[0::3])
    ones = [one] + [swap(one, "dp", nd, k) for k in range(1, nd)]
    rest, near, own = join(
        me, [(rest, to(rest, 4)), (near, to(near, 1))], [(0, 0, 2 * WIDE), (1, 0, NEAR)], singles=ones
    )
    up, down, near, own = join(
        me,
        [(rest, to(rest, 3)), (near, to(near, 2)), (own, to(own, 1))],
        [(0, 0, WIDE), (0, WIDE, WIDE), (1, 0, NEAR), (2, 0, SUB)],
    )
    got = to(up, 2), to(down, 1), to(near, 4)
    spots = [nf * k + j for j in (0, CORES) for k in range(nd)]
    parts = [(own, spots), (to(own, 0), [k + 1 for k in spots])]
    every = [(0, 0, WIDE), (1, 0, WIDE), (2, 0, NEAR)]
    a1t, a1, qkv, vec, w = project(me, tokens, parts)
    up, down, near = join(me, list(zip((up, down, near), got)), every, (a1t,))
    got = to(near, 3), to(up, 1), to(down, 2)
    here = beside(me, [(near,), (up,), (down,)])
    crossed = to(here, 0)
    o, ot, lse = attend(halves, qkv, (here,))
    there = beside(me, [(v,) for v in got], (o, crossed))
    sources = []
    parts = ((0, NEAR, (2, 4, 16, 8)), (NEAR, WIDE, (16, 8, 4, 2)), (NEAR + WIDE, WIDE, (16, 8, 2, 4)))
    for value, far, core in ((here, 0, 0), (crossed, 0, 1), (there, 1, 0), (to(there, 0), 1, 1)):
        ranges = []
        for first, rows, bits in parts:
            owners = [far * bits[3] + core]
            for bit in bits[:3]:
                owners = owners + [k + bit for k in owners]
            ranges.append((first, rows, tuple(owners)))
        sources.append((value, tuple(ranges)))
    y, part, dz1, do, dvec, wa, *terms = middle(me, tokens, a1, o, cotangent, vec, sources, a1t, ot)
    first, second, third = ((own, to(other, 0)) for own, other in zip(terms[0::2], terms[1::2]))
    head = attend_back_first(halves, qkv, o, do, lse, 1)
    (first, second, third), sends = merge(
        me, [(*first, 0, 1, 1), (*second, 0, 2, nx), (*third, 0, 3, 2 * nx)], ((0,), (1,), (2,)), (head,)
    )
    got = [to(v, bit) for v, bit in zip(sends, (1, 2, 3))]
    dqkv = attend_back_rest(halves, qkv, o, do, lse, head, 1, deps=(first,))
    own, other = joint_grads(me, a1t, dqkv, deps=tuple(got))
    (first, second, third, joint), sends = merge(
        me,
        [(first, got[0], 0, 2, 1), (second, got[1], 0, 3, nx), (third, got[2], 0, 2, nx), (own, to(other, 0), 0, 1, 1)],
        ((0, 2), (1,), (3,)),
    )
    got = [to(v, bit) for v, bit in zip(sends, (2, 3, 1))]
    dx, dvec = inputs(tokens, dqkv, dz1, part, vec, dvec, w, wa, deps=(first,))
    vecs = [lax.all_gather(dvec, "fsdp", axis=0)]
    below = first.shape[1]
    (first, second, third, joint), sends = merge(
        me,
        [(first, got[0], 0, 3, 1), (second, got[1], 0, 1, 1), (third, got[0], below, 1, 1), (joint, got[2], 0, 2, 1)],
        ((0,), (1, 2), (3,)),
        vecs=vecs,
    )
    got = [to(v, bit) for v, bit in zip(sends, (3, 1, 2))]
    below = second.shape[1]
    keep, send, joint, far = last_merge(
        me, [(first, got[0], 0), (second, got[1], 0), (third, got[1], below)], (joint, got[2]), 3
    )
    sums = [keep, to(send, 4)]
    (joint,), (far,) = merge(me, [(joint, to(far, 3), 0, 4, 1)], ((0,),))
    keep3, far3 = joint, to(far, 4)

    *grads, squares = collect([sums, [keep3[0], far3[0]]], nd * nf)
    squares = lax.all_to_all(squares, both, 0, 0, tiled=True)
    norm, *new = adam(grads, squares, turn_norms(state))
    return (y, dx, norm[0, 0], *turn_norms(new))


def layer_general(me, tokens, cotangent, halves, one, rest):
    a1t, a1, qkv, vec, w = project(me, tokens, [(one, range(OWNERS))])
    o, ot, lse = attend(halves, qkv)
    sources = [(rest, ((0, ROWS, tuple(range(OWNERS))),))]
    y, part, dz1, do, dvec, wa, *terms = middle(me, tokens, a1, o, cotangent, vec, sources, a1t, ot)
    head = attend_back_first(halves, qkv, o, do, lse, 1)
    dqkv = attend_back_rest(halves, qkv, o, do, lse, head, 1)
    terms += joint_grads(me, a1t, dqkv)
    dx, dvec = inputs(tokens, dqkv, dz1, part, vec, dvec, w, wa)
    terms = [
        jnp.stack([own, other], axis=1).reshape((OWNERS,) + own.shape[1:]).astype(F32)
        for own, other in zip(terms[0::2], terms[1::2])
    ]
    return (y, dx) + unpack_whole(*terms, dvec)


def general(n, tokens, cotangent, halves, *state):
    both = ("dp", "fsdp")
    rounded = [m.astype(BF16) for m in state[0::3]]
    packed = pack_whole([lax.all_gather(w, both, axis=0, tiled=True) for w in rounded])
    me = jnp.zeros((7,), jnp.int32)
    y, dx, *terms = layer_general(me, tokens, cotangent, halves, *packed)
    q, wo, wa, wu, wd, wf, nv = [
        lax.psum_scatter(t, both, scatter_dimension=0, tiled=True) for t in terms
    ]
    got = [
        jnp.concatenate(column_blocks(ordered(wu)) + [wd, wf, wo, wa], axis=0),
        jnp.concatenate([q, jnp.pad(nv, ((0, 0), (0, 128 - nv.shape[1])))], axis=1),
    ]
    *grads, squares = collect([[g[None]] for g in got], n)
    squares = lax.all_to_all(squares, both, 0, 0, tiled=True)
    norm, *new = adam(grads, squares, turn_norms(state))
    return (y, dx, norm[0, 0], *turn_norms(new))


def solution(mesh):
    rows = P(("dp", "fsdp"), None)
    nd, nf = mesh.shape["dp"], mesh.shape["fsdp"]
    return jax.shard_map(
        functools.partial(body, nd, nf),
        mesh=mesh,
        in_specs=(rows, rows, P(("dp", "fsdp"))) + (rows,) * 21,
        out_specs=(rows, rows, P()) + (rows,) * 21,
        check_vma=False,
    )
```

```python
import functools
import jax
import jax.numpy as jnp
from jax import lax
from jax.experimental import pallas as pl
from jax.experimental.pallas import tpu as pltpu
from jax.sharding import PartitionSpec as P

D = 512
H = 8
HD = 64
FF = 2048
STEP = 5
PAIRS = H // 2
SUB = 16
OWNERS = D // SUB
COLS = FF // D
F32 = jnp.float32
BF16 = jnp.bfloat16
MIB = 1024 * 1024
CORES = 2


def params(mib):
    return pltpu.CompilerParams(vmem_limit_bytes=mib * MIB)


def cost(flops, mib, trans=0):
    return pl.CostEstimate(flops=flops, bytes_accessed=int(mib * MIB), transcendentals=trans)


def dot(a, b):
    return lax.dot_general(a, b, (((1,), (0,)), ((), ())), preferred_element_type=F32)


def dot_nt(a, b):
    return lax.dot_general(a, b, (((1,), (1,)), ((), ())), preferred_element_type=F32)


def normed(values):
    center = values - jnp.mean(values, axis=-1, keepdims=True)
    scale = lax.rsqrt(jnp.mean(center * center, axis=-1, keepdims=True) + 1e-05)
    return center * scale, scale


def norm_back(grad, unit, scale, gain):
    inner = grad * gain
    first = jnp.mean(inner, axis=-1, keepdims=True)
    second = jnp.mean(inner * unit, axis=-1, keepdims=True)
    return scale * (inner - first - unit * second)


def full(shape, once=True):
    zeros = (0,) * len(shape)
    if once:
        return pl.BlockSpec(shape, lambda *_: zeros, pipeline_mode=pl.Buffered(1))
    return pl.BlockSpec(shape, lambda *_: zeros)


def turned(values):
    return values.T.reshape(OWNERS // CORES, CORES, SUB, values.shape[0])


def sds(shape, dtype):
    return jax.ShapeDtypeStruct(shape, dtype)


def hbm(value):
    return pltpu.with_memory_space_constraint(value, pltpu.HBM)


def launch(kernel, name, ins, outs, grid, scratch=(), price=None, deps=(), scalars=0, aliases=None, room=24):
    count = len(ins)

    def wrapped(*refs):
        kernel(*refs[:count], *refs[count + len(deps) :])

    in_specs = [s for _, s in ins[scalars:]] + [pl.BlockSpec(memory_space=pl.ANY)] * len(deps)
    return pl.pallas_call(
        wrapped if deps else kernel,
        grid_spec=pltpu.PrefetchScalarGridSpec(
            num_scalar_prefetch=scalars,
            grid=grid,
            in_specs=in_specs,
            out_specs=[s for _, s in outs],
            scratch_shapes=list(scratch),
        ),
        out_shape=[o for o, _ in outs],
        input_output_aliases=aliases or {},
        compiler_params=params(room),
        cost_estimate=price,
        name=name,
    )(*[a for a, _ in ins], *deps)


def local(kernel, name, me, ins, outs, deps=()):
    count = 1 + len(ins)

    def wrapped(*refs):
        kernel(*refs[:count], *refs[count + len(deps) :])

    vmem = pl.BlockSpec(memory_space=pltpu.VMEM)
    return pl.pallas_call(
        wrapped,
        in_specs=[pl.BlockSpec(memory_space=pltpu.SMEM)] + [vmem] * len(ins) + [pl.BlockSpec(memory_space=pl.ANY)] * len(deps),
        out_specs=[vmem] * len(outs),
        out_shape=outs,
        compiler_params=params(16),
        cost_estimate=cost(MIB, 4),
        name=name,
    )(me, *ins, *deps)


def project_kernel(places, me_ref, x_ref, *refs):
    parts = refs[:-5]
    a1t_ref, a_ref, qkv_ref, vec_ref, w_ref = refs[-5:]

    @pl.when(pl.program_id(0) == 0)
    def _():
        for part, distances in zip(parts, places):
            for k, distance in enumerate(distances):
                owner = jnp.bitwise_xor(me_ref[5], distance)
                w_ref[pl.ds(pl.multiple_of(owner * SUB, SUB), SUB), :] = part[k]
        vec_ref[...] = w_ref[:, 3 * D : 3 * D + 128].astype(F32).T[0:8, :]

    unit, _ = normed(x_ref[...].astype(F32))
    a1 = (unit * vec_ref[0:1, :] + vec_ref[1:2, :]).astype(BF16)
    a_ref[...] = a1
    a1t_ref[...] = turned(a1)
    for j in range(3):
        qkv_ref[j] = dot(a1, w_ref[:, j * D : (j + 1) * D]).astype(BF16)


def project(me, x, parts, rows=512):
    t = x.shape[0]
    width = parts[0][0].shape[-1]
    places = tuple(tuple(distances) for _, distances in parts)
    row = pl.BlockSpec((rows, D), lambda i, *_: (i, 0))
    pairs = OWNERS // CORES
    return launch(
        functools.partial(project_kernel, places),
        "project",
        [(me, None), (x, row)] + [(p, full(p.shape)) for p, _ in parts],
        [
            (sds((pairs, CORES, SUB, t), BF16), pl.BlockSpec((pairs, CORES, SUB, rows), lambda i, *_: (0, 0, 0, i))),
            (sds((t, D), BF16), row),
            (sds((3, t, D), BF16), pl.BlockSpec((3, rows, D), lambda i, *_: (0, i, 0))),
            (sds((8, D), F32), full((8, D), False)),
            (sds((D, width), BF16), full((D, width), False)),
        ],
        grid=(t // rows,),
        price=cost(2 * t * D * 3 * D, 9),
        scalars=1,
    )


def by_head(values):
    lane = lax.broadcasted_iota(jnp.int32, values.shape, 1)
    zero = jnp.zeros_like(values)
    return jnp.concatenate(
        [jnp.where(lane < HD, values, zero), jnp.where(lane >= HD, values, zero)], axis=0
    )


def own_blocks(values, blk):
    return jnp.concatenate([values[:HD, :blk], values[HD:, blk:]], axis=0)


def diagonal(blk):
    row = lax.broadcasted_iota(jnp.int32, (blk, 2 * blk), 0)
    col = lax.broadcasted_iota(jnp.int32, (blk, 2 * blk), 1)
    return row <= jnp.where(col >= blk, col - blk, col)


def over_blocks(halves_ref, per, front, back):
    def path(firsts):
        ready = front(0, firsts[0])
        for i in range(per):
            later = front(i + 1, firsts[i + 1]) if i + 1 < per else None
            back(i, firsts[i], ready)
            ready = later

    @pl.when(halves_ref[0] == 0)
    def _():
        path([0] * per)

    @pl.when(halves_ref[0] != 0)
    def _():
        path([0] * (per // 2) + [per // 2] * (per // 2))


FORWARD_BLOCK = 512
BACK_BLOCK = 128


def attend_kernel(halves_ref, qkv_ref, o_ref, ot_ref, lse_ref, vt_ref):
    q_ref, k_ref, v_ref = (qkv_ref.at[j] for j in range(3))
    blk = FORWARD_BLOCK
    vt_ref[...] = v_ref[...].T
    allowed = diagonal(blk)

    def front(i, first):
        queries = by_head(q_ref[i * blk : (i + 1) * blk, :] * jnp.bfloat16(0.125))
        return dot_nt(k_ref[first * blk : (i + 1) * blk, :], queries)

    def back(i, first, st):
        rows = slice(i * blk, (i + 1) * blk)
        n = (i - first) * blk
        last = jnp.where(allowed, st[n:, :], -1e30)
        top = jnp.max(last, axis=0, keepdims=True)
        if n:
            top = jnp.maximum(top, jnp.max(st[:n, :], axis=0, keepdims=True))
        expo = jnp.exp(last - top)
        total = jnp.sum(expo, axis=0, keepdims=True)
        expo = expo.astype(BF16)
        if n:
            rest = jnp.exp(st[:n, :] - top)
            total = total + jnp.sum(rest, axis=0, keepdims=True)
            expo = jnp.concatenate([rest.astype(BF16), expo], axis=0)
        out = dot(vt_ref[:, first * blk : (i + 1) * blk], expo) * (1.0 / total)
        out = own_blocks(out, blk).astype(BF16)
        lse = top + jnp.log(total)
        lse_ref[0, 0:1, rows] = lse[:, :blk]
        lse_ref[0, 1:2, rows] = lse[:, blk:]
        ot_ref[:, :, :, rows] = out.reshape(128 // SUB // CORES, CORES, SUB, blk)
        o_ref[rows, :] = out.T

    over_blocks(halves_ref, q_ref.shape[0] // blk, front, back)


def attend(halves, qkv, deps=()):
    t = qkv.shape[1]
    pairs = OWNERS // CORES
    part = 128 // SUB // CORES
    return launch(
        attend_kernel,
        "attend",
        [
            (halves, None),
            (qkv, pl.BlockSpec((3, t, 128), lambda p, *_: (0, 0, p))),
        ],
        [
            (sds((t, D), BF16), pl.BlockSpec((t, 128), lambda p, *_: (0, p))),
            (sds((pairs, CORES, SUB, t), BF16), pl.BlockSpec((part, CORES, SUB, t), lambda p, *_: (p, 0, 0, 0))),
            (sds((PAIRS, 2, t), F32), pl.BlockSpec((1, 2, t), lambda p, *_: (p, 0, 0))),
        ],
        grid=(PAIRS,),
        scratch=[pltpu.VMEM((128, t), BF16)],
        price=cost(4 * t * t * D, 8, t * t * H),
        scalars=1,
        deps=deps,
    )


def attend_back_kernel(halves_ref, qkv_ref, o_ref, do_ref, lse_ref, dqkv_ref, kt_ref, dk_ref, dv_ref):
    q_ref, k_ref, v_ref = (qkv_ref.at[j] for j in range(3))
    blk = BACK_BLOCK
    kt_ref[...] = k_ref[...].T
    prod = (do_ref[...].astype(F32) * o_ref[...].astype(F32)).T
    delta = [jnp.sum(prod[h * HD : (h + 1) * HD, :], axis=0, keepdims=True) for h in range(2)]
    allowed = diagonal(blk)

    def front(i, first):
        rows, keys = slice(i * blk, (i + 1) * blk), slice(first * blk, (i + 1) * blk)
        queries = by_head(q_ref[rows, :] * jnp.bfloat16(0.125))
        grads = by_head(do_ref[rows, :])
        return queries, grads, dot_nt(k_ref[keys, :], queries), dot_nt(v_ref[keys, :], grads)

    def gather(ref, first, i, value):
        n = (i - first) * blk
        if n:
            ref[first * blk : i * blk, :] += value[:n]
        ref[i * blk : (i + 1) * blk, :] = value[n:]

    def back(i, first, ready):
        queries, grads, st, dpt = ready
        rows, keys = slice(i * blk, (i + 1) * blk), slice(first * blk, (i + 1) * blk)
        n = (i - first) * blk
        lse = jnp.concatenate([lse_ref[0, 0:1, rows], lse_ref[0, 1:2, rows]], axis=1)
        rowsum = jnp.concatenate([d[:, rows] for d in delta], axis=1)
        pt = jnp.where(allowed, jnp.exp(st[n:, :] - lse), 0.0)
        if n:
            pt = jnp.concatenate([jnp.exp(st[:n, :] - lse), pt], axis=0)
        dst = (pt * (dpt - rowsum)).astype(BF16)
        gather(dv_ref, first, i, dot(pt.astype(BF16), grads))
        gather(dk_ref, first, i, dot(dst, queries))
        dqt = dot(kt_ref[:, keys], dst) * 0.125
        dqkv_ref[0, rows, :] = own_blocks(dqt, blk).T.astype(BF16)

    over_blocks(halves_ref, q_ref.shape[0] // blk, front, back)
    dqkv_ref[1] = dk_ref[...].astype(BF16)
    dqkv_ref[2] = dv_ref[...].astype(BF16)


def attend_back_first(halves, qkv, o, do, lse, count):
    t = qkv.shape[1]
    col = pl.BlockSpec((t, 128), lambda p, *_: (0, p))
    three = pl.BlockSpec((3, t, 128), lambda p, *_: (0, 0, p))
    return launch(
        attend_back_kernel,
        "attend_back_first",
        [(halves, None), (hbm(qkv), three), (o, col), (do, col), (lse, pl.BlockSpec((1, 2, t), lambda p, *_: (p, 0, 0)))],
        [(sds((3, t, D), BF16), three)],
        grid=(count,),
        scratch=[pltpu.VMEM((128, t), BF16)] + [pltpu.VMEM((t, 128), F32)] * 2,
        price=cost(10 * t * t * 128 * count, 2.5 * count, t * t * 2 * count),
        scalars=1,
    )[0]


def attend_back_rest(halves, qkv, o, do, lse, into, first, deps=()):
    t = qkv.shape[1]
    col = pl.BlockSpec((t, 128), lambda p, *_: (0, first + p))
    three = pl.BlockSpec((3, t, 128), lambda p, *_: (0, 0, first + p))
    count = PAIRS - first
    return launch(
        attend_back_kernel,
        "attend_back_rest",
        [(halves, None), (hbm(qkv), three), (o, col), (do, col), (lse, pl.BlockSpec((1, 2, t), lambda p, *_: (first + p, 0, 0)))],
        [(sds((3, t, D), BF16), three)],
        grid=(count,),
        scratch=[pltpu.VMEM((128, t), BF16)] + [pltpu.VMEM((t, 128), F32)] * 2,
        price=cost(10 * t * t * 128 * count, 2.5 * count, t * t * 2 * count),
        scalars=1,
        deps=(into,) + tuple(deps),
        aliases={5: 0},
    )[0]


def joint_kernel(me_ref, a1t_ref, dqkv_ref, own_ref, other_ref):
    t = dqkv_ref.shape[1]
    split_cores(me_ref, dot(a1t_ref[...].reshape(D, t), dqkv_ref[0]), own_ref, other_ref)


def joint_grads(me, a1t, dqkv, deps=()):
    t = dqkv.shape[1]
    pairs = OWNERS // CORES
    out = (sds((pairs, SUB, 3 * D), BF16), pl.BlockSpec((pairs, SUB, D), lambda i, *_: (0, 0, i)))
    return launch(
        joint_kernel,
        "joint_grads",
        [(me, None), (a1t, full(a1t.shape)), (dqkv, pl.BlockSpec((1, t, D), lambda i, *_: (i, 0, 0)))],
        [out, out],
        grid=(3,),
        price=cost(2 * t * D * 3 * D, 6),
        scalars=1,
        deps=deps,
    )


NEAR = 3 * SUB
ROWS = NEAR + 2 * COLS * SUB
WIDE = COLS * SUB


def near_weight(ref, j):
    return ref[:, SUB * j : SUB * (j + 1), :].reshape(D, D)


def block_of(ref, j):
    return near_weight(ref, 3 + j)


def lower(ref, j):
    halfway = COLS // CORES
    core, part = j // halfway, j % halfway
    per = OWNERS // CORES // halfway
    rows = [ref[CORES * p + core, NEAR + COLS * SUB : ROWS, :] for p in range(per * part, per * (part + 1))]
    return jnp.concatenate(rows, axis=0)


def middle_rows(x_ref, a1_ref, o_ref, dy_ref, vec_ref, w_ref, y_ref, part_ref, dz1o_ref, do_ref, dvec_ref,
                a2t_ref, et_ref, df_ref, du_ref, dz2_ref, dz1_ref, datt_ref, step, late):
    rows = x_ref.shape[0]
    here = pl.ds(pl.multiple_of(step * rows, rows), rows)
    c1, g2, b2, c2 = (vec_ref[k : k + 1, :] for k in (2, 3, 4, 5))
    x = x_ref[...].astype(F32)
    att = dot(o_ref[...], near_weight(w_ref, 0))
    t1 = jax.nn.sigmoid(dot(a1_ref[...], near_weight(w_ref, 1)) + c1)
    h1 = t1 * att + (1.0 - t1) * x
    unit, scale = normed(h1)
    a2 = (unit * g2 + b2).astype(BF16)
    a2t_ref[:, :, :, here] = turned(a2)
    t2 = jax.nn.sigmoid(dot(a2, near_weight(w_ref, 2)) + c2)
    df = (dy_ref[...].astype(F32) * t2).astype(BF16)
    df_ref[here, :] = df
    late()
    kc = 0.7978845608028654

    def ahead(j):
        return dot(a2, block_of(w_ref, j)), dot_nt(df, lower(w_ref, j))

    f = da2 = None
    ready = ahead(0)
    for j in range(COLS):
        u, de = ready
        if j + 1 < COLS:
            ready = ahead(j + 1)
        sq = u * u
        half = 0.5 * jnp.tanh(u * (kc + (kc * 0.044715) * sq)) + 0.5
        gel = u * half
        e = gel.astype(BF16)
        slope = half + gel * (1.0 - half) * (2.0 * kc + (6.0 * kc * 0.044715) * sq)
        du = (de * slope).astype(BF16)
        et_ref[j, :, :, here] = e.T.reshape(et_ref.shape[1:3] + (rows,))
        du_ref[j, here, :] = du
        part = dot(e, lower(w_ref, j))
        f = part if f is None else f + part
        part = dot_nt(du, block_of(w_ref, j))
        da2 = part if da2 is None else da2 + part
    y_ref[...] = (t2 * f + (1.0 - t2) * h1).astype(BF16)
    dz2 = (dy_ref[...].astype(F32) * (f - h1) * t2 * (1.0 - t2)).astype(BF16)
    dz2_ref[here, :] = dz2
    da2 = da2 + dot_nt(dz2, near_weight(w_ref, 2))
    dh1 = dy_ref[...].astype(F32) * (1.0 - t2) + norm_back(da2, unit, scale, g2)
    dz1 = (dh1 * (att - x_ref[...].astype(F32)) * t1 * (1.0 - t1)).astype(BF16)
    datt = (dh1 * t1).astype(BF16)
    dz1_ref[here, :] = dz1
    dz1o_ref[...] = dz1
    datt_ref[here, :] = datt
    part_ref[...] = dh1 * (1.0 - t1)
    do_ref[...] = dot_nt(datt, near_weight(w_ref, 0)).astype(BF16)

    def total(v):
        return jnp.sum(v, axis=0, keepdims=True)

    dvec_ref[2:3, :] += total(dz1.astype(F32))
    dvec_ref[3:4, :] += total(da2 * unit)
    dvec_ref[4:5, :] += total(da2)
    dvec_ref[5:6, :] += total(dz2.astype(F32))


def split_cores(me_ref, value, own_ref, other_ref, at=slice(None)):
    value = value.reshape(OWNERS // CORES, CORES, SUB, D)
    low = me_ref[0] == 0
    own_ref[:, at, :] = jnp.where(low, value[:, 0], value[:, 1]).astype(BF16)
    other_ref[:, at, :] = jnp.where(low, value[:, 1], value[:, 0]).astype(BF16)


SETS = (2, 2, 1)


def middle_kernel(plan, *refs):
    count = len(plan)
    me_ref, x_ref, a1_ref, o_ref, dy_ref, vec_ref = refs[:6]
    sources = refs[6 : 6 + count]
    a1t_hbm, ot_hbm = refs[6 + count : 8 + count]
    y_ref, part_ref, dz1o_ref, do_ref, dvec_ref, wa_ref = refs[8 + count : 14 + count]
    own1, other1, own2, other2, own3, other3 = refs[14 + count : 20 + count]
    w_ref, a1t_ref, ot_ref, sem, a2t_ref, et_ref, df_ref, du_ref, dz2_ref, dz1_ref, datt_ref = refs[20 + count :]
    step = pl.program_id(0)
    t = df_ref.shape[0]
    blocks = t // x_ref.shape[0]

    def copies():
        return [
            pltpu.make_async_copy(a1t_hbm, a1t_ref, sem.at[0]),
            pltpu.make_async_copy(ot_hbm, ot_ref, sem.at[1]),
        ]

    def gets(early):
        found, count = [], 2
        for source, ranges in zip(sources, plan):
            for first, rows, distances in ranges:
                at = slice(first, first + rows)
                for k, distance in enumerate(distances):
                    owner = jnp.bitwise_xor(me_ref[5], distance)
                    if early == (first < NEAR):
                        to = w_ref.at[owner, at, :]
                        found.append(pltpu.make_async_copy(source.at[k, at, :], to, sem.at[count]))
                    count += 1
        return found

    def late():
        @pl.when(step == 0)
        def _():
            for copy in gets(False):
                copy.wait()

    @pl.when(step == 0)
    def _():
        for copy in gets(True) + gets(False) + copies():
            copy.start()
        dvec_ref[...] = jnp.zeros_like(dvec_ref)
        for copy in gets(True):
            copy.wait()
        wa_ref[...] = near_weight(w_ref, 1)

    @pl.when(step < blocks)
    def _():
        middle_rows(x_ref, a1_ref, o_ref, dy_ref, vec_ref, w_ref, y_ref, part_ref, dz1o_ref, do_ref, dvec_ref,
                    a2t_ref, et_ref, df_ref, du_ref, dz2_ref, dz1_ref, datt_ref, step, late)

    def product(left, right, own_ref, other_ref, j):
        at = slice(SUB * j, SUB * (j + 1))
        split_cores(me_ref, dot(left.reshape(D, t), right), own_ref, other_ref, at)

    each = COLS // SETS[0]
    for k in range(SETS[0]):
        @pl.when(step == blocks + k)
        def _(k=k):
            for j in range(each):
                product(a2t_ref[...], du_ref[each * k + j], own1, other1, j)

    for k in range(SETS[1]):
        @pl.when(step == blocks + SETS[0] + k)
        def _(k=k):
            for j in range(each):
                at = SUB * (each * k + j)
                left = et_ref[:, :, at : at + SUB, :]
                left = left.reshape(CORES, OWNERS // CORES, SUB, t).swapaxes(0, 1)
                product(left, df_ref[...], own2, other2, j)

    @pl.when(step == blocks + SETS[0] + SETS[1])
    def _():
        for copy in copies():
            copy.wait()
        product(a2t_ref[...], dz2_ref[...], own3, other3, 0)
        product(ot_ref[...], datt_ref[...], own3, other3, 1)
        product(a1t_ref[...], dz1_ref[...], own3, other3, 2)


def middle(me, x, a1, o, dy, vec, sources, a1t, ot, rows=512):
    t = x.shape[0]
    blocks = t // rows
    pairs = OWNERS // CORES
    row = pl.BlockSpec((rows, D), lambda i, *_: (jnp.minimum(i, blocks - 1), 0))
    outs = []
    begin = blocks
    for steps, wide in zip(SETS, (COLS, COLS, 3)):
        block = (pairs, SUB * wide // steps, D)
        spec = pl.BlockSpec(block, lambda i, *_, begin=begin, steps=steps: (0, jnp.clip(i - begin, 0, steps - 1), 0))
        outs += [(sds((pairs, SUB * wide, D), BF16), spec)] * 2
        begin += steps
    wide = FF // OWNERS
    plan = tuple(ranges for _, ranges in sources)
    count = sum(len(distances) for ranges in plan for _, _, distances in ranges)
    hbm_ref = pl.BlockSpec(memory_space=pl.ANY)
    return launch(
        functools.partial(middle_kernel, plan),
        "middle",
        [(me, None)]
        + [(v, row) for v in (x, a1, o, dy)]
        + [(vec, full(vec.shape))]
        + [(v, hbm_ref) for v, _ in sources]
        + [(a1t, hbm_ref), (ot, hbm_ref)],
        [
            (sds((t, D), BF16), row),
            (sds((t, D), F32), row),
            (sds((t, D), BF16), row),
            (sds((t, D), BF16), row),
            (sds((8, D), F32), full((8, D), False)),
            (sds((D, D), BF16), full((D, D), False)),
        ]
        + outs,
        grid=(begin,),
        scratch=[
            pltpu.VMEM((OWNERS, ROWS, D), BF16),
            pltpu.VMEM((pairs, CORES, SUB, t), BF16),
            pltpu.VMEM((pairs, CORES, SUB, t), BF16),
            pltpu.SemaphoreType.DMA((2 + count,)),
            pltpu.VMEM((pairs, CORES, SUB, t), BF16),
            pltpu.VMEM((COLS, D // wide, wide, t), BF16),
            pltpu.VMEM((t, D), BF16),
            pltpu.VMEM((COLS, t, D), BF16),
            pltpu.VMEM((t, D), BF16),
            pltpu.VMEM((t, D), BF16),
            pltpu.VMEM((t, D), BF16),
        ],
        price=cost(2 * t * D * (6 * FF + 9 * D), 20, t * FF),
        scalars=1,
        room=46,
    )


def merge_kernel(plan, groups, gots, beside, me_ref, *refs):
    count = len(plan)
    outs = refs[count + gots + beside :]
    for group, members in enumerate(groups):
        begin = 0
        for k in members:
            arrived, first, bit = plan[k]
            own_ref, got_ref = refs[k], refs[count + arrived]
            keep_ref, send_ref = outs[k], outs[count + group]
            rows, width = own_ref.shape[-2:]
            at, to = slice(first, first + rows), slice(begin, begin + rows)
            total = own_ref[...].astype(F32) + got_ref[:, at, :].astype(F32).reshape(own_ref.shape)
            blocks = send_ref.shape[0]
            low = me_ref[bit] == 0
            keep = jnp.where(low, total[:, 0], total[:, 1]).astype(BF16)
            send = jnp.where(low, total[:, 1], total[:, 0]).astype(BF16)
            keep_ref[:, :, :width] = keep.reshape(blocks, rows, width)
            send_ref[:, to, :width] = send.reshape(blocks, rows, width)
            begin += rows
    if beside:
        vec = jnp.sum(refs[count + gots][...], axis=0)
        vec = jnp.concatenate([vec, jnp.zeros((120, D), F32)], axis=0).T
        vec = vec.reshape(OWNERS // (2 * CORES), 2, CORES, SUB, 128)
        vec = jnp.where(me_ref[1] == 0, vec[:, 0], vec[:, 1])
        vec = jnp.where(me_ref[0] == 0, vec[:, 0], vec[:, 1])
        vec = vec.reshape((vec.shape[0] // 2, 2, SUB, 128))
        keep_ref[:, :, width:] = jnp.where(low, vec[:, 0], vec[:, 1]).astype(BF16)
        send_ref[:, :, width:] = jnp.where(low, vec[:, 1], vec[:, 0]).astype(BF16)


def merge(me, items, groups, deps=(), vecs=()):
    owns, gots, plan, keeps = [], [], [], []
    for k, (own, got, first, bit, inner) in enumerate(items):
        blocks, rows, width = own.shape
        outer = blocks // (2 * inner)
        owns.append(own.reshape(outer, 2, inner, rows, width))
        known = [j for j, other in enumerate(gots) if other is got]
        if not known:
            known = [len(gots)]
            gots.append(got)
        plan.append((known[0], first, bit))
        width += 128 if vecs and k == len(items) - 1 else 0
        keeps.append(sds((blocks // 2, rows, width), BF16))
    sends = []
    for members in groups:
        blocks, _, width = keeps[members[0]].shape
        sends.append(sds((blocks, sum(keeps[k].shape[1] for k in members), width), BF16))
    kernel = functools.partial(merge_kernel, tuple(plan), groups, len(gots), len(vecs))
    done = local(kernel, "merge", me, owns + gots + list(vecs), keeps + sends, deps)
    return done[: len(items)], done[len(items) :]


def last_kernel(places, bit, me_ref, *refs):
    count = len(places)
    outs = refs[-4:]
    begin = 0
    for k, (arrived, first) in enumerate(places):
        rows = refs[k].shape[1]
        at = slice(begin, begin + rows)
        for j in range(2):
            block = jnp.bitwise_xor(me_ref[4], j)
            got = refs[count + arrived][block, first : first + rows, :]
            outs[j][at, :] = (refs[k][block].astype(F32) + got.astype(F32)).astype(BF16)
        begin += rows
    merge_kernel(((0, 0, bit),), ((0,),), 1, 0, me_ref, *refs[-6:-4], *outs[2:])


def last_merge(me, items, other, bit):
    gots, places = [], []
    for _, got, first in items:
        known = [j for j, value in enumerate(gots) if value is got]
        if not known:
            known = [len(gots)]
            gots.append(got)
        places.append((known[0], first))
    ins = [own for own, _, _ in items] + gots
    outs = [sds((sum(own.shape[1] for own, _, _ in items), D), BF16)] * 2
    blocks, rows, width = other[0].shape
    ins += [other[0].reshape(blocks // 2, 2, 1, rows, width), other[1]]
    outs += [sds((blocks // 2, rows, width), BF16)] * 2
    return local(functools.partial(last_kernel, tuple(places), bit), "last_merge", me, ins, outs)


def inputs_kernel(x_ref, dqkv_ref, dz1_ref, part_ref, vec_ref, dvec_ref, w_ref, wa_ref, dx_ref, out_ref, acc_ref):
    step = pl.program_id(0)

    @pl.when(step == 0)
    def _():
        acc_ref[...] = dvec_ref[...]

    unit, scale = normed(x_ref[...].astype(F32))
    da1 = dot_nt(dz1_ref[...], wa_ref[...])
    for j in range(3):
        da1 = da1 + dot_nt(dqkv_ref[j], w_ref[:, D * j : D * (j + 1)])
    dx_ref[...] = part_ref[...] + norm_back(da1, unit, scale, vec_ref[0:1, :])
    acc_ref[0:1, :] += jnp.sum(da1 * unit, axis=0, keepdims=True)
    acc_ref[1:2, :] += jnp.sum(da1, axis=0, keepdims=True)

    @pl.when(step == pl.num_programs(0) - 1)
    def _():
        out_ref[...] = acc_ref[...]


def inputs(x, dqkv, dz1, part, vec, dvec, w, wa, rows=512, deps=()):
    t = x.shape[0]
    row = pl.BlockSpec((rows, D), lambda i: (i, 0))
    shape = (8, D)
    return launch(
        inputs_kernel,
        "inputs",
        [
            (x, row),
            (dqkv, pl.BlockSpec((3, rows, D), lambda i: (0, i, 0))),
            (dz1, row),
            (part, row),
            (vec, full((8, D))),
            (dvec, full((8, D))),
            (w, full(w.shape)),
            (wa, full(wa.shape)),
        ],
        [(sds((t, D), F32), row), (sds(shape, F32), full(shape, False))],
        grid=(t // rows,),
        scratch=[pltpu.VMEM((8, D), F32)],
        price=cost(2 * t * D * 4 * D, 12),
        deps=deps,
    )


def collect_kernel(counts, *refs):
    total = jnp.float32(0.0)
    begin = 0
    outs = refs[sum(counts) :]
    for k, count in enumerate(counts):
        parts = refs[begin : begin + count]
        begin += count
        if count == 1:
            value = jnp.sum(parts[0][...].astype(F32), axis=0)
        else:
            value = sum(p[...].astype(F32) for p in parts)
        outs[k][...] = value
        total = total + jnp.sum(value * value)
    outs[-1][...] = jnp.full(outs[-1].shape, total, F32)


def collect(groups, n):
    shapes = [g[0].shape[1:] if len(g) == 1 else g[0].shape for g in groups]
    return pl.pallas_call(
        functools.partial(collect_kernel, tuple(len(g) for g in groups)),
        out_shape=[sds(s, F32) for s in shapes] + [sds((n, 1, 128), F32)],
        compiler_params=params(16),
        cost_estimate=cost(MIB, 3),
        name="collect",
    )(*[v for g in groups for v in g])


RATES = (D ** (-0.5), (D // 16) ** (-0.5), D ** (-0.5), D ** (-0.5), FF ** (-0.5), D ** (-0.5), 0.5)


def update(grad, master, moment, square, clip, rate):
    clipped = grad * clip
    new_moment = 0.5 * moment + 0.5 * clipped
    new_square = 0.5 * square + 0.5 * clipped * clipped
    fix = 1.0 - 0.5**STEP
    stepped = new_moment / fix / (jnp.sqrt(new_square / fix) + 1e-08)
    return (master - rate * (stepped + 0.01 * master), new_moment, new_square)


def adam_kernel(*refs):
    down_ref, joint_ref, sq_ref = refs[:3]
    state = refs[3:24]
    norm_ref = refs[24]
    outs = refs[25:]
    sub = joint_ref.shape[0]
    norm = jnp.sqrt(jnp.sum(sq_ref[...], axis=0)[0:1, 0:1])
    norm_ref[...] = jnp.broadcast_to(norm, norm_ref.shape)
    clip = jnp.minimum(1.0, 1.0 / (norm + 1e-06))

    def piece(index, grad, at):
        old = [state[3 * index + k][at] for k in range(3)]
        new = update(grad, *old, clip, RATES[index])
        for k in range(3):
            outs[3 * index + k][at] = new[k]

    every = slice(None)
    piece(0, joint_ref[:, : 3 * D], (every, every))
    turned_vec = jnp.concatenate([joint_ref[:, 3 * D :], jnp.zeros((128 - sub, 128), F32)], axis=0).T
    piece(6, turned_vec[0:6, 0:sub], (every, every))

    def down(j, count=1):
        return down_ref[sub * j : sub * (j + count), :]

    up = jnp.concatenate([down(j) for j in range(COLS)], axis=1)
    step = FF // OWNERS
    order = [up[:, FF // CORES * c + step * p :][:, :step] for p in range(OWNERS // CORES) for c in range(CORES)]
    piece(3, jnp.concatenate(order, axis=1), (every, every))
    piece(4, down(COLS, COLS), (every, every))
    piece(5, down(2 * COLS), (every, every))
    piece(1, down(2 * COLS + 1), (every, every))
    piece(2, down(2 * COLS + 2), (every, every))


def adam(grads, squares, state):
    return pl.pallas_call(
        adam_kernel,
        out_shape=[sds((1, 128), F32)] + [sds(s.shape, F32) for s in state],
        compiler_params=params(24),
        cost_estimate=cost(4 * MIB, 4),
        name="adam",
    )(*grads, squares, *state)


def ordered(up):
    rows = up.shape[0]
    return up.reshape(rows, OWNERS // CORES, CORES, FF // OWNERS).swapaxes(1, 2).reshape(rows, FF)


def turn_norms(state):
    return tuple(state[:18]) + tuple(s.T for s in state[18:])


def column_blocks(w):
    return [w[..., D * j : D * (j + 1)] for j in range(w.shape[-1] // D)]


def pack_kernel(qkv_ref, attn_ref, gate_ref, up_ref, down_ref, fgate_ref, norms_ref, one_ref, near_ref, rest_ref):
    sub = qkv_ref.shape[0]
    norms = jnp.concatenate([norms_ref[...], jnp.zeros((128 - norms_ref.shape[0], sub), F32)], axis=0)
    norms = jnp.concatenate([norms, jnp.zeros((128, 128 - sub), F32)], axis=1).T[0:sub]
    one = jnp.concatenate([qkv_ref[...], norms], axis=1).astype(BF16)
    one_ref[...] = one
    for j, ref in enumerate((attn_ref, gate_ref, fgate_ref)):
        near_ref[0, sub * j : sub * (j + 1), :] = ref[...].astype(BF16)
    step = FF // OWNERS
    up = up_ref[...]
    order = [up[:, step * (CORES * p + c) :][:, :step] for c in range(CORES) for p in range(OWNERS // CORES)]
    up = jnp.concatenate(order, axis=1).astype(BF16)
    for j in range(COLS):
        rest_ref[0, sub * j : sub * (j + 1), :] = up[:, D * j : D * (j + 1)]
    rest_ref[0, sub * COLS :, :] = down_ref[...].astype(BF16)


def pack(masters):
    sub = masters[0].shape[0]
    ins = [(hbm(v), full(v.shape)) for v in [*masters[:6], masters[6].T]]
    shapes = [(sub, 3 * D + 128), (1, 3 * sub, D), (1, 2 * COLS * sub, D)]
    outs = [(sds(s, BF16), full(s, False)) for s in shapes]
    return launch(pack_kernel, "pack", ins, outs, grid=(1,), price=cost(MIB, 3))


def beside_kernel(per, me_ref, *refs):
    out_ref = refs[-1]
    begin = 0
    for k in range(0, len(refs) - 1, per):
        n, rows, _ = refs[k].shape
        for j in range(per):
            out_ref[n * j : n * (j + 1), begin : begin + rows, :] = refs[k + j][...]
        begin += rows


def beside(me, items, deps=()):
    ins = [v for item in items for v in item]
    shape = (sum(v.shape[0] for v in items[0]), sum(item[0].shape[1] for item in items), D)
    return local(functools.partial(beside_kernel, len(items[0])), "beside", me, ins, [sds(shape, BF16)], deps)[0]


def three_kernel(me_ref, *refs):
    count = (len(refs) - 1) // 3
    begin = 0
    for k in range(count):
        for j in range(2):
            half = refs[2 * k + j]
            n, rows, _ = half.shape
            refs[2 * count + k][n * j : n * (j + 1)] = half[...]
            refs[-1][n * j : n * (j + 1), begin : begin + rows, :] = half[...]
        begin += rows


def join_beside(me, items, deps=()):
    ins = [v for item in items for v in item]
    n = 2 * items[0][0].shape[0]
    outs = [sds((n, one.shape[1], D), BF16) for one, _ in items]
    outs.append(sds((n, sum(one.shape[1] for one, _ in items), D), BF16))
    return local(three_kernel, "join_beside", me, ins, outs, deps)


def join_kernel(cuts, count, me_ref, *refs):
    outs = refs[len(refs) - len(cuts) - (1 if count else 0) :]
    for k, (item, first, rows) in enumerate(cuts):
        for j in range(2):
            half = refs[2 * item + j]
            n = half.shape[0]
            outs[k][n * j : n * (j + 1)] = half[:, first : first + rows, :]
    for k in range(count):
        outs[-1][k] = refs[len(refs) - len(outs) - count + k][...]


def join(me, items, cuts, deps=(), singles=()):
    ins = [v for item in items for v in item] + list(singles)
    outs = [sds((2 * items[i][0].shape[0], rows, items[i][0].shape[2]), BF16) for i, _, rows in cuts]
    if singles:
        outs.append(sds((len(singles),) + singles[0].shape, BF16))
    return local(functools.partial(join_kernel, tuple(cuts), len(singles)), "join", me, ins, outs, deps)


def pack_whole(weights):
    qkv, attn, gate, up, down, fgate, norms = weights
    one = jnp.concatenate([qkv, jnp.pad(norms, ((0, 0), (0, 128 - norms.shape[1])))], axis=1)
    rest = [attn, gate, fgate] + column_blocks(ordered(up))
    rest = [p.reshape(OWNERS, SUB, D) for p in rest] + [down.reshape(OWNERS, COLS * SUB, D)]
    return one.reshape(OWNERS, SUB, one.shape[1]), jnp.concatenate(rest, axis=1)


def unpack_whole(one, two, three, joint, vec):
    def blocks(g, start, count):
        parts = [g[:, SUB * j : SUB * (j + 1), :].reshape(D, D) for j in range(start, start + count)]
        return jnp.concatenate(parts, axis=1)

    up = blocks(one, 0, COLS).reshape(D, CORES, OWNERS // CORES, FF // OWNERS)
    return (
        joint.reshape(D, 3 * D),
        blocks(three, 1, 1),
        blocks(three, 2, 1),
        up.swapaxes(1, 2).reshape(D, FF),
        two.reshape(FF, D),
        blocks(three, 0, 1),
        vec[:6].T,
    )


def swap(value, axis, size, bit):
    return lax.ppermute(value, axis, [(i, i ^ bit) for i in range(size)])


def body(nd, nf, tokens, cotangent, halves, *state):
    n = nd * nf
    if n == OWNERS and nf == 2 * CORES:
        return direct(nd, nf, tokens, cotangent, halves, *state)
    return general(n, tokens, cotangent, halves, *state)


def direct(nd, nf, tokens, cotangent, halves, *state):
    both = ("dp", "fsdp")
    nx = nf // CORES
    f = lax.axis_index("fsdp").astype(jnp.int32)
    d = lax.axis_index("dp").astype(jnp.int32)
    me = jnp.stack([f % 2, f // 2, d % 2, (d // 2) % 2, d // 4, d * nf + f, d])

    def to(v, bit):
        axis, size, step = (("fsdp", nf, 1), ("fsdp", nf, 2), ("dp", nd, 1), ("dp", nd, 2), ("dp", nd, 4))[bit]
        return swap(v, axis, size, step)

    one, near, rest = pack(state[0::3])
    ones = [one] + [swap(one, "dp", nd, k) for k in range(1, nd)]
    rest, near, own = join(
        me, [(rest, to(rest, 4)), (near, to(near, 1))], [(0, 0, 2 * WIDE), (1, 0, NEAR)], singles=ones
    )
    up, down, near, own = join(
        me,
        [(rest, to(rest, 3)), (near, to(near, 2)), (own, to(own, 1))],
        [(0, 0, WIDE), (0, WIDE, WIDE), (1, 0, NEAR), (2, 0, SUB)],
    )
    got = to(near, 4), to(up, 2), to(down, 1)
    spots = [nf * k + j for j in (0, CORES) for k in range(nd)]
    parts = [(own, spots), (to(own, 0), [k + 1 for k in spots])]
    a1t, a1, qkv, vec, w = project(me, tokens, parts)
    near, up, down, here = join_beside(me, list(zip((near, up, down), got)), (a1t,))
    got = to(near, 3), to(up, 1), to(down, 2)
    crossed = to(here, 0)
    o, ot, lse = attend(halves, qkv, (here,))
    there = beside(me, [(v,) for v in got], (o, crossed))
    sources = []
    parts = ((0, NEAR, (2, 4, 16, 8)), (NEAR, WIDE, (16, 8, 4, 2)), (NEAR + WIDE, WIDE, (16, 8, 2, 4)))
    for value, far, core in ((here, 0, 0), (crossed, 0, 1), (there, 1, 0), (to(there, 0), 1, 1)):
        ranges = []
        for first, rows, bits in parts:
            owners = [far * bits[3] + core]
            for bit in bits[:3]:
                owners = owners + [k + bit for k in owners]
            ranges.append((first, rows, tuple(owners)))
        sources.append((value, tuple(ranges)))
    y, part, dz1, do, dvec, wa, *terms = middle(me, tokens, a1, o, cotangent, vec, sources, a1t, ot)
    first, second, third = ((own, to(other, 0)) for own, other in zip(terms[0::2], terms[1::2]))
    head = attend_back_first(halves, qkv, o, do, lse, 1)
    (first, second, third), sends = merge(
        me, [(*first, 0, 1, 1), (*second, 0, 2, nx), (*third, 0, 3, 2 * nx)], ((0,), (1,), (2,)), (head,)
    )
    got = [to(v, bit) for v, bit in zip(sends, (1, 2, 3))]
    dqkv = attend_back_rest(halves, qkv, o, do, lse, head, 1, deps=(first,))
    own, other = joint_grads(me, a1t, dqkv, deps=tuple(got))
    (first, second, third, joint), sends = merge(
        me,
        [(first, got[0], 0, 2, 1), (second, got[1], 0, 3, nx), (third, got[2], 0, 2, nx), (own, to(other, 0), 0, 1, 1)],
        ((0, 2), (1,), (3,)),
    )
    got = [to(v, bit) for v, bit in zip(sends, (2, 3, 1))]
    dx, dvec = inputs(tokens, dqkv, dz1, part, vec, dvec, w, wa, deps=(first,))
    vecs = [lax.all_gather(dvec, "fsdp", axis=0)]
    below = first.shape[1]
    (first, second, third, joint), sends = merge(
        me,
        [(first, got[0], 0, 3, 1), (second, got[1], 0, 1, 1), (third, got[0], below, 1, 1), (joint, got[2], 0, 2, 1)],
        ((0,), (1, 2), (3,)),
        vecs=vecs,
    )
    got = [to(v, bit) for v, bit in zip(sends, (3, 1, 2))]
    below = second.shape[1]
    keep, send, joint, far = last_merge(
        me, [(first, got[0], 0), (second, got[1], 0), (third, got[1], below)], (joint, got[2]), 3
    )
    sums = [keep, to(send, 4)]
    (joint,), (far,) = merge(me, [(joint, to(far, 3), 0, 4, 1)], ((0,),))
    keep3, far3 = joint, to(far, 4)

    *grads, squares = collect([sums, [keep3[0], far3[0]]], nd * nf)
    squares = lax.all_to_all(squares, both, 0, 0, tiled=True)
    norm, *new = adam(grads, squares, turn_norms(state))
    return (y, dx, norm[0, 0], *turn_norms(new))


def layer_general(me, tokens, cotangent, halves, one, rest):
    a1t, a1, qkv, vec, w = project(me, tokens, [(one, range(OWNERS))])
    o, ot, lse = attend(halves, qkv)
    sources = [(rest, ((0, ROWS, tuple(range(OWNERS))),))]
    y, part, dz1, do, dvec, wa, *terms = middle(me, tokens, a1, o, cotangent, vec, sources, a1t, ot)
    head = attend_back_first(halves, qkv, o, do, lse, 1)
    dqkv = attend_back_rest(halves, qkv, o, do, lse, head, 1)
    terms += joint_grads(me, a1t, dqkv)
    dx, dvec = inputs(tokens, dqkv, dz1, part, vec, dvec, w, wa)
    terms = [
        jnp.stack([own, other], axis=1).reshape((OWNERS,) + own.shape[1:]).astype(F32)
        for own, other in zip(terms[0::2], terms[1::2])
    ]
    return (y, dx) + unpack_whole(*terms, dvec)


def general(n, tokens, cotangent, halves, *state):
    both = ("dp", "fsdp")
    rounded = [m.astype(BF16) for m in state[0::3]]
    packed = pack_whole([lax.all_gather(w, both, axis=0, tiled=True) for w in rounded])
    me = jnp.zeros((7,), jnp.int32)
    y, dx, *terms = layer_general(me, tokens, cotangent, halves, *packed)
    q, wo, wa, wu, wd, wf, nv = [
        lax.psum_scatter(t, both, scatter_dimension=0, tiled=True) for t in terms
    ]
    got = [
        jnp.concatenate(column_blocks(ordered(wu)) + [wd, wf, wo, wa], axis=0),
        jnp.concatenate([q, jnp.pad(nv, ((0, 0), (0, 128 - nv.shape[1])))], axis=1),
    ]
    *grads, squares = collect([[g[None]] for g in got], n)
    squares = lax.all_to_all(squares, both, 0, 0, tiled=True)
    norm, *new = adam(grads, squares, turn_norms(state))
    return (y, dx, norm[0, 0], *turn_norms(new))


def solution(mesh):
    rows = P(("dp", "fsdp"), None)
    nd, nf = mesh.shape["dp"], mesh.shape["fsdp"]
    return jax.shard_map(
        functools.partial(body, nd, nf),
        mesh=mesh,
        in_specs=(rows, rows, P(("dp", "fsdp"))) + (rows,) * 21,
        out_specs=(rows, rows, P()) + (rows,) * 21,
        check_vma=False,
    )
```
